256 devices in a mesh: gx: 4 (over y_lo, core), gy: 4 (over x), gz: 16 (over y_hi, z).
Axes of the slice: x: 4, y: 4 (y_hi: 2, y_lo: 2; y = y_hi * 2 + y_lo), z: 8, core: 2. Of those that a mesh axis runs over, the one named last changes fastest.
Arguments:
- permeability: float32 [512, 64, 512], P('gz', 'gx', 'gy'), may hold values from 0.1 to 10
- accumulation: float32 [512, 64, 512], P('gz', 'gx', 'gy'), may hold values from 0.0001 to 0.001
- source_term: float32 [512, 64, 512], P('gz', 'gx', 'gy'), may hold values from -1.6 to 1.6
- vertical_trans: float32 [512, 64, 512], P('gz', 'gx', 'gy'), may hold values from 0.05 to 0.5
Outputs:
- pressure: float32 [512, 64, 512], P('gz', 'gx', 'gy')
- residual: float32 [512, 64, 512], P('gz', 'gx', 'gy')
The draws below stay inside these ranges and needn't reach their ends.
All inputs are finite; a program needn't handle non-finite values.
Results may differ from the reference program's by a relative error of at most 0.0003.
Values sent between devices are 32-bit elements; how exact they have to be, the bound alone decides.
A program may use at most 64 MiB of HBM per device.

```python
import math
import jax
import jax.numpy as jnp
from jax import lax

CB = 16
SWEEPS = 8
NX = 64
NY = 512
NZ = 512


def draw_permeability(key, part):
    key = jax.random.fold_in(key, 11)
    level_key, fine_key = jax.random.split(key, 2)
    nodes_x = NX // CB
    nodes_y = NY // CB
    levels = jax.random.uniform(level_key, (NZ, nodes_x, nodes_y), jnp.float32, -2.3, 2.3)
    fine = 0.6 * jax.random.normal(fine_key, (NZ, NX, NY), jnp.float32)
    blocky = jnp.repeat(jnp.repeat(levels, CB, axis=1), CB, axis=2)
    return jnp.clip(jnp.exp(blocky + fine), 0.1, 10.0).astype(jnp.float32)


def draw_source_term(key, part):
    key = jax.random.fold_in(key, 23)
    noise_key, amp_key, phase_key = jax.random.split(key, 3)
    along_x = (jnp.arange(NX).astype(jnp.float32) / NX)[None, :, None]
    along_y = (jnp.arange(NY).astype(jnp.float32) / NY)[None, None, :]
    noise = 0.2 * jax.random.normal(noise_key, (NZ, NX, NY), jnp.float32)
    smooth_scale = 0.003
    amps = jax.random.uniform(amp_key, (6, NZ), jnp.float32, 0.3, 1.0) * smooth_scale
    phases = jax.random.uniform(phase_key, (6, NZ), jnp.float32, -math.pi, math.pi)
    smooth = jnp.zeros((NZ, NX, NY), jnp.float32)
    for mode in range(3):
        wave = 2.0 * math.pi * (mode + 1)
        smooth = smooth + amps[mode][:, None, None] * jnp.cos(wave * along_x + phases[mode][:, None, None])
        smooth = smooth + amps[3 + mode][:, None, None] * jnp.cos(wave * along_y + phases[3 + mode][:, None, None])
    return jnp.clip(noise + smooth, -1.6, 1.6).astype(jnp.float32)


def steps_of(own_key, shape, pieces, low, high):
    factor_of = 1.0
    for axis_at, blocks in pieces:
        heights = jax.random.uniform(jax.random.fold_in(jax.random.fold_in(own_key, 6), axis_at), (blocks,), jnp.float32, low / len(pieces), high / len(pieces))
        factor_of = factor_of * jnp.repeat(jnp.exp(heights), shape[axis_at] // blocks).reshape((-1,) + (1,) * (len(shape) - 1 - axis_at))
    return factor_of


def setup_inputs(seed: int = 0) -> dict:
    splits = jax.random.split(jax.random.key(seed), 5)
    return {
        "permeability": draw_permeability(jax.random.fold_in(splits[4], 71), 0),
        "accumulation": jnp.clip(jnp.exp(math.log(0.001) - 2.3025852 * jax.random.uniform(splits[1], (NZ, NX, NY), jnp.float32) ** steps_of(splits[1], (NZ, NX, NY), ((0, 16), (1, 4), (2, 4)), -0.2, 0.2)), 0.0001, 0.001),
        "source_term": draw_source_term(jax.random.fold_in(splits[4], 71), 0),
        "vertical_trans": jnp.clip(jnp.exp(math.log(0.5) - 2.3025851 * jax.random.uniform(splits[3], (NZ, NX, NY), jnp.float32) ** steps_of(splits[3], (NZ, NX, NY), ((0, 16), (1, 4), (2, 4)), -0.2, 0.2)), 0.05, 0.5),
    }


HIGH = lax.Precision.HIGHEST
OFFSETS = ((0, 0), (1, 0), (0, 1), (1, 1))
PAIRS = ((0, 0), (0, 1), (0, 2), (0, 3), (1, 1), (1, 2), (1, 3), (2, 2), (2, 3), (3, 3))

def harmonic(left_perm, right_perm):
    return 2.0 * left_perm * right_perm / (left_perm + right_perm)

def bilinear_weights(frac_u, frac_v):
    return [(1.0 - frac_u) * (1.0 - frac_v), frac_u * (1.0 - frac_v), (1.0 - frac_u) * frac_v, frac_u * frac_v]

def orderings(first, second):
    if first == second:
        return ((first, first),)
    return ((first, second), (second, first))

def solve_layers(system):
    layer_count = system.shape[0]
    nodes_x = system.shape[2]
    nodes_y = system.shape[3]
    matrix = jnp.zeros((layer_count, nodes_x, nodes_y, nodes_x, nodes_y), jnp.float32)
    index_x = jnp.arange(nodes_x)
    index_y = jnp.arange(nodes_y)
    for code in range(9):
        step_x = code // 3 - 1
        step_y = code % 3 - 1
        hop_x = (index_x[None, :] == (index_x[:, None] + step_x) % nodes_x).astype(jnp.float32)
        hop_y = (index_y[None, :] == (index_y[:, None] + step_y) % nodes_y).astype(jnp.float32)
        matrix = matrix + jnp.einsum('lij,ia,jb->lijab', system[:, code], hop_x, hop_y, precision=HIGH)
    matrix = matrix.reshape(layer_count, nodes_x * nodes_y, nodes_x * nodes_y)
    factor = jnp.linalg.cholesky(matrix)
    right_side = system[:, 9].reshape(layer_count, nodes_x * nodes_y, 1)
    solved = jax.scipy.linalg.cho_solve((factor, True), right_side)
    return solved.reshape(layer_count, nodes_x, nodes_y)

def layer_cycle(layer_args):
    perm_layer, accum_layer, source_layer = layer_args
    half_block = CB // 2
    nodes_x = NX // CB
    nodes_y = NY // CB
    along_x = jnp.arange(NX)
    along_y = jnp.arange(NY)
    local_u = (along_x - half_block) % CB
    local_v = (along_y - half_block) % CB
    owner_x = (along_x - half_block) % NX // CB
    owner_y = (along_y - half_block) % NY // CB
    frac_u = (local_u.astype(jnp.float32) / CB)[:, None]
    frac_v = (local_v.astype(jnp.float32) / CB)[None, :]
    basis = jnp.stack(bilinear_weights(frac_u, frac_v)) * jnp.ones((1, NX, NY), jnp.float32)
    east_ghost = jnp.stack(bilinear_weights(jnp.ones_like(frac_v), frac_v))
    north_ghost = jnp.stack(bilinear_weights(frac_u, jnp.ones_like(frac_u)))
    east_edge = (local_u == CB - 1)[:, None]
    north_edge = (local_v == CB - 1)[None, :]
    interior = (local_u >= 1)[:, None] & (local_v >= 1)[None, :]
    t_east = harmonic(perm_layer, jnp.roll(perm_layer, -1, 0))
    t_west = jnp.roll(t_east, 1, 0)
    t_north = harmonic(perm_layer, jnp.roll(perm_layer, -1, 1))
    t_south = jnp.roll(t_north, 1, 1)
    total_t = t_west + t_east + t_south + t_north

    def sides(values):
        east_vals = jnp.where(east_edge, east_ghost, jnp.roll(values, -1, 1))
        north_vals = jnp.where(north_edge, north_ghost, jnp.roll(values, -1, 2))
        return (jnp.roll(values, 1, 1), east_vals, jnp.roll(values, 1, 2), north_vals)
    for sweep in range(SWEEPS):
        west_vals, east_vals, south_vals, north_vals = sides(basis)
        updated = (t_west * west_vals + t_east * east_vals + t_south * south_vals + t_north * north_vals) / total_t
        basis = jnp.where(interior, updated, basis)
    west_vals, east_vals, south_vals, north_vals = sides(basis)
    diff_east = basis - east_vals
    diff_north = basis - north_vals
    terms = []
    for first, second in PAIRS:
        terms.append(accum_layer * basis[first] * basis[second] + t_east * diff_east[first] * diff_east[second] + t_north * diff_north[first] * diff_north[second])
    for corner in range(4):
        terms.append(basis[corner] * source_layer)
    stacked = jnp.stack(terms)
    hot_x = (owner_x[:, None] == jnp.arange(nodes_x)[None, :]).astype(jnp.float32)
    hot_y = (owner_y[:, None] == jnp.arange(nodes_y)[None, :]).astype(jnp.float32)
    sums = jnp.einsum('fab,bj->faj', stacked, hot_y, precision=HIGH)
    sums = jnp.einsum('faj,ai->fij', sums, hot_x, precision=HIGH)
    stencil = jnp.zeros((10, nodes_x, nodes_y), jnp.float32)
    for position, (first, second) in enumerate(PAIRS):
        for row_corner, col_corner in orderings(first, second):
            shift_x, shift_y = OFFSETS[row_corner]
            code = (OFFSETS[col_corner][0] - shift_x + 1) * 3 + (OFFSETS[col_corner][1] - shift_y + 1)
            stencil = stencil.at[code].add(jnp.roll(sums[position], (shift_x, shift_y), (0, 1)))
    for corner in range(4):
        shift_x, shift_y = OFFSETS[corner]
        stencil = stencil.at[9].add(jnp.roll(sums[10 + corner], (shift_x, shift_y), (0, 1)))
    coarse = solve_layers(stencil[None])[0]
    pressure = jnp.zeros((NX, NY), jnp.float32)
    for corner in range(4):
        shift_x, shift_y = OFFSETS[corner]
        node_x = (owner_x + shift_x) % nodes_x
        node_y = (owner_y + shift_y) % nodes_y
        pressure = pressure + basis[corner] * coarse[node_x][:, node_y]
    flow = accum_layer * pressure + t_east * (pressure - jnp.roll(pressure, -1, 0)) + t_west * (pressure - jnp.roll(pressure, 1, 0))
    flow = flow + t_north * (pressure - jnp.roll(pressure, -1, 1)) + t_south * (pressure - jnp.roll(pressure, 1, 1))
    return (pressure, flow)

def reference(permeability, accumulation, source_term, vertical_trans):
    pressure, flow = lax.map(layer_cycle, (permeability, accumulation, source_term))
    zero_layer = jnp.zeros_like(pressure[:1])
    upper_t = jnp.concatenate([vertical_trans[:-1], jnp.zeros_like(vertical_trans[:1])], 0)
    lower_t = jnp.concatenate([jnp.zeros_like(vertical_trans[:1]), vertical_trans[:-1]], 0)
    above = jnp.concatenate([pressure[1:], zero_layer], 0)
    below = jnp.concatenate([zero_layer, pressure[:-1]], 0)
    flow = flow + upper_t * (pressure - above) + lower_t * (pressure - below)
    residual = source_term - flow
    return (pressure, residual)
```

```python
import jax
import jax.numpy as jnp
from jax import lax
from jax.experimental import pallas as pl
from jax.experimental.pallas import tpu as pltpu
from jax.sharding import PartitionSpec as P

SWEEPS = 8
LAYERS = 32
SIDE = 4
DEPTH = 16
DUALS = 9
MESH = pl.DeviceIdType.MESH
F32 = jnp.float32
LX, LY, LXY = 0, 1, 2


def lane_roll(value, groups):
    by = (groups * 32) % 128
    return value if by == 0 else pltpu.roll(value, by, axis=1)


def sub_roll(value, by):
    return pltpu.roll(value, by % 8, axis=0)


def inverse(value):
    guess = pl.reciprocal(value, approx=True)
    guess = guess * (2.0 - value * guess)
    return guess * (2.0 - value * guess)


def harmonic(left, right):
    return 2.0 * left * right * inverse(left + right)


def node_shift(value, by, row):
    if by % 8 == 0:
        return lane_roll(value, -(by // 8))
    turned = sub_roll(value, -by)
    if by > 0:
        return jnp.where(row < 8 - by, turned, lane_roll(turned, -1))
    return jnp.where(row >= -by, turned, lane_roll(turned, 1))


def factor(b):
    low = {}
    inv = [None] * 4
    for k in range(4):
        pivot = b[(k, k)]
        for m in range(k):
            if low.get((k, m)) is not None:
                pivot = pivot - low[(k, m)] * work[(k, m)]
        inv[k] = inverse(pivot)
        if k == 0:
            work = {}
        for i in range(k + 1, 4):
            entry = b[(i, k)]
            for m in range(k):
                if low.get((i, m)) is None or work.get((k, m)) is None:
                    continue
                term = low[(i, m)] * work[(k, m)]
                entry = -term if entry is None else entry - term
            work[(i, k)] = entry
            low[(i, k)] = None if entry is None else entry * inv[k]
    return low, inv


def forward(low, column):
    out = []
    for i in range(4):
        value = column[i]
        for m in range(i):
            if low[(i, m)] is not None and out[m] is not None:
                term = low[(i, m)] * out[m]
                value = -term if value is None else value - term
        out.append(value)
    return out


def scaled(inv, column):
    return [None if v is None else v * inv[k] for k, v in enumerate(column)]


def inner(left, right):
    total = None
    for a, b in zip(left, right):
        if a is None or b is None:
            continue
        total = a * b if total is None else total + a * b
    return total


def subtract(value, term):
    if term is None:
        return value
    return -term if value is None else value - term


def shift_or_none(value, by, row):
    return None if value is None else node_shift(value, by, row)


def solve_nodes(b, c, d, row):
    for step in (1, 2, 4, 8):
        a = [[shift_or_none(c[m][k], -step, row) for m in range(4)] for k in range(4)]
        low, inv = factor(b)
        up = [forward(low, [c[i][k] for i in range(4)]) for k in range(4)]
        down = [forward(low, [a[i][k] for i in range(4)]) for k in range(4)]
        side = scaled(inv, forward(low, d))
        up_s = [scaled(inv, col) for col in up]
        down_s = [scaled(inv, col) for col in down]
        new_b = {}
        for i in range(4):
            for k in range(i + 1):
                value = subtract(b[(i, k)], shift_or_none(inner(up[i], up_s[k]), -step, row))
                new_b[(i, k)] = subtract(value, shift_or_none(inner(down[i], down_s[k]), step, row))
        new_d = []
        for i in range(4):
            value = subtract(d[i], shift_or_none(inner(up[i], side), -step, row))
            new_d.append(subtract(value, shift_or_none(inner(down[i], side), step, row)))
        new_c = [
            [subtract(None, shift_or_none(inner(down[i], up_s[k]), step, row)) for k in range(4)]
            for i in range(4)
        ]
        b, c, d = new_b, new_c, new_d
    both = [[c[i][k] + node_shift(c[k][i], -16, row) for k in range(4)] for i in range(4)]
    low, inv = factor(b)
    cols = [forward(low, [both[i][k] for i in range(4)]) for k in range(4)]
    cols_s = [scaled(inv, col) for col in cols]
    side = scaled(inv, forward(low, d))
    last = {}
    for i in range(4):
        for k in range(i + 1):
            last[(i, k)] = b[(i, k)] - node_shift(inner(cols[i], cols_s[k]), 16, row)
    right = [d[i] - node_shift(inner(cols[i], side), 16, row) for i in range(4)]
    low, inv = factor(last)
    value = scaled(inv, forward(low, right))
    for i in (2, 1, 0):
        for k in range(i + 1, 4):
            value[i] = value[i] - low[(k, i)] * value[k]
    return value


def corner_sums(g, r):
    k = [
        g[(3, 3)],
        g[(2, 3)] - g[(3, 3)],
        g[(1, 3)] - g[(3, 3)],
        g[(0, 3)] - g[(1, 3)] - g[(2, 3)] + g[(3, 3)],
        g[(2, 2)] - 2.0 * g[(2, 3)] + g[(3, 3)],
        g[(1, 2)] - g[(1, 3)] - g[(2, 3)] + g[(3, 3)],
        (g[(0, 2)] - g[(1, 2)] - g[(2, 2)]) + (2.0 * g[(2, 3)] - g[(0, 3)] + g[(1, 3)] - g[(3, 3)]),
        g[(1, 1)] - 2.0 * g[(1, 3)] + g[(3, 3)],
        (g[(0, 1)] - g[(1, 1)] - g[(1, 2)]) + (2.0 * g[(1, 3)] - g[(0, 3)] + g[(2, 3)] - g[(3, 3)]),
        (g[(0, 0)] + g[(1, 1)] + g[(2, 2)] + g[(3, 3)])
        - 2.0 * (g[(0, 1)] + g[(0, 2)] + g[(1, 3)] + g[(2, 3)] - g[(0, 3)] - g[(1, 2)]),
        r[3],
        r[2] - r[3],
        r[1] - r[3],
        r[0] - r[1] - r[2] + r[3],
    ]
    return k


GRAM = ((0, 0), (0, 1), (0, 2), (0, 3), (1, 1), (1, 2), (1, 3), (2, 2), (2, 3), (3, 3))


def assemble(t, row):
    def back(value):
        return node_shift(value, -1, row)

    b, d = {}, []
    c = [[None] * 4 for _ in range(4)]
    for i in range(4):
        w = (i - 1) % 4
        b[(i, i)] = t[0][i] + t[4][w] + back(t[7][i] + t[9][w])
        d.append(t[10][i] + t[11][w] + back(t[12][i] + t[13][w]))
        edge = t[1][i] + back(t[8][i])
        e = (i + 1) % 4
        b[(max(i, e), min(i, e))] = edge
        c[i][i] = t[2][i] + t[6][w]
        c[i][e] = t[3][i]
        c[e][i] = t[5][i]
    b[(2, 0)] = None
    b[(3, 1)] = None
    return b, c, d


def kernel(
    perm, accum, source, vtrans, press_out, resid_out,
    hx, ax, sx, vt, row24, row8, tp, at, st, te, tn, co, bf, sums, ga, nodes, cb, pt, py, ry, fp, po, ro,
    up_layer, down_pair,
    local_sem, send_sem, recv_sem, gsend_sem, grecv_sem, out_sem,
):
    gx, gy, gz = lax.axis_index("gx"), lax.axis_index("gy"), lax.axis_index("gz")

    def peer(dx, dy, dz):
        return (
            lax.rem(gx + (dx + SIDE), SIDE),
            lax.rem(gy + (dy + SIDE), SIDE),
            lax.rem(gz + (dz + DEPTH), DEPTH),
        )

    local = [
        pltpu.make_async_copy(perm.at[:, 0], hx.at[1], local_sem.at[0]),
        pltpu.make_async_copy(perm.at[:, 1], hx.at[2], local_sem.at[1]),
        pltpu.make_async_copy(accum.at[:, 0], ax.at[1], local_sem.at[2]),
        pltpu.make_async_copy(accum.at[:, 1], ax.at[2], local_sem.at[3]),
        pltpu.make_async_copy(source.at[:, 0], sx.at[1], local_sem.at[4]),
        pltpu.make_async_copy(source.at[:, 1], sx.at[2], local_sem.at[5]),
        pltpu.make_async_copy(vtrans, vt, local_sem.at[6]),
    ]
    for copy in local:
        copy.start()

    barrier = pltpu.get_barrier_semaphore()
    for dx in range(SIDE):
        for dy in range(SIDE):
            if dx or dy:
                pl.semaphore_signal(barrier, inc=1, device_id=peer(dx, dy, 0), device_id_type=MESH)
    for dz in (-1, 1):
        pl.semaphore_signal(barrier, inc=1, device_id=peer(0, 0, dz), device_id_type=MESH)
    pl.semaphore_wait(barrier, 17)

    def remote(src, dst, at_sem, target):
        return pltpu.make_async_remote_copy(
            src_ref=src, dst_ref=dst, send_sem=send_sem.at[at_sem], recv_sem=recv_sem.at[at_sem],
            device_id=target, device_id_type=MESH,
        )

    west, east = peer(-1, 0, 0), peer(1, 0, 0)
    south, north = peer(0, -1, 0), peer(0, 1, 0)
    perm_w = remote(perm.at[:, 0], hx.at[3], 0, west)
    perm_e = remote(perm.at[:, 1], hx.at[0], 1, east)
    perm_w.start()
    perm_e.start()
    for copy in local[:2]:
        copy.wait()
    hx_rows = hx.reshape(4 * 256, 128)
    ax_rows = ax.reshape(4 * 256, 128)
    sx_rows = sx.reshape(4 * 256, 128)
    row8[...] = hx_rows[pl.ds(512, LAYERS, stride=8), :]
    perm_r = remote(row8, row24, 2, west)
    perm_r.start()
    accum_w = remote(accum.at[:, 0], ax.at[3], 3, west)
    source_w = remote(source.at[:, 0], sx.at[3], 4, west)
    accum_w.start()
    source_w.start()
    for copy in local[2:]:
        copy.wait()
    vt_up = remote(vt.at[pl.ds(496, 16)], down_pair.at[1], 5, peer(0, 0, 1))
    vt_up.start()

    row = lax.broadcasted_iota(jnp.int32, (8, 128), 0)
    lane = lax.broadcasted_iota(jnp.int32, (8, 128), 1)
    group = lane // 32
    u_base = jnp.where(group % 2 == 1, 8, 0)
    row0 = row == 0
    row7 = row == 7
    u0 = u_base == 0
    u8 = u_base == 8

    perm_w.wait()
    perm_e.wait()
    perm_r.wait()
    for x in range(8):
        tp[x, pl.ds(8, 128), :] = hx_rows[pl.ds(x, 128, stride=8), :].T
    tp[8, pl.ds(8, 128), :] = jnp.concatenate(
        [hx_rows[pl.ds(256, 96, stride=8), :], row24[...]], axis=0
    ).T
    strip_s = remote(tp.at[:, pl.ds(8, 16), :], tp.at[:, pl.ds(136, 16), :], 6, south)
    strip_n = remote(tp.at[:, pl.ds(128, 8), :], tp.at[:, pl.ds(0, 8), :], 7, north)
    strip_s.start()
    strip_n.start()
    accum_s = remote(at.at[:, pl.ds(8, 8), :], at.at[:, pl.ds(136, 8), :], 8, south)
    source_s = remote(st.at[:, pl.ds(8, 8), :], st.at[:, pl.ds(136, 8), :], 9, south)

    def relax(k, carry):
        d = lax.rem(k + 1, DUALS)

        @pl.when(k == 3)
        def _():
            accum_w.wait()
            source_w.wait()
            for x in range(8):
                at[x, pl.ds(8, 128), :] = ax_rows[pl.ds(x, 128, stride=8), :].T
                st[x, pl.ds(8, 128), :] = sx_rows[pl.ds(x, 128, stride=8), :].T
            accum_s.start()
            source_s.start()

        @pl.when(k == 7)
        def _():
            strip_s.wait()
            strip_n.wait()

        cells = [[tp[x, pl.ds(16 * d + p, 8, stride=2), :] for p in range(2)] for x in range(9)]
        t_e = [[harmonic(cells[x][p], cells[x + 1][p]) for p in range(2)] for x in range(8)]
        for x in range(8):
            after = tp[x, pl.ds(16 * d + 2, 8, stride=2), :]
            t_n = [harmonic(cells[x][0], cells[x][1]), harmonic(cells[x][1], after)]
            t_s = [sub_roll(t_n[1], 1), t_n[0]]
            for p in range(2):
                t_w = t_e[x - 1][p] if x else lane_roll(t_e[7][p], 1)
                te[d, x, p] = t_e[x][p]
                tn[d, x, p] = t_n[p]
                inv = inverse((t_w + t_e[x][p]) + (t_s[p] + t_n[p]))
                co[0, x, p] = t_w * inv
                co[1, x, p] = t_e[x][p] * inv
                co[2, x, p] = t_s[p] * inv
                co[3, x, p] = t_n[p] * inv
            co[4, x, 0] = jnp.where(row7, 0.0, co[3, x, 1])
        co[4, 0, 1] = jnp.where(u8, 0.0, co[1, 7, 0])
        co[4, 1, 1] = jnp.where(u8, 0.0, co[1, 7, 1])

        fixed = [[row0 | u0, u0]] + [[row0, None]] * 7
        for kind in range(3):
            vals = []
            for x in range(8):
                along_x = 1.0 - (u_base + x).astype(F32) / 16.0
                pair = []
                for p in range(2):
                    along_y = 1.0 - (2 * row + p).astype(F32) / 16.0
                    pair.append((along_x, along_y, along_x * along_y)[kind])
                vals.append(pair)
            for _ in range(SWEEPS):
                new = []
                for x in range(8):
                    pair = []
                    for p in range(2):
                        west_v = vals[x - 1][p] if x else lane_roll(vals[7][p], 1)
                        east_v = vals[x + 1][p] if x < 7 else lane_roll(vals[0][p], -1)
                        south_v = vals[x][0] if p else sub_roll(vals[x][1], 1)
                        north_v = sub_roll(vals[x][0], -1) if p else vals[x][1]
                        c_e = co[4, p, 1] if x == 7 and kind != LY else co[1, x, p]
                        c_n = co[4, x, 0] if p and kind != LX else co[3, x, p]
                        value = (co[0, x, p] * west_v + c_e * east_v) + (co[2, x, p] * south_v + c_n * north_v)
                        keep = fixed[x][p]
                        pair.append(value if keep is None else jnp.where(keep, vals[x][p], value))
                    new.append(pair)
                vals = new
            for x in range(8):
                for p in range(2):
                    bf[kind, d, x, p] = vals[x][p]
        return carry

    lax.fori_loop(0, DUALS, relax, 0)

    def gram(d, carry):
        @pl.when(d == 8)
        def _():
            accum_s.wait()
            source_s.wait()

        acc = {}

        def add(key, value):
            acc[key] = value if key not in acc else acc[key] + value

        for x in range(8):
            for p in range(2):
                a = at[x, pl.ds(16 * d + p, 8, stride=2), :]
                s = st[x, pl.ds(16 * d + p, 8, stride=2), :]
                here = [bf[kind, d, x, p] for kind in range(3)]
                t_e, t_n = te[d, x, p], tn[d, x, p]
                mass, d_e, d_n = [], [], []
                for kind in range(3):
                    if x < 7:
                        east_v = bf[kind, d, x + 1, p]
                    else:
                        east_v = lane_roll(bf[kind, d, 0, p], -1)
                        if kind != LY:
                            east_v = jnp.where(u8, 0.0, east_v)
                    if p:
                        north_v = sub_roll(bf[kind, d, x, 0], -1)
                        if kind != LX:
                            north_v = jnp.where(row7, 0.0, north_v)
                    else:
                        north_v = bf[kind, d, x, 1]
                    d_e.append(here[kind] - east_v)
                    d_n.append(here[kind] - north_v)
                    mass.append(a * here[kind])
                add((0, 0), a)
                add("r0", s)
                for kind in range(3):
                    add((0, kind + 1), mass[kind])
                    add("r" + str(kind + 1), s * here[kind])
                    w_e, w_n = t_e * d_e[kind], t_n * d_n[kind]
                    for other in range(kind, 3):
                        add((kind + 1, other + 1), mass[kind] * here[other] + w_e * d_e[other] + w_n * d_n[other])
        mine = row == d - 1
        for index, key in enumerate(GRAM + ("r0", "r1", "r2", "r3")):
            value = acc[key]
            value = value + sub_roll(value, 4)
            value = value + sub_roll(value, 2)
            value = value + sub_roll(value, 1)
            sums[index] = jnp.where(mine, value, sums[index])
        return carry

    lax.fori_loop(1, DUALS, gram, 0)

    whole = []
    for index in range(14):
        value = sums[index]
        whole.append(value + lane_roll(value, -1))
    entries = corner_sums({key: whole[i] for i, key in enumerate(GRAM)}, whole[10:])
    for k in range(4):
        packed = jnp.zeros((8, 128), F32)
        for q in range(4):
            if 4 * k + q < 14:
                packed = jnp.where(group == q, lane_roll(entries[4 * k + q], q - 2), packed)
        ga[0, k] = packed
    gathers = []
    for dx in range(SIDE):
        for dy in range(SIDE):
            if dx or dy:
                slot = (-dx % SIDE) * SIDE + (-dy % SIDE)
                gathers.append(
                    pltpu.make_async_remote_copy(
                        src_ref=ga.at[0], dst_ref=ga.at[slot],
                        send_sem=gsend_sem.at[slot], recv_sem=grecv_sem.at[slot],
                        device_id=peer(dx, dy, 0), device_id_type=MESH,
                    )
                )
    for copy in gathers:
        copy.start()
    for copy in gathers:
        copy.wait()

    table = []
    for index in range(14):
        k, q = index // 4, index % 4
        by_x = []
        for i in range(SIDE):
            value = lane_roll(ga[i * SIDE, k], -q)
            for g in range(1, SIDE):
                value = jnp.where(group == g, lane_roll(ga[i * SIDE + g, k], g - q), value)
            by_x.append(value)
        table.append(by_x)
    b, c, d_side = assemble(table, row)
    coarse = solve_nodes(b, c, d_side, row)

    def everywhere(value, g):
        value = jnp.where(group == g, value, 0.0)
        value = value + lane_roll(value, 1)
        return value + lane_roll(value, 2)

    first_half = lane < 64
    for at_row, g in ((0, 3), (8, 0), (16, 1)):
        mid = everywhere(coarse[0], g)
        nodes[0, pl.ds(at_row, 8), :] = jnp.where(first_half, everywhere(coarse[3], g), mid)
        nodes[1, pl.ds(at_row, 8), :] = jnp.where(first_half, mid, everywhere(coarse[1], g))
    for d in range(DUALS):
        c0 = jnp.broadcast_to(nodes[0, pl.ds(7 + d, 1), :], (8, 128))
        c1 = jnp.broadcast_to(nodes[1, pl.ds(7 + d, 1), :], (8, 128))
        c2 = jnp.broadcast_to(nodes[0, pl.ds(8 + d, 1), :], (8, 128))
        c3 = jnp.broadcast_to(nodes[1, pl.ds(8 + d, 1), :], (8, 128))
        cb[d, 0] = c3
        cb[d, 1] = c2 - c3
        cb[d, 2] = c1 - c3
        cb[d, 3] = (c0 - c1) - (c2 - c3)

    def interpolate(d, carry):
        w = [cb[d, k] for k in range(4)]
        for x in range(8):
            for p in range(2):
                value = (w[0] + w[1] * bf[0, d, x, p]) + (w[2] * bf[1, d, x, p] + w[3] * bf[2, d, x, p])
                pt[d, x, p] = value
                py[x, pl.ds(16 * d + p, 8, stride=2), :] = value
        return carry

    lax.fori_loop(0, DUALS, interpolate, 0)

    lane_full = lax.broadcasted_iota(jnp.int32, (128, 128), 1)
    middle = (lane_full >= 32) & (lane_full < 96)

    def to_rows(src, dst):
        for x in range(0, 8, 2):
            both = jnp.where(
                middle, src[x, pl.ds(8, 128), :], pltpu.roll(src[x + 1, pl.ds(8, 128), :], 64, axis=1)
            ).T
            dst[pl.ds(x, 32, stride=16), :] = both[32:64]
            dst[pl.ds(8 + x, 32, stride=16), :] = both[64:96]
            dst[pl.ds(x + 1, 32, stride=16), :] = both[96:128]
            dst[pl.ds(9 + x, 32, stride=16), :] = both[0:32]

    to_rows(py, po)
    low_send = remote(po.at[pl.ds(0, 16)], up_layer, 10, peer(0, 0, -1))
    high_send = remote(po.at[pl.ds(496, 16)], down_pair.at[0], 11, peer(0, 0, 1))
    low_send.start()
    high_send.start()
    press_copy = pltpu.make_async_copy(po, press_out, out_sem.at[0])
    press_copy.start()

    def balance(d, carry):
        val = [[pt[d, x, p] for p in range(2)] for x in range(8)]
        f_e = [[None, None] for _ in range(8)]
        for x in range(8):
            for p in range(2):
                east_v = val[x + 1][p] if x < 7 else lane_roll(val[0][p], -1)
                f_e[x][p] = te[d, x, p] * (val[x][p] - east_v)
        for x in range(8):
            after = sub_roll(jnp.where(row0, pt[d + 1, x, 0], val[x][0]), -1)
            f_n0 = tn[d, x, 0] * (val[x][0] - val[x][1])
            f_n1 = tn[d, x, 1] * (val[x][1] - after)
            before = sub_roll(jnp.where(row7, fp[x], f_n1), 1)
            fp[x] = f_n1
            f_n = (f_n0, f_n1)
            f_s = (before, f_n0)
            for p in range(2):
                f_w = f_e[x - 1][p] if x else lane_roll(f_e[7][p], 1)
                a = at[x, pl.ds(16 * d + p, 8, stride=2), :]
                s = st[x, pl.ds(16 * d + p, 8, stride=2), :]
                flow = a * val[x][p] + (f_e[x][p] - f_w) + (f_n[p] - f_s[p])
                ry[x, pl.ds(16 * d + p, 8, stride=2), :] = s - flow
        return carry

    lax.fori_loop(0, DUALS, balance, 0)
    to_rows(ry, ro)

    def vertical(l, carry):
        r0 = pl.multiple_of(l * 16, 16)
        here = po[pl.ds(r0, 16), :]
        f_up = vt[pl.ds(r0, 16), :] * (here - po[pl.ds(r0 + 16, 16), :])
        ro[pl.ds(r0, 16), :] = ro[pl.ds(r0, 16), :] - f_up + carry
        return f_up

    last_flux = lax.fori_loop(0, LAYERS - 1, vertical, jnp.zeros((16, 128), F32))
    vt_up.wait()
    low_send.wait()
    high_send.wait()
    above = jnp.where(gz < DEPTH - 1, vt[pl.ds(496, 16), :] * (po[pl.ds(496, 16), :] - up_layer[...]), 0.0)
    below = jnp.where(gz > 0, down_pair[1] * (down_pair[0] - po[pl.ds(0, 16), :]), 0.0)
    ro[pl.ds(496, 16), :] = ro[pl.ds(496, 16), :] - above + last_flux
    ro[pl.ds(0, 16), :] = ro[pl.ds(0, 16), :] + below
    resid_copy = pltpu.make_async_copy(ro, resid_out, out_sem.at[1])
    resid_copy.start()
    press_copy.wait()
    resid_copy.wait()


def body(permeability, accumulation, source_term, vertical_trans):
    split = (LAYERS, 2, 8, 128)
    vmem = lambda *shape: pltpu.VMEM(shape, F32)
    anywhere = pl.BlockSpec(memory_space=pl.ANY)
    pressure, residual = pl.pallas_call(
        kernel,
        out_shape=[jax.ShapeDtypeStruct((512, 128), F32)] * 2,
        in_specs=[anywhere] * 4,
        out_specs=[anywhere] * 2,
        scratch_shapes=[
            vmem(4, 32, 8, 128),
            vmem(4, 32, 8, 128),
            vmem(4, 32, 8, 128),
            vmem(512, 128),
            vmem(32, 128),
            vmem(32, 128),
            vmem(9, 152, 128),
            vmem(8, 144, 128),
            vmem(8, 144, 128),
            vmem(9, 8, 2, 8, 128),
            vmem(9, 8, 2, 8, 128),
            vmem(5, 8, 2, 8, 128),
            vmem(3, 9, 8, 2, 8, 128),
            vmem(14, 8, 128),
            vmem(16, 4, 8, 128),
            vmem(2, 24, 128),
            vmem(9, 4, 8, 128),
            vmem(10, 8, 2, 8, 128),
            vmem(8, 144, 128),
            vmem(8, 144, 128),
            vmem(8, 8, 128),
            vmem(512, 128),
            vmem(512, 128),
            vmem(16, 128),
            vmem(2, 16, 128),
            pltpu.SemaphoreType.DMA((7,)),
            pltpu.SemaphoreType.DMA((12,)),
            pltpu.SemaphoreType.DMA((12,)),
            pltpu.SemaphoreType.DMA((16,)),
            pltpu.SemaphoreType.DMA((16,)),
            pltpu.SemaphoreType.DMA((2,)),
        ],
        compiler_params=pltpu.CompilerParams(
            collective_id=0, has_side_effects=True, vmem_limit_bytes=40 * 1024 * 1024
        ),
    )(
        permeability.reshape(split),
        accumulation.reshape(split),
        source_term.reshape(split),
        vertical_trans.reshape(512, 128),
    )
    return pressure.reshape(32, 16, 128), residual.reshape(32, 16, 128)


def solution(mesh):
    spec = P("gz", "gx", "gy")
    return jax.shard_map(
        body, mesh=mesh, in_specs=(spec,) * 4, out_specs=(spec, spec), check_vma=False
    )
```

```python
import jax
import jax.numpy as jnp
from jax import lax
from jax.experimental import pallas as pl
from jax.experimental.pallas import tpu as pltpu
from jax.sharding import PartitionSpec as P

SWEEPS = 8
LAYERS = 32
SIDE = 4
DEPTH = 16
DUALS = 9
MESH = pl.DeviceIdType.MESH
F32 = jnp.float32
LX, LY, LXY = 0, 1, 2


def lane_roll(value, groups):
    by = (groups * 32) % 128
    return value if by == 0 else pltpu.roll(value, by, axis=1)


def sub_roll(value, by):
    return pltpu.roll(value, by % 8, axis=0)


def inverse(value):
    guess = pl.reciprocal(value, approx=True)
    guess = guess * (2.0 - value * guess)
    return guess * (2.0 - value * guess)


def harmonic(left, right):
    return 2.0 * left * right * inverse(left + right)


def node_shift(value, by, row):
    if by % 8 == 0:
        return lane_roll(value, -(by // 8))
    turned = sub_roll(value, -by)
    if by > 0:
        return jnp.where(row < 8 - by, turned, lane_roll(turned, -1))
    return jnp.where(row >= -by, turned, lane_roll(turned, 1))


def factor(b):
    low = {}
    inv = [None] * 4
    for k in range(4):
        pivot = b[(k, k)]
        for m in range(k):
            if low.get((k, m)) is not None:
                pivot = pivot - low[(k, m)] * work[(k, m)]
        inv[k] = inverse(pivot)
        if k == 0:
            work = {}
        for i in range(k + 1, 4):
            entry = b[(i, k)]
            for m in range(k):
                if low.get((i, m)) is None or work.get((k, m)) is None:
                    continue
                term = low[(i, m)] * work[(k, m)]
                entry = -term if entry is None else entry - term
            work[(i, k)] = entry
            low[(i, k)] = None if entry is None else entry * inv[k]
    return low, inv


def forward(low, column):
    out = []
    for i in range(4):
        value = column[i]
        for m in range(i):
            if low[(i, m)] is not None and out[m] is not None:
                term = low[(i, m)] * out[m]
                value = -term if value is None else value - term
        out.append(value)
    return out


def scaled(inv, column):
    return [None if v is None else v * inv[k] for k, v in enumerate(column)]


def inner(left, right):
    total = None
    for a, b in zip(left, right):
        if a is None or b is None:
            continue
        total = a * b if total is None else total + a * b
    return total


def subtract(value, term):
    if term is None:
        return value
    return -term if value is None else value - term


def shift_or_none(value, by, row):
    return None if value is None else node_shift(value, by, row)


def solve_nodes(b, c, d, row):
    for step in (1, 2, 4, 8):
        a = [[shift_or_none(c[m][k], -step, row) for m in range(4)] for k in range(4)]
        low, inv = factor(b)
        up = [forward(low, [c[i][k] for i in range(4)]) for k in range(4)]
        down = [forward(low, [a[i][k] for i in range(4)]) for k in range(4)]
        side = scaled(inv, forward(low, d))
        up_s = [scaled(inv, col) for col in up]
        down_s = [scaled(inv, col) for col in down]
        new_b = {}
        for i in range(4):
            for k in range(i + 1):
                value = subtract(b[(i, k)], shift_or_none(inner(up[i], up_s[k]), -step, row))
                new_b[(i, k)] = subtract(value, shift_or_none(inner(down[i], down_s[k]), step, row))
        new_d = []
        for i in range(4):
            value = subtract(d[i], shift_or_none(inner(up[i], side), -step, row))
            new_d.append(subtract(value, shift_or_none(inner(down[i], side), step, row)))
        new_c = [
            [subtract(None, shift_or_none(inner(down[i], up_s[k]), step, row)) for k in range(4)]
            for i in range(4)
        ]
        b, c, d = new_b, new_c, new_d
    both = [[c[i][k] + node_shift(c[k][i], -16, row) for k in range(4)] for i in range(4)]
    low, inv = factor(b)
    cols = [forward(low, [both[i][k] for i in range(4)]) for k in range(4)]
    cols_s = [scaled(inv, col) for col in cols]
    side = scaled(inv, forward(low, d))
    last = {}
    for i in range(4):
        for k in range(i + 1):
            last[(i, k)] = b[(i, k)] - node_shift(inner(cols[i], cols_s[k]), 16, row)
    right = [d[i] - node_shift(inner(cols[i], side), 16, row) for i in range(4)]
    low, inv = factor(last)
    value = scaled(inv, forward(low, right))
    for i in (2, 1, 0):
        for k in range(i + 1, 4):
            value[i] = value[i] - low[(k, i)] * value[k]
    return value


def corner_sums(g, r):
    k = [
        g[(3, 3)],
        g[(2, 3)] - g[(3, 3)],
        g[(1, 3)] - g[(3, 3)],
        g[(0, 3)] - g[(1, 3)] - g[(2, 3)] + g[(3, 3)],
        g[(2, 2)] - 2.0 * g[(2, 3)] + g[(3, 3)],
        g[(1, 2)] - g[(1, 3)] - g[(2, 3)] + g[(3, 3)],
        (g[(0, 2)] - g[(1, 2)] - g[(2, 2)]) + (2.0 * g[(2, 3)] - g[(0, 3)] + g[(1, 3)] - g[(3, 3)]),
        g[(1, 1)] - 2.0 * g[(1, 3)] + g[(3, 3)],
        (g[(0, 1)] - g[(1, 1)] - g[(1, 2)]) + (2.0 * g[(1, 3)] - g[(0, 3)] + g[(2, 3)] - g[(3, 3)]),
        (g[(0, 0)] + g[(1, 1)] + g[(2, 2)] + g[(3, 3)])
        - 2.0 * (g[(0, 1)] + g[(0, 2)] + g[(1, 3)] + g[(2, 3)] - g[(0, 3)] - g[(1, 2)]),
        r[3],
        r[2] - r[3],
        r[1] - r[3],
        r[0] - r[1] - r[2] + r[3],
    ]
    return k


GRAM = ((0, 0), (0, 1), (0, 2), (0, 3), (1, 1), (1, 2), (1, 3), (2, 2), (2, 3), (3, 3))


def assemble(t, row):
    def back(value):
        return node_shift(value, -1, row)

    b, d = {}, []
    c = [[None] * 4 for _ in range(4)]
    for i in range(4):
        w = (i - 1) % 4
        b[(i, i)] = t[0][i] + t[4][w] + back(t[7][i] + t[9][w])
        d.append(t[10][i] + t[11][w] + back(t[12][i] + t[13][w]))
        edge = t[1][i] + back(t[8][i])
        e = (i + 1) % 4
        b[(max(i, e), min(i, e))] = edge
        c[i][i] = t[2][i] + t[6][w]
        c[i][e] = t[3][i]
        c[e][i] = t[5][i]
    b[(2, 0)] = None
    b[(3, 1)] = None
    return b, c, d


def kernel(
    perm, accum, source, vtrans, press_out, resid_out,
    hx, ax, sx, vt, row24, row8, tp, at, st, te, tn, co, bf, sums, ga, nodes, cb, pt, py, ry, fp, po, ro,
    up_layer, down_pair,
    local_sem, send_sem, recv_sem, gsend_sem, grecv_sem, out_sem,
):
    gx, gy, gz = lax.axis_index("gx"), lax.axis_index("gy"), lax.axis_index("gz")

    def peer(dx, dy, dz):
        return (
            lax.rem(gx + (dx + SIDE), SIDE),
            lax.rem(gy + (dy + SIDE), SIDE),
            lax.rem(gz + (dz + DEPTH), DEPTH),
        )

    local = [
        pltpu.make_async_copy(perm.at[:, 0], hx.at[1], local_sem.at[0]),
        pltpu.make_async_copy(perm.at[:, 1], hx.at[2], local_sem.at[1]),
        pltpu.make_async_copy(accum.at[:, 0], ax.at[1], local_sem.at[2]),
        pltpu.make_async_copy(accum.at[:, 1], ax.at[2], local_sem.at[3]),
        pltpu.make_async_copy(source.at[:, 0], sx.at[1], local_sem.at[4]),
        pltpu.make_async_copy(source.at[:, 1], sx.at[2], local_sem.at[5]),
        pltpu.make_async_copy(vtrans, vt, local_sem.at[6]),
    ]
    for copy in local:
        copy.start()

    barrier = pltpu.get_barrier_semaphore()
    for dx in range(SIDE):
        for dy in range(SIDE):
            if dx or dy:
                pl.semaphore_signal(barrier, inc=1, device_id=peer(dx, dy, 0), device_id_type=MESH)
    has_below, has_above = gz > 0, gz < DEPTH - 1
    for dz, there in ((-1, has_below), (1, has_above)):

        @pl.when(there)
        def _():
            pl.semaphore_signal(barrier, inc=1, device_id=peer(0, 0, dz), device_id_type=MESH)

    pl.semaphore_wait(barrier, 15 + jnp.minimum(gz, 1) + jnp.minimum(DEPTH - 1 - gz, 1))

    def remote(src, dst, at_sem, target):
        return pltpu.make_async_remote_copy(
            src_ref=src, dst_ref=dst, send_sem=send_sem.at[at_sem], recv_sem=recv_sem.at[at_sem],
            device_id=target, device_id_type=MESH,
        )

    west, east = peer(-1, 0, 0), peer(1, 0, 0)
    south, north = peer(0, -1, 0), peer(0, 1, 0)
    perm_w = remote(perm.at[:, 0], hx.at[3], 0, west)
    perm_e = remote(perm.at[:, 1], hx.at[0], 1, east)
    perm_w.start()
    perm_e.start()
    for copy in local[:2]:
        copy.wait()
    hx_rows = hx.reshape(4 * 256, 128)
    ax_rows = ax.reshape(4 * 256, 128)
    sx_rows = sx.reshape(4 * 256, 128)
    row8[...] = hx_rows[pl.ds(512, LAYERS, stride=8), :]
    perm_r = remote(row8, row24, 2, west)
    perm_r.start()
    accum_w = remote(accum.at[:, 0], ax.at[3], 3, west)
    source_w = remote(source.at[:, 0], sx.at[3], 4, west)
    accum_w.start()
    source_w.start()
    for copy in local[2:]:
        copy.wait()
    vt_up = remote(vt.at[pl.ds(496, 16)], down_pair.at[1], 5, peer(0, 0, 1))

    @pl.when(has_above)
    def _():
        vt_up.start()

    row = lax.broadcasted_iota(jnp.int32, (8, 128), 0)
    lane = lax.broadcasted_iota(jnp.int32, (8, 128), 1)
    group = lane // 32
    u_base = jnp.where(group % 2 == 1, 8, 0)
    row0 = row == 0
    row7 = row == 7
    u0 = u_base == 0
    u8 = u_base == 8

    perm_w.wait()
    perm_e.wait()
    perm_r.wait()
    for x in range(8):
        tp[x, pl.ds(8, 128), :] = hx_rows[pl.ds(x, 128, stride=8), :].T
    tp[8, pl.ds(8, 128), :] = jnp.concatenate(
        [hx_rows[pl.ds(256, 96, stride=8), :], row24[...]], axis=0
    ).T
    strip_s = remote(tp.at[:, pl.ds(8, 16), :], tp.at[:, pl.ds(136, 16), :], 6, south)
    strip_n = remote(tp.at[:, pl.ds(128, 8), :], tp.at[:, pl.ds(0, 8), :], 7, north)
    strip_s.start()
    strip_n.start()
    accum_s = remote(at.at[:, pl.ds(8, 8), :], at.at[:, pl.ds(136, 8), :], 8, south)
    source_s = remote(st.at[:, pl.ds(8, 8), :], st.at[:, pl.ds(136, 8), :], 9, south)

    def relax(k, carry):
        d = lax.rem(k + 1, DUALS)

        @pl.when(k == 3)
        def _():
            accum_w.wait()
            source_w.wait()
            for x in range(8):
                at[x, pl.ds(8, 128), :] = ax_rows[pl.ds(x, 128, stride=8), :].T
                st[x, pl.ds(8, 128), :] = sx_rows[pl.ds(x, 128, stride=8), :].T
            accum_s.start()
            source_s.start()

        @pl.when(k == 7)
        def _():
            strip_s.wait()
            strip_n.wait()

        cells = [[tp[x, pl.ds(16 * d + p, 8, stride=2), :] for p in range(2)] for x in range(9)]
        t_e = [[harmonic(cells[x][p], cells[x + 1][p]) for p in range(2)] for x in range(8)]
        for x in range(8):
            after = tp[x, pl.ds(16 * d + 2, 8, stride=2), :]
            t_n = [harmonic(cells[x][0], cells[x][1]), harmonic(cells[x][1], after)]
            t_s = [sub_roll(t_n[1], 1), t_n[0]]
            for p in range(2):
                t_w = t_e[x - 1][p] if x else lane_roll(t_e[7][p], 1)
                te[d, x, p] = t_e[x][p]
                tn[d, x, p] = t_n[p]
                inv = inverse((t_w + t_e[x][p]) + (t_s[p] + t_n[p]))
                co[0, x, p] = t_w * inv
                co[1, x, p] = t_e[x][p] * inv
                co[2, x, p] = t_s[p] * inv
                co[3, x, p] = t_n[p] * inv
            co[4, x, 0] = jnp.where(row7, 0.0, co[3, x, 1])
        co[4, 0, 1] = jnp.where(u8, 0.0, co[1, 7, 0])
        co[4, 1, 1] = jnp.where(u8, 0.0, co[1, 7, 1])

        fixed = [[row0 | u0, u0]] + [[row0, None]] * 7
        for kind in range(3):
            vals = []
            for x in range(8):
                along_x = 1.0 - (u_base + x).astype(F32) / 16.0
                pair = []
                for p in range(2):
                    along_y = 1.0 - (2 * row + p).astype(F32) / 16.0
                    pair.append((along_x, along_y, along_x * along_y)[kind])
                vals.append(pair)
            for _ in range(SWEEPS):
                new = []
                for x in range(8):
                    pair = []
                    for p in range(2):
                        west_v = vals[x - 1][p] if x else lane_roll(vals[7][p], 1)
                        east_v = vals[x + 1][p] if x < 7 else lane_roll(vals[0][p], -1)
                        south_v = vals[x][0] if p else sub_roll(vals[x][1], 1)
                        north_v = sub_roll(vals[x][0], -1) if p else vals[x][1]
                        c_e = co[4, p, 1] if x == 7 and kind != LY else co[1, x, p]
                        c_n = co[4, x, 0] if p and kind != LX else co[3, x, p]
                        value = (co[0, x, p] * west_v + c_e * east_v) + (co[2, x, p] * south_v + c_n * north_v)
                        keep = fixed[x][p]
                        pair.append(value if keep is None else jnp.where(keep, vals[x][p], value))
                    new.append(pair)
                vals = new
            for x in range(8):
                for p in range(2):
                    bf[kind, d, x, p] = vals[x][p]
        return carry

    lax.fori_loop(0, DUALS, relax, 0)

    def gram(d, carry):
        @pl.when(d == 8)
        def _():
            accum_s.wait()
            source_s.wait()

        acc = {}

        def add(key, value):
            acc[key] = value if key not in acc else acc[key] + value

        for x in range(8):
            for p in range(2):
                a = at[x, pl.ds(16 * d + p, 8, stride=2), :]
                s = st[x, pl.ds(16 * d + p, 8, stride=2), :]
                here = [bf[kind, d, x, p] for kind in range(3)]
                t_e, t_n = te[d, x, p], tn[d, x, p]
                mass, d_e, d_n = [], [], []
                for kind in range(3):
                    if x < 7:
                        east_v = bf[kind, d, x + 1, p]
                    else:
                        east_v = lane_roll(bf[kind, d, 0, p], -1)
                        if kind != LY:
                            east_v = jnp.where(u8, 0.0, east_v)
                    if p:
                        north_v = sub_roll(bf[kind, d, x, 0], -1)
                        if kind != LX:
                            north_v = jnp.where(row7, 0.0, north_v)
                    else:
                        north_v = bf[kind, d, x, 1]
                    d_e.append(here[kind] - east_v)
                    d_n.append(here[kind] - north_v)
                    mass.append(a * here[kind])
                add((0, 0), a)
                add("r0", s)
                for kind in range(3):
                    add((0, kind + 1), mass[kind])
                    add("r" + str(kind + 1), s * here[kind])
                    w_e, w_n = t_e * d_e[kind], t_n * d_n[kind]
                    for other in range(kind, 3):
                        add((kind + 1, other + 1), mass[kind] * here[other] + w_e * d_e[other] + w_n * d_n[other])
        mine = row == d - 1
        for index, key in enumerate(GRAM + ("r0", "r1", "r2", "r3")):
            value = acc[key]
            value = value + sub_roll(value, 4)
            value = value + sub_roll(value, 2)
            value = value + sub_roll(value, 1)
            sums[index] = jnp.where(mine, value, sums[index])
        return carry

    lax.fori_loop(1, DUALS, gram, 0)

    whole = []
    for index in range(14):
        value = sums[index]
        whole.append(value + lane_roll(value, -1))
    entries = corner_sums({key: whole[i] for i, key in enumerate(GRAM)}, whole[10:])
    for k in range(4):
        packed = jnp.zeros((8, 128), F32)
        for q in range(4):
            if 4 * k + q < 14:
                packed = jnp.where(group == q, lane_roll(entries[4 * k + q], q - 2), packed)
        ga[0, k] = packed
    gathers = []
    for dx in range(SIDE):
        for dy in range(SIDE):
            if dx or dy:
                slot = (-dx % SIDE) * SIDE + (-dy % SIDE)
                gathers.append(
                    pltpu.make_async_remote_copy(
                        src_ref=ga.at[0], dst_ref=ga.at[slot],
                        send_sem=gsend_sem.at[slot], recv_sem=grecv_sem.at[slot],
                        device_id=peer(dx, dy, 0), device_id_type=MESH,
                    )
                )
    for copy in gathers:
        copy.start()
    for copy in gathers:
        copy.wait()

    table = []
    for index in range(14):
        k, q = index // 4, index % 4
        by_x = []
        for i in range(SIDE):
            value = lane_roll(ga[i * SIDE, k], -q)
            for g in range(1, SIDE):
                value = jnp.where(group == g, lane_roll(ga[i * SIDE + g, k], g - q), value)
            by_x.append(value)
        table.append(by_x)
    b, c, d_side = assemble(table, row)
    coarse = solve_nodes(b, c, d_side, row)

    def everywhere(value, g):
        value = jnp.where(group == g, value, 0.0)
        value = value + lane_roll(value, 1)
        return value + lane_roll(value, 2)

    first_half = lane < 64
    for at_row, g in ((0, 3), (8, 0), (16, 1)):
        mid = everywhere(coarse[0], g)
        nodes[0, pl.ds(at_row, 8), :] = jnp.where(first_half, everywhere(coarse[3], g), mid)
        nodes[1, pl.ds(at_row, 8), :] = jnp.where(first_half, mid, everywhere(coarse[1], g))
    for d in range(DUALS):
        c0 = jnp.broadcast_to(nodes[0, pl.ds(7 + d, 1), :], (8, 128))
        c1 = jnp.broadcast_to(nodes[1, pl.ds(7 + d, 1), :], (8, 128))
        c2 = jnp.broadcast_to(nodes[0, pl.ds(8 + d, 1), :], (8, 128))
        c3 = jnp.broadcast_to(nodes[1, pl.ds(8 + d, 1), :], (8, 128))
        cb[d, 0] = c3
        cb[d, 1] = c2 - c3
        cb[d, 2] = c1 - c3
        cb[d, 3] = (c0 - c1) - (c2 - c3)

    def interpolate(d, carry):
        w = [cb[d, k] for k in range(4)]
        for x in range(8):
            for p in range(2):
                value = (w[0] + w[1] * bf[0, d, x, p]) + (w[2] * bf[1, d, x, p] + w[3] * bf[2, d, x, p])
                pt[d, x, p] = value
                py[x, pl.ds(16 * d + p, 8, stride=2), :] = value
        return carry

    lax.fori_loop(0, DUALS, interpolate, 0)

    lane_full = lax.broadcasted_iota(jnp.int32, (128, 128), 1)
    middle = (lane_full >= 32) & (lane_full < 96)

    def to_rows(src, dst):
        for x in range(0, 8, 2):
            both = jnp.where(
                middle, src[x, pl.ds(8, 128), :], pltpu.roll(src[x + 1, pl.ds(8, 128), :], 64, axis=1)
            ).T
            dst[pl.ds(x, 32, stride=16), :] = both[32:64]
            dst[pl.ds(8 + x, 32, stride=16), :] = both[64:96]
            dst[pl.ds(x + 1, 32, stride=16), :] = both[96:128]
            dst[pl.ds(9 + x, 32, stride=16), :] = both[0:32]

    to_rows(py, po)
    low_send = remote(po.at[pl.ds(0, 16)], up_layer, 10, peer(0, 0, -1))
    high_send = remote(po.at[pl.ds(496, 16)], down_pair.at[0], 11, peer(0, 0, 1))

    @pl.when(has_below)
    def _():
        low_send.start()

    @pl.when(has_above)
    def _():
        high_send.start()

    press_copy = pltpu.make_async_copy(po, press_out, out_sem.at[0])
    press_copy.start()

    def balance(d, carry):
        val = [[pt[d, x, p] for p in range(2)] for x in range(8)]
        f_e = [[None, None] for _ in range(8)]
        for x in range(8):
            for p in range(2):
                east_v = val[x + 1][p] if x < 7 else lane_roll(val[0][p], -1)
                f_e[x][p] = te[d, x, p] * (val[x][p] - east_v)
        for x in range(8):
            after = sub_roll(jnp.where(row0, pt[d + 1, x, 0], val[x][0]), -1)
            f_n0 = tn[d, x, 0] * (val[x][0] - val[x][1])
            f_n1 = tn[d, x, 1] * (val[x][1] - after)
            before = sub_roll(jnp.where(row7, fp[x], f_n1), 1)
            fp[x] = f_n1
            f_n = (f_n0, f_n1)
            f_s = (before, f_n0)
            for p in range(2):
                f_w = f_e[x - 1][p] if x else lane_roll(f_e[7][p], 1)
                a = at[x, pl.ds(16 * d + p, 8, stride=2), :]
                s = st[x, pl.ds(16 * d + p, 8, stride=2), :]
                flow = a * val[x][p] + (f_e[x][p] - f_w) + (f_n[p] - f_s[p])
                ry[x, pl.ds(16 * d + p, 8, stride=2), :] = s - flow
        return carry

    lax.fori_loop(0, DUALS, balance, 0)
    to_rows(ry, ro)

    def vertical(l, carry):
        r0 = pl.multiple_of(l * 16, 16)
        here = po[pl.ds(r0, 16), :]
        f_up = vt[pl.ds(r0, 16), :] * (here - po[pl.ds(r0 + 16, 16), :])
        ro[pl.ds(r0, 16), :] = ro[pl.ds(r0, 16), :] - f_up + carry
        return f_up

    last_flux = lax.fori_loop(0, LAYERS - 1, vertical, jnp.zeros((16, 128), F32))

    @pl.when(has_below)
    def _():
        vt_up.wait_recv()
        high_send.wait_recv()
        low_send.wait_send()

    @pl.when(has_above)
    def _():
        low_send.wait_recv()
        high_send.wait_send()
        vt_up.wait_send()

    above = jnp.where(gz < DEPTH - 1, vt[pl.ds(496, 16), :] * (po[pl.ds(496, 16), :] - up_layer[...]), 0.0)
    below = jnp.where(gz > 0, down_pair[1] * (down_pair[0] - po[pl.ds(0, 16), :]), 0.0)
    ro[pl.ds(496, 16), :] = ro[pl.ds(496, 16), :] - above + last_flux
    ro[pl.ds(0, 16), :] = ro[pl.ds(0, 16), :] + below
    resid_copy = pltpu.make_async_copy(ro, resid_out, out_sem.at[1])
    resid_copy.start()
    press_copy.wait()
    resid_copy.wait()


def body(permeability, accumulation, source_term, vertical_trans):
    split = (LAYERS, 2, 8, 128)
    vmem = lambda *shape: pltpu.VMEM(shape, F32)
    anywhere = pl.BlockSpec(memory_space=pl.ANY)
    in_hbm = pl.BlockSpec(memory_space=pltpu.HBM)
    pressure, residual = pl.pallas_call(
        kernel,
        out_shape=[jax.ShapeDtypeStruct((512, 128), F32)] * 2,
        in_specs=[in_hbm] * 4,
        out_specs=[anywhere] * 2,
        scratch_shapes=[
            vmem(4, 32, 8, 128),
            vmem(4, 32, 8, 128),
            vmem(4, 32, 8, 128),
            vmem(512, 128),
            vmem(32, 128),
            vmem(32, 128),
            vmem(9, 152, 128),
            vmem(8, 144, 128),
            vmem(8, 144, 128),
            vmem(9, 8, 2, 8, 128),
            vmem(9, 8, 2, 8, 128),
            vmem(5, 8, 2, 8, 128),
            vmem(3, 9, 8, 2, 8, 128),
            vmem(14, 8, 128),
            vmem(16, 4, 8, 128),
            vmem(2, 24, 128),
            vmem(9, 4, 8, 128),
            vmem(10, 8, 2, 8, 128),
            vmem(8, 144, 128),
            vmem(8, 144, 128),
            vmem(8, 8, 128),
            vmem(512, 128),
            vmem(512, 128),
            vmem(16, 128),
            vmem(2, 16, 128),
            pltpu.SemaphoreType.DMA((7,)),
            pltpu.SemaphoreType.DMA((12,)),
            pltpu.SemaphoreType.DMA((12,)),
            pltpu.SemaphoreType.DMA((16,)),
            pltpu.SemaphoreType.DMA((16,)),
            pltpu.SemaphoreType.DMA((2,)),
        ],
        compiler_params=pltpu.CompilerParams(
            collective_id=0, has_side_effects=True, vmem_limit_bytes=40 * 1024 * 1024
        ),
    )(
        *(
            pltpu.with_memory_space_constraint(value, pltpu.HBM)
            for value in (
                permeability.reshape(split),
                accumulation.reshape(split),
                source_term.reshape(split),
                vertical_trans.reshape(512, 128),
            )
        ),
    )
    return pressure.reshape(32, 16, 128), residual.reshape(32, 16, 128)


def solution(mesh):
    spec = P("gz", "gx", "gy")
    return jax.shard_map(
        body, mesh=mesh, in_specs=(spec,) * 4, out_specs=(spec, spec), check_vma=False
    )
```

```python
import jax
import jax.numpy as jnp
from jax import lax
from jax.experimental import pallas as pl
from jax.experimental.pallas import tpu as pltpu
from jax.sharding import PartitionSpec as P

SWEEPS = 8
LAYERS = 32
SIDE = 4
DEPTH = 16
DUALS = 9
MESH = pl.DeviceIdType.MESH
F32 = jnp.float32
LX, LY = 0, 1


def lane_roll(value, groups):
    by = (groups * 32) % 128
    return value if by == 0 else pltpu.roll(value, by, axis=1)


def sub_roll(value, by):
    return pltpu.roll(value, by % 8, axis=0)


def inverse(value):
    guess = pl.reciprocal(value, approx=True)
    guess = guess * (2.0 - value * guess)
    return guess * (2.0 - value * guess)


def harmonic(left, right):
    return 2.0 * left * right * inverse(left + right)


def node_shift(value, by, row):
    if by % 8 == 0:
        return lane_roll(value, -(by // 8))
    turned = sub_roll(value, -by)
    if by > 0:
        return jnp.where(row < 8 - by, turned, lane_roll(turned, -1))
    return jnp.where(row >= -by, turned, lane_roll(turned, 1))


def factor(b):
    low = {}
    inv = [None] * 4
    for k in range(4):
        pivot = b[(k, k)]
        for m in range(k):
            if low.get((k, m)) is not None:
                pivot = pivot - low[(k, m)] * work[(k, m)]
        inv[k] = inverse(pivot)
        if k == 0:
            work = {}
        for i in range(k + 1, 4):
            entry = b[(i, k)]
            for m in range(k):
                if low.get((i, m)) is None or work.get((k, m)) is None:
                    continue
                term = low[(i, m)] * work[(k, m)]
                entry = -term if entry is None else entry - term
            work[(i, k)] = entry
            low[(i, k)] = None if entry is None else entry * inv[k]
    return low, inv


def forward(low, column):
    out = []
    for i in range(4):
        value = column[i]
        for m in range(i):
            if low[(i, m)] is not None and out[m] is not None:
                term = low[(i, m)] * out[m]
                value = -term if value is None else value - term
        out.append(value)
    return out


def scaled(inv, column):
    return [None if v is None else v * inv[k] for k, v in enumerate(column)]


def inner(left, right):
    total = None
    for a, b in zip(left, right):
        if a is None or b is None:
            continue
        total = a * b if total is None else total + a * b
    return total


def subtract(value, term):
    if term is None:
        return value
    return -term if value is None else value - term


def shift_or_none(value, by, row):
    return None if value is None else node_shift(value, by, row)


def solve_nodes(b, c, d, row):
    for step in (1, 2, 4, 8):
        a = [[shift_or_none(c[m][k], -step, row) for m in range(4)] for k in range(4)]
        low, inv = factor(b)
        up = [forward(low, [c[i][k] for i in range(4)]) for k in range(4)]
        down = [forward(low, [a[i][k] for i in range(4)]) for k in range(4)]
        side = scaled(inv, forward(low, d))
        up_s = [scaled(inv, col) for col in up]
        down_s = [scaled(inv, col) for col in down]
        new_b = {}
        for i in range(4):
            for k in range(i + 1):
                value = subtract(b[(i, k)], shift_or_none(inner(up[i], up_s[k]), -step, row))
                new_b[(i, k)] = subtract(value, shift_or_none(inner(down[i], down_s[k]), step, row))
        new_d = []
        for i in range(4):
            value = subtract(d[i], shift_or_none(inner(up[i], side), -step, row))
            new_d.append(subtract(value, shift_or_none(inner(down[i], side), step, row)))
        new_c = [
            [subtract(None, shift_or_none(inner(down[i], up_s[k]), step, row)) for k in range(4)]
            for i in range(4)
        ]
        b, c, d = new_b, new_c, new_d
    both = [[c[i][k] + node_shift(c[k][i], -16, row) for k in range(4)] for i in range(4)]
    low, inv = factor(b)
    cols = [forward(low, [both[i][k] for i in range(4)]) for k in range(4)]
    cols_s = [scaled(inv, col) for col in cols]
    side = scaled(inv, forward(low, d))
    last = {}
    for i in range(4):
        for k in range(i + 1):
            last[(i, k)] = b[(i, k)] - node_shift(inner(cols[i], cols_s[k]), 16, row)
    right = [d[i] - node_shift(inner(cols[i], side), 16, row) for i in range(4)]
    low, inv = factor(last)
    value = scaled(inv, forward(low, right))
    for i in (2, 1, 0):
        for k in range(i + 1, 4):
            value[i] = value[i] - low[(k, i)] * value[k]
    return value


def corner_sums(g, r):
    k = [
        g[(3, 3)],
        g[(2, 3)] - g[(3, 3)],
        g[(1, 3)] - g[(3, 3)],
        g[(0, 3)] - g[(1, 3)] - g[(2, 3)] + g[(3, 3)],
        g[(2, 2)] - 2.0 * g[(2, 3)] + g[(3, 3)],
        g[(1, 2)] - g[(1, 3)] - g[(2, 3)] + g[(3, 3)],
        (g[(0, 2)] - g[(1, 2)] - g[(2, 2)]) + (2.0 * g[(2, 3)] - g[(0, 3)] + g[(1, 3)] - g[(3, 3)]),
        g[(1, 1)] - 2.0 * g[(1, 3)] + g[(3, 3)],
        (g[(0, 1)] - g[(1, 1)] - g[(1, 2)]) + (2.0 * g[(1, 3)] - g[(0, 3)] + g[(2, 3)] - g[(3, 3)]),
        (g[(0, 0)] + g[(1, 1)] + g[(2, 2)] + g[(3, 3)])
        - 2.0 * (g[(0, 1)] + g[(0, 2)] + g[(1, 3)] + g[(2, 3)] - g[(0, 3)] - g[(1, 2)]),
        r[3],
        r[2] - r[3],
        r[1] - r[3],
        r[0] - r[1] - r[2] + r[3],
    ]
    return k


GRAM = ((0, 0), (0, 1), (0, 2), (0, 3), (1, 1), (1, 2), (1, 3), (2, 2), (2, 3), (3, 3))


def assemble(t, row):
    def back(value):
        return node_shift(value, -1, row)

    b, d = {}, []
    c = [[None] * 4 for _ in range(4)]
    for i in range(4):
        w = (i - 1) % 4
        b[(i, i)] = t[0][i] + t[4][w] + back(t[7][i] + t[9][w])
        d.append(t[10][i] + t[11][w] + back(t[12][i] + t[13][w]))
        edge = t[1][i] + back(t[8][i])
        e = (i + 1) % 4
        b[(max(i, e), min(i, e))] = edge
        c[i][i] = t[2][i] + t[6][w]
        c[i][e] = t[3][i]
        c[e][i] = t[5][i]
    b[(2, 0)] = None
    b[(3, 1)] = None
    return b, c, d


def kernel(
    perm, accum, source, vtrans, press_out, resid_out,
    hx, ax, sx, vt, row24, row8, lo_out, hi_out, lo_n, lo_ne0, lo_ne1, lo_nw, hi_s, hi_se0, hi_se1, hi_sw,
    tp, ta, ts, teq, tnq, bq, tew, tnw, bw, te, tn, bf, co, sums, ga, gk, nodes, cb, pt, py, ry, fp, po, ro,
    up_layer, down_pair,
    local_sem, send_sem, recv_sem, gsend_sem, grecv_sem, out_sem,
):
    gx, gy, gz = lax.axis_index("gx"), lax.axis_index("gy"), lax.axis_index("gz")

    def peer(dx, dy, dz):
        return (
            lax.rem(gx + (dx + SIDE), SIDE),
            lax.rem(gy + (dy + SIDE), SIDE),
            lax.rem(gz + (dz + DEPTH), DEPTH),
        )

    local = [
        pltpu.make_async_copy(perm.at[:, 0], hx.at[1], local_sem.at[0]),
        pltpu.make_async_copy(perm.at[:, 1], hx.at[2], local_sem.at[1]),
        pltpu.make_async_copy(accum.at[:, 0], ax.at[0], local_sem.at[2]),
        pltpu.make_async_copy(accum.at[:, 1], ax.at[1], local_sem.at[3]),
        pltpu.make_async_copy(source.at[:, 0], sx.at[0], local_sem.at[4]),
        pltpu.make_async_copy(source.at[:, 1], sx.at[1], local_sem.at[5]),
        pltpu.make_async_copy(vtrans, vt, local_sem.at[6]),
    ]
    for copy in local:
        copy.start()

    has_below, has_above = gz > 0, gz < DEPTH - 1
    barrier = pltpu.get_barrier_semaphore()
    for dx in range(SIDE):
        for dy in range(SIDE):
            if dx or dy:
                pl.semaphore_signal(barrier, inc=1, device_id=peer(dx, dy, 0), device_id_type=MESH)
    for dz, there in ((-1, has_below), (1, has_above)):

        @pl.when(there)
        def _():
            pl.semaphore_signal(barrier, inc=1, device_id=peer(0, 0, dz), device_id_type=MESH)

    row = lax.broadcasted_iota(jnp.int32, (8, 128), 0)
    lane = lax.broadcasted_iota(jnp.int32, (8, 128), 1)
    group = lane // 32
    lower = lane < 64
    u_base = jnp.where(group % 2 == 1, 8, 0)
    row0 = row == 0
    row7 = row == 7
    u0 = u_base == 0
    u8 = u_base == 8

    hx_rows = hx.reshape(4 * 256, 128)
    ax_rows = ax.reshape(3 * 256, 128)
    sx_rows = sx.reshape(3 * 256, 128)

    def edges(rows, base, at_row, depth, with_high):
        for half in range(2):
            for m in range(2):
                first = base + 256 * half + 4 * m
                turned = jnp.concatenate([rows[pl.ds(first + q, 32, stride=8), :] for q in range(4)], axis=0).T
                lo_out[half, m, pl.ds(at_row, depth), :] = turned[:depth]
                if with_high:
                    hi_out[half, m] = turned[120:]

    local[0].wait()
    local[1].wait()
    row8[...] = hx_rows[pl.ds(512, LAYERS, stride=8), :]
    edges(hx_rows, 256, 0, 16, True)
    for copy in local[2:]:
        copy.wait()
    edges(ax_rows, 0, 16, 8, False)
    edges(sx_rows, 0, 24, 8, False)

    pl.semaphore_wait(barrier, 15 + jnp.minimum(gz, 1) + jnp.minimum(DEPTH - 1 - gz, 1))

    def remote(src, dst, at_sem, target):
        return pltpu.make_async_remote_copy(
            src_ref=src, dst_ref=dst, send_sem=send_sem.at[at_sem], recv_sem=recv_sem.at[at_sem],
            device_id=target, device_id_type=MESH,
        )

    west, east = peer(-1, 0, 0), peer(1, 0, 0)
    south, north = peer(0, -1, 0), peer(0, 1, 0)
    perm_w = remote(hx.at[1], hx.at[3], 0, west)
    perm_r = remote(row8, row24, 1, west)
    low_s = remote(lo_out, lo_n, 2, south)
    low_sw0 = remote(lo_out.at[0], lo_ne0, 3, peer(-1, -1, 0))
    low_sw1 = remote(lo_out.at[1, 0, pl.ds(0, 16)], lo_ne1, 4, peer(-1, -1, 0))
    accum_w = remote(ax.at[0], ax.at[2], 5, west)
    source_w = remote(sx.at[0], sx.at[2], 6, west)
    perm_e = remote(hx.at[2], hx.at[0], 7, east)
    low_se = remote(lo_out.at[1, :, pl.ds(0, 16)], lo_nw, 8, peer(1, -1, 0))
    high_n = remote(hi_out, hi_s, 9, north)
    high_nw0 = remote(hi_out.at[0], hi_se0, 10, peer(-1, 1, 0))
    high_nw1 = remote(hi_out.at[1, 0], hi_se1, 11, peer(-1, 1, 0))
    high_ne = remote(hi_out.at[1], hi_sw, 12, peer(1, 1, 0))
    vt_up = remote(vt.at[pl.ds(496, 16)], down_pair.at[1], 13, peer(0, 0, 1))
    first_sends = [perm_w, perm_r, low_s, low_sw0, low_sw1, accum_w, source_w]
    later_sends = [perm_e, low_se, high_n, high_nw0, high_nw1, high_ne]
    for copy in first_sends + later_sends:
        copy.start()

    @pl.when(has_above)
    def _():
        vt_up.start()

    def pick(at_group, left, by_left, right, by_right):
        return jnp.where(group == at_group, lane_roll(left, by_left), lane_roll(right, by_right))

    perm_w.wait_recv()
    perm_r.wait_recv()
    for x in range(9):
        if x < 8:
            part = hx_rows[pl.ds(512 + x, 64, stride=8), :]
        else:
            part = jnp.concatenate([hx_rows[pl.ds(768, 32, stride=8), :], row24[...]], axis=0)
        tp[1, x, pl.ds(8, 128), :] = jnp.concatenate([part, part], axis=0).T

    def north_owned():
        low_s.wait_recv()
        low_sw0.wait_recv()
        low_sw1.wait_recv()
        for t in range(2):
            at = pl.ds(8 * t, 8)
            for x in range(8):
                m, q = x // 4, x % 4
                tp[1, x, pl.ds(136 + 8 * t, 8), :] = pick(2, lo_n[1, m, at, :], 2 - q, lo_ne0[m, at, :], 3 - q)
            tp[1, 8, pl.ds(136 + 8 * t, 8), :] = pick(2, lo_ne0[0, at, :], 2, lo_ne1[at, :], 3)

    def relax(sel_lo, sel_hi, at_lo, at_hi, put_t, put_b):
        def cell(x, off):
            return jnp.where(
                lower,
                tp[sel_lo, x, pl.ds(at_lo + off, 8, stride=2), :],
                tp[sel_hi, x, pl.ds(at_hi + off, 8, stride=2), :],
            )

        cells = [[cell(x, p) for p in range(2)] for x in range(9)]
        t_e = [[harmonic(cells[x][p], cells[x + 1][p]) for p in range(2)] for x in range(8)]
        for x in range(8):
            t_n = [harmonic(cells[x][0], cells[x][1]), harmonic(cells[x][1], cell(x, 2))]
            t_s = [sub_roll(t_n[1], 1), t_n[0]]
            for p in range(2):
                t_w = t_e[x - 1][p] if x else lane_roll(t_e[7][p], 1)
                put_t(x, p, t_e[x][p], t_n[p])
                inv = inverse((t_w + t_e[x][p]) + (t_s[p] + t_n[p]))
                if p == 0 and x == 0:
                    inv = jnp.where(row0 | u0, 0.0, inv)
                elif p == 0:
                    inv = jnp.where(row0, 0.0, inv)
                elif x == 0:
                    inv = jnp.where(u0, 0.0, inv)
                co[0, x, p] = t_w * inv
                co[1, x, p] = t_e[x][p] * inv
                co[2, x, p] = t_s[p] * inv
                co[3, x, p] = t_n[p] * inv

        def sweep(vals):
            new = []
            for x in range(8):
                pair = []
                for p in range(2):
                    west_v = vals[x - 1][p] if x else lane_roll(vals[7][p], 1)
                    east_v = vals[x + 1][p] if x < 7 else lane_roll(vals[0][p], -1)
                    south_v = vals[x][0] if p else sub_roll(vals[x][1], 1)
                    north_v = sub_roll(vals[x][0], -1) if p else vals[x][1]
                    pair.append(
                        (co[0, x, p] * west_v + co[1, x, p] * east_v) + (co[2, x, p] * south_v + co[3, x, p] * north_v)
                    )
                new.append(pair)
            return new

        def plus(left, right):
            return [[left[x][p] + right[x][p] for p in range(2)] for x in range(8)]

        def along(x, p):
            return 1.0 - (u_base + x).astype(F32) / 16.0, 1.0 - (2 * row + p).astype(F32) / 16.0

        for kind in range(3):
            push = []
            for x in range(8):
                pair = []
                for p in range(2):
                    w_x, w_y = along(x, p)
                    if kind == LX:
                        value = co[0, x, p] - co[1, x, p]
                    elif kind == LY:
                        value = co[2, x, p] - co[3, x, p]
                    else:
                        value = (co[0, x, p] - co[1, x, p]) * w_y + (co[2, x, p] - co[3, x, p]) * w_x
                    pair.append(value)
                push.append(pair)
            vals = plus(push, sweep(push))
            vals = plus(vals, sweep(sweep(vals)))
            vals = plus(vals, sweep(sweep(sweep(sweep(vals)))))
            for x in range(8):
                for p in range(2):
                    w_x, w_y = along(x, p)
                    put_b(kind, x, p, (w_x, w_y, w_x * w_y)[kind] + vals[x][p] * (1.0 / 16.0))

    def owned(k, carry):
        @pl.when(k == 3)
        def _():
            north_owned()

        at_lo = 16 + 16 * lax.rem(k, 2) + 64 * (k // 2)

        def put_t(x, p, east_t, north_t):
            teq[k, x, p] = east_t
            tnq[k, x, p] = north_t

        def put_b(kind, x, p, value):
            bq[kind, k, x, p] = value

        relax(1, 1, at_lo, at_lo + 32, put_t, put_b)
        return carry

    lax.fori_loop(0, 4, owned, 0)

    accum_w.wait_recv()
    source_w.wait_recv()
    for rows, turned, at_row in ((ax_rows, ta, 16), (sx_rows, ts, 24)):
        for x in range(8):
            m, q = x // 4, x % 4
            part = rows[pl.ds(256 + x, 64, stride=8), :]
            turned[x, pl.ds(0, 128), :] = jnp.concatenate([part, part], axis=0).T
            at = pl.ds(at_row, 8)
            turned[x, pl.ds(128, 8), :] = pick(2, lo_n[1, m, at, :], 2 - q, lo_ne0[m, at, :], 3 - q)

    def gram(k, carry):
        at_lo = 8 + 16 * lax.rem(k, 2) + 64 * (k // 2)

        def load(ref, x, p):
            return jnp.where(
                lower,
                ref[x, pl.ds(at_lo + p, 8, stride=2), :],
                ref[x, pl.ds(at_lo + 32 + p, 8, stride=2), :],
            )

        acc = {}

        def add(key, value):
            acc[key] = value if key not in acc else acc[key] + value

        for x in range(8):
            for p in range(2):
                a = load(ta, x, p)
                s = load(ts, x, p)
                here = [bq[kind, k, x, p] for kind in range(3)]
                t_e, t_n = teq[k, x, p], tnq[k, x, p]
                mass, d_e, d_n = [], [], []
                for kind in range(3):
                    if x < 7:
                        east_v = bq[kind, k, x + 1, p]
                    else:
                        east_v = lane_roll(bq[kind, k, 0, p], -1)
                        if kind != LY:
                            east_v = jnp.where(u8, 0.0, east_v)
                    if p:
                        north_v = sub_roll(bq[kind, k, x, 0], -1)
                        if kind != LX:
                            north_v = jnp.where(row7, 0.0, north_v)
                    else:
                        north_v = bq[kind, k, x, 1]
                    d_e.append(here[kind] - east_v)
                    d_n.append(here[kind] - north_v)
                    mass.append(a * here[kind])
                add((0, 0), a)
                add("r0", s)
                for kind in range(3):
                    add((0, kind + 1), mass[kind])
                    add("r" + str(kind + 1), s * here[kind])
                    w_e, w_n = t_e * d_e[kind], t_n * d_n[kind]
                    for other in range(kind, 3):
                        add((kind + 1, other + 1), mass[kind] * here[other] + w_e * d_e[other] + w_n * d_n[other])
        for index, key in enumerate(GRAM + ("r0", "r1", "r2", "r3")):
            value = acc[key]
            value = value + sub_roll(value, 4)
            value = value + sub_roll(value, 2)
            value = value + sub_roll(value, 1)
            sums[k, index] = value + lane_roll(value, -1)
        return carry

    def send_sums(piece):
        whole = []
        for index in range(14):
            value = jnp.where(row % 2 == 1, sums[2 * piece + 1, index], sums[2 * piece, index])
            whole.append(jnp.where(row % 4 < 2, value, lane_roll(value, -2)))
        entries = corner_sums({key: whole[i] for i, key in enumerate(GRAM)}, whole[10:])
        for m in range(2):
            packed = jnp.zeros((8, 128), F32)
            for t in range(8 * m, min(8 * m + 8, 14)):
                here = (group == t % 4) & (row // 4 == t // 4 % 2)
                packed = jnp.where(here, lane_roll(entries[t], t % 4), packed)
            ga[piece, 0, m] = packed
        copies = []
        for dx in range(SIDE):
            for dy in range(SIDE):
                if dx or dy:
                    slot = (-dx % SIDE) * SIDE + (-dy % SIDE)
                    copies.append(
                        pltpu.make_async_remote_copy(
                            src_ref=ga.at[piece, 0], dst_ref=ga.at[piece, slot],
                            send_sem=gsend_sem.at[piece, slot], recv_sem=grecv_sem.at[piece, slot],
                            device_id=peer(dx, dy, 0), device_id_type=MESH,
                        )
                    )
        for copy in copies:
            copy.start()
        return copies

    lax.fori_loop(0, 2, gram, 0)
    gathers = send_sums(0)
    lax.fori_loop(2, 4, gram, 0)
    gathers = gathers + send_sums(1)

    for copy in later_sends:
        copy.wait_recv()
    for x in range(9):
        part = hx_rows[pl.ds(x if x < 8 else 256, 64, stride=8), :]
        tp[0, x, pl.ds(8, 128), :] = jnp.concatenate([part, part], axis=0).T
    for x in range(8):
        m, q = x // 4, x % 4
        for t in range(2):
            at = pl.ds(8 * t, 8)
            tp[0, x, pl.ds(136 + 8 * t, 8), :] = pick(2, lo_nw[m, at, :], 2 - q, lo_n[0, m, at, :], 3 - q)
        tp[0, x, pl.ds(0, 8), :] = pick(0, hi_sw[m], -q, hi_s[0, m], 1 - q)
        tp[1, x, pl.ds(0, 8), :] = pick(2, hi_s[1, m], 2 - q, hi_se0[m], 3 - q)
    for t in range(2):
        at = pl.ds(8 * t, 8)
        tp[0, 8, pl.ds(136 + 8 * t, 8), :] = pick(2, lo_n[0, 0, at, :], 2, lo_n[1, 0, at, :], 3)
    tp[0, 8, pl.ds(0, 8), :] = pick(0, hi_s[0, 0], 0, hi_s[1, 0], 1)
    tp[1, 8, pl.ds(0, 8), :] = pick(2, hi_se0[0], 2, hi_se1[...], 3)

    def others(k, carry):
        edge = k // 4
        at_lo = (16 + 16 * lax.rem(k, 2) + 64 * (k // 2)) * (1 - edge)

        def put_t(x, p, east_t, north_t):
            tew[x, p] = east_t
            tnw[x, p] = north_t

        def put_b(kind, x, p, value):
            bw[kind, x, p] = value

        relax(0, edge, at_lo, at_lo + 32 * (1 - edge), put_t, put_b)

        @pl.when(k < 4)
        def _():
            d_lo = 1 + lax.rem(k, 2) + 4 * (k // 2)

            def merge(own, other, put):
                crossed = pltpu.roll(jnp.where(lower, own, other), 64, axis=1)
                put(d_lo, jnp.where(lower, other, crossed))
                put(d_lo + 2, jnp.where(lower, crossed, own))

            for x in range(8):
                for p in range(2):

                    def put_te(d, value):
                        te[d, x, p] = value

                    def put_tn(d, value):
                        tn[d, x, p] = value

                    merge(teq[k, x, p], tew[x, p], put_te)
                    merge(tnq[k, x, p], tnw[x, p], put_tn)
                    for kind in range(3):

                        def put_bf(d, value):
                            bf[kind, d, x, p] = value

                        merge(bq[kind, k, x, p], bw[kind, x, p], put_bf)

        @pl.when(k == 4)
        def _():
            te[0] = tew[...]
            tn[0] = tnw[...]
            for kind in range(3):
                bf[kind, 0] = bw[kind]

        return carry

    lax.fori_loop(0, 5, others, 0)

    for copy in gathers:
        copy.wait()
    for slot in range(SIDE * SIDE):
        for m in range(2):
            first, second = ga[0, slot, m], ga[1, slot, m]
            crossed = sub_roll(jnp.where(row < 4, second, first), 4)
            gk[slot, 2 * m] = jnp.where(row < 4, first, crossed)
            gk[slot, 2 * m + 1] = jnp.where(row < 4, crossed, second)

    table = []
    for index in range(14):
        k, q = index // 4, index % 4
        by_x = []
        for i in range(SIDE):
            value = lane_roll(gk[i * SIDE, k], -q)
            for g in range(1, SIDE):
                value = jnp.where(group == g, lane_roll(gk[i * SIDE + g, k], g - q), value)
            by_x.append(value)
        table.append(by_x)
    b, c, d_side = assemble(table, row)
    coarse = solve_nodes(b, c, d_side, row)

    def everywhere(value, g):
        value = jnp.where(group == g, value, 0.0)
        value = value + lane_roll(value, 1)
        return value + lane_roll(value, 2)

    for at_row, g in ((0, 3), (8, 0), (16, 1)):
        mid = everywhere(coarse[0], g)
        nodes[0, pl.ds(at_row, 8), :] = jnp.where(lower, everywhere(coarse[3], g), mid)
        nodes[1, pl.ds(at_row, 8), :] = jnp.where(lower, mid, everywhere(coarse[1], g))
    for d in range(DUALS):
        c0 = jnp.broadcast_to(nodes[0, pl.ds(7 + d, 1), :], (8, 128))
        c1 = jnp.broadcast_to(nodes[1, pl.ds(7 + d, 1), :], (8, 128))
        c2 = jnp.broadcast_to(nodes[0, pl.ds(8 + d, 1), :], (8, 128))
        c3 = jnp.broadcast_to(nodes[1, pl.ds(8 + d, 1), :], (8, 128))
        cb[d, 0] = c3
        cb[d, 1] = c2 - c3
        cb[d, 2] = c1 - c3
        cb[d, 3] = (c0 - c1) - (c2 - c3)

    def interpolate(d, carry):
        w = [cb[d, k] for k in range(4)]
        for x in range(8):
            for p in range(2):
                value = (w[0] + w[1] * bf[0, d, x, p]) + (w[2] * bf[1, d, x, p] + w[3] * bf[2, d, x, p])
                pt[d, x, p] = value
                py[x, pl.ds(16 * d + p, 8, stride=2), :] = value
        return carry

    lax.fori_loop(0, DUALS, interpolate, 0)

    lane_full = lax.broadcasted_iota(jnp.int32, (128, 128), 1)
    middle = (lane_full >= 32) & (lane_full < 96)

    def to_rows(src, dst):
        for x in range(0, 8, 2):
            both = jnp.where(
                middle, src[x, pl.ds(8, 128), :], pltpu.roll(src[x + 1, pl.ds(8, 128), :], 64, axis=1)
            ).T
            dst[pl.ds(x, 32, stride=16), :] = both[32:64]
            dst[pl.ds(8 + x, 32, stride=16), :] = both[64:96]
            dst[pl.ds(x + 1, 32, stride=16), :] = both[96:128]
            dst[pl.ds(9 + x, 32, stride=16), :] = both[0:32]

    to_rows(py, po)
    low_send = remote(po.at[pl.ds(0, 16)], up_layer, 14, peer(0, 0, -1))
    high_send = remote(po.at[pl.ds(496, 16)], down_pair.at[0], 15, peer(0, 0, 1))

    @pl.when(has_below)
    def _():
        low_send.start()

    @pl.when(has_above)
    def _():
        high_send.start()

    press_copy = pltpu.make_async_copy(po, press_out, out_sem.at[0])
    press_copy.start()

    def balance(d, carry):
        val = [[pt[d, x, p] for p in range(2)] for x in range(8)]
        f_e = [[None, None] for _ in range(8)]
        for x in range(8):
            for p in range(2):
                east_v = val[x + 1][p] if x < 7 else lane_roll(val[0][p], -1)
                f_e[x][p] = te[d, x, p] * (val[x][p] - east_v)
        for x in range(8):
            after = sub_roll(jnp.where(row0, pt[d + 1, x, 0], val[x][0]), -1)
            f_n0 = tn[d, x, 0] * (val[x][0] - val[x][1])
            f_n1 = tn[d, x, 1] * (val[x][1] - after)
            before = sub_roll(jnp.where(row7, fp[x], f_n1), 1)
            fp[x] = f_n1
            f_n = (f_n0, f_n1)
            f_s = (before, f_n0)
            for p in range(2):
                f_w = f_e[x - 1][p] if x else lane_roll(f_e[7][p], 1)
                ry[x, pl.ds(16 * d + p, 8, stride=2), :] = (f_e[x][p] - f_w) + (f_n[p] - f_s[p])
        return carry

    lax.fori_loop(0, DUALS, balance, 0)
    to_rows(ry, ro)

    for half in range(2):
        before = None
        for l in range(LAYERS):
            at = pl.ds(16 * l + 8 * half, 8)
            here = po[at, :]
            value = sx[half, l] - ax[half, l] * here - ro[at, :]
            if before is not None:
                value = value + before
            if l < LAYERS - 1:
                before = vt[at, :] * (here - po[pl.ds(16 * (l + 1) + 8 * half, 8), :])
                value = value - before
            ro[at, :] = value

    @pl.when(has_below)
    def _():
        vt_up.wait_recv()
        high_send.wait_recv()
        low_send.wait_send()

    @pl.when(has_above)
    def _():
        low_send.wait_recv()
        high_send.wait_send()
        vt_up.wait_send()

    above = jnp.where(has_above, vt[pl.ds(496, 16), :] * (po[pl.ds(496, 16), :] - up_layer[...]), 0.0)
    below = jnp.where(has_below, down_pair[1] * (down_pair[0] - po[pl.ds(0, 16), :]), 0.0)
    ro[pl.ds(496, 16), :] = ro[pl.ds(496, 16), :] - above
    ro[pl.ds(0, 16), :] = ro[pl.ds(0, 16), :] + below
    resid_copy = pltpu.make_async_copy(ro, resid_out, out_sem.at[1])
    resid_copy.start()
    for copy in first_sends + later_sends:
        copy.wait_send()
    press_copy.wait()
    resid_copy.wait()


def body(permeability, accumulation, source_term, vertical_trans):
    split = (LAYERS, 2, 8, 128)
    vmem = lambda *shape: pltpu.VMEM(shape, F32)
    anywhere = pl.BlockSpec(memory_space=pl.ANY)
    in_hbm = pl.BlockSpec(memory_space=pltpu.HBM)
    pressure, residual = pl.pallas_call(
        kernel,
        out_shape=[jax.ShapeDtypeStruct((512, 128), F32)] * 2,
        in_specs=[in_hbm] * 4,
        out_specs=[anywhere] * 2,
        scratch_shapes=[
            vmem(4, 32, 8, 128),
            vmem(3, 32, 8, 128),
            vmem(3, 32, 8, 128),
            vmem(512, 128),
            vmem(32, 128),
            vmem(32, 128),
            vmem(2, 2, 32, 128),
            vmem(2, 2, 8, 128),
            vmem(2, 2, 32, 128),
            vmem(2, 32, 128),
            vmem(16, 128),
            vmem(2, 16, 128),
            vmem(2, 2, 8, 128),
            vmem(2, 8, 128),
            vmem(8, 128),
            vmem(2, 8, 128),
            vmem(2, 9, 152, 128),
            vmem(8, 136, 128),
            vmem(8, 136, 128),
            vmem(4, 8, 2, 8, 128),
            vmem(4, 8, 2, 8, 128),
            vmem(3, 4, 8, 2, 8, 128),
            vmem(8, 2, 8, 128),
            vmem(8, 2, 8, 128),
            vmem(3, 8, 2, 8, 128),
            vmem(9, 8, 2, 8, 128),
            vmem(9, 8, 2, 8, 128),
            vmem(3, 9, 8, 2, 8, 128),
            vmem(4, 8, 2, 8, 128),
            vmem(4, 14, 8, 128),
            vmem(2, 16, 2, 8, 128),
            vmem(16, 4, 8, 128),
            vmem(2, 24, 128),
            vmem(9, 4, 8, 128),
            vmem(10, 8, 2, 8, 128),
            vmem(8, 144, 128),
            vmem(8, 144, 128),
            vmem(8, 8, 128),
            vmem(512, 128),
            vmem(512, 128),
            vmem(16, 128),
            vmem(2, 16, 128),
            pltpu.SemaphoreType.DMA((7,)),
            pltpu.SemaphoreType.DMA((16,)),
            pltpu.SemaphoreType.DMA((16,)),
            pltpu.SemaphoreType.DMA((2, 16)),
            pltpu.SemaphoreType.DMA((2, 16)),
            pltpu.SemaphoreType.DMA((2,)),
        ],
        compiler_params=pltpu.CompilerParams(
            collective_id=0, has_side_effects=True, vmem_limit_bytes=40 * 1024 * 1024
        ),
    )(
        *(
            pltpu.with_memory_space_constraint(value, pltpu.HBM)
            for value in (
                permeability.reshape(split),
                accumulation.reshape(split),
                source_term.reshape(split),
                vertical_trans.reshape(512, 128),
            )
        ),
    )
    return pressure.reshape(32, 16, 128), residual.reshape(32, 16, 128)


def solution(mesh):
    spec = P("gz", "gx", "gy")
    return jax.shard_map(
        body, mesh=mesh, in_specs=(spec,) * 4, out_specs=(spec, spec), check_vma=False
    )
```

```python
import jax
import jax.numpy as jnp
from jax import lax
from jax.experimental import pallas as pl
from jax.experimental.pallas import tpu as pltpu
from jax.sharding import PartitionSpec as P

LAYERS = 32
SETS = 2
SIDE = 4
DEPTH = 16
MIDDLE = DEPTH // 2
DUALS = 9
MESH = pl.DeviceIdType.MESH
F32 = jnp.float32
LX, LY = 0, 1


def lane_roll(value, groups):
    by = (groups * 16) % 128
    return value if by == 0 else pltpu.roll(value, by, axis=1)


def sub_roll(value, by):
    return pltpu.roll(value, by % 8, axis=0)


def inverse(value, rounds=1):
    guess = pl.reciprocal(value, approx=True)
    for _ in range(rounds):
        guess = guess * (2.0 - value * guess)
    return guess


def harmonic(left, right):
    return 2.0 * left * right * inverse(left + right)


def node_shift(value, by, slot):
    if by % 4 == 0:
        return sub_roll(value, -(by // 4))
    turned = lane_roll(value, -2 * by)
    if by > 0:
        return jnp.where(slot < 4 - by, turned, sub_roll(turned, -1))
    return jnp.where(slot >= -by, turned, sub_roll(turned, 1))


def factor(b):
    low = {}
    inv = [None] * 4
    for k in range(4):
        pivot = b[(k, k)]
        for m in range(k):
            if low.get((k, m)) is not None:
                pivot = pivot - low[(k, m)] * work[(k, m)]
        inv[k] = inverse(pivot, 2)
        if k == 0:
            work = {}
        for i in range(k + 1, 4):
            entry = b[(i, k)]
            for m in range(k):
                if low.get((i, m)) is None or work.get((k, m)) is None:
                    continue
                term = low[(i, m)] * work[(k, m)]
                entry = -term if entry is None else entry - term
            work[(i, k)] = entry
            low[(i, k)] = None if entry is None else entry * inv[k]
    return low, inv


def forward(low, column):
    out = []
    for i in range(4):
        value = column[i]
        for m in range(i):
            if low[(i, m)] is not None and out[m] is not None:
                term = low[(i, m)] * out[m]
                value = -term if value is None else value - term
        out.append(value)
    return out


def scaled(inv, column):
    return [None if v is None else v * inv[k] for k, v in enumerate(column)]


def inner(left, right):
    total = None
    for a, b in zip(left, right):
        if a is None or b is None:
            continue
        total = a * b if total is None else total + a * b
    return total


def subtract(value, term):
    if term is None:
        return value
    return -term if value is None else value - term


def shift_or_none(value, by, slot):
    return None if value is None else node_shift(value, by, slot)


def solve_nodes(b, c, d, slot):
    for step in (1, 2, 4, 8):
        a = [[shift_or_none(c[m][k], -step, slot) for m in range(4)] for k in range(4)]
        low, inv = factor(b)
        up = [forward(low, [c[i][k] for i in range(4)]) for k in range(4)]
        down = [forward(low, [a[i][k] for i in range(4)]) for k in range(4)]
        side = scaled(inv, forward(low, d))
        up_s = [scaled(inv, col) for col in up]
        down_s = [scaled(inv, col) for col in down]
        new_b = {}
        for i in range(4):
            for k in range(i + 1):
                value = subtract(b[(i, k)], shift_or_none(inner(up[i], up_s[k]), -step, slot))
                new_b[(i, k)] = subtract(value, shift_or_none(inner(down[i], down_s[k]), step, slot))
        new_d = []
        for i in range(4):
            value = subtract(d[i], shift_or_none(inner(up[i], side), -step, slot))
            new_d.append(subtract(value, shift_or_none(inner(down[i], side), step, slot)))
        new_c = [
            [subtract(None, shift_or_none(inner(down[i], up_s[k]), step, slot)) for k in range(4)]
            for i in range(4)
        ]
        b, c, d = new_b, new_c, new_d
    both = [[c[i][k] + node_shift(c[k][i], -16, slot) for k in range(4)] for i in range(4)]
    low, inv = factor(b)
    cols = [forward(low, [both[i][k] for i in range(4)]) for k in range(4)]
    cols_s = [scaled(inv, col) for col in cols]
    side = scaled(inv, forward(low, d))
    last = {}
    for i in range(4):
        for k in range(i + 1):
            last[(i, k)] = b[(i, k)] - node_shift(inner(cols[i], cols_s[k]), 16, slot)
    right = [d[i] - node_shift(inner(cols[i], side), 16, slot) for i in range(4)]
    low, inv = factor(last)
    value = scaled(inv, forward(low, right))
    for i in (2, 1, 0):
        for k in range(i + 1, 4):
            value[i] = value[i] - low[(k, i)] * value[k]
    return value


def corner_sums(g, r):
    k = [
        g[(3, 3)],
        g[(2, 3)] - g[(3, 3)],
        g[(1, 3)] - g[(3, 3)],
        g[(0, 3)] - g[(1, 3)] - g[(2, 3)] + g[(3, 3)],
        g[(2, 2)] - 2.0 * g[(2, 3)] + g[(3, 3)],
        g[(1, 2)] - g[(1, 3)] - g[(2, 3)] + g[(3, 3)],
        (g[(0, 2)] - g[(1, 2)] - g[(2, 2)]) + (2.0 * g[(2, 3)] - g[(0, 3)] + g[(1, 3)] - g[(3, 3)]),
        g[(1, 1)] - 2.0 * g[(1, 3)] + g[(3, 3)],
        (g[(0, 1)] - g[(1, 1)] - g[(1, 2)]) + (2.0 * g[(1, 3)] - g[(0, 3)] + g[(2, 3)] - g[(3, 3)]),
        (g[(0, 0)] + g[(1, 1)] + g[(2, 2)] + g[(3, 3)])
        - 2.0 * (g[(0, 1)] + g[(0, 2)] + g[(1, 3)] + g[(2, 3)] - g[(0, 3)] - g[(1, 2)]),
        r[3],
        r[2] - r[3],
        r[1] - r[3],
        r[0] - r[1] - r[2] + r[3],
    ]
    return k


GRAM = ((0, 0), (0, 1), (0, 2), (0, 3), (1, 1), (1, 2), (1, 3), (2, 2), (2, 3), (3, 3))


def assemble(t, slot):
    def back(value):
        return node_shift(value, -1, slot)

    b, d = {}, []
    c = [[None] * 4 for _ in range(4)]
    for i in range(4):
        w = (i - 1) % 4
        b[(i, i)] = t[0][i] + t[4][w] + back(t[7][i] + t[9][w])
        d.append(t[10][i] + t[11][w] + back(t[12][i] + t[13][w]))
        edge = t[1][i] + back(t[8][i])
        e = (i + 1) % 4
        b[(max(i, e), min(i, e))] = edge
        c[i][i] = t[2][i] + t[6][w]
        c[i][e] = t[3][i]
        c[e][i] = t[5][i]
    b[(2, 0)] = None
    b[(3, 1)] = None
    return b, c, d


def kernel(
    perm, accum, source, vtrans, press_out, resid_out,
    hx, ax, sx, vt, row24, row8, lo_out, hi_out, lo_n, lo_ne0, lo_ne1, lo_nw, hi_s, hi_se, hi_sw,
    tp, first_rows, ta, ts, teq, tnq, bq, tew, tnw, bw, tem, tnm, co, wt, sums, ga, nodes, cb, pu, pm, hm, yp, yh, po, ro,
    up_layer, down_pair, ready,
    local_sem, send_sem, recv_sem, gsend_sem, grecv_sem, vsend_sem, vrecv_sem, out_sem,
):
    gx, gy, gz = lax.axis_index("gx"), lax.axis_index("gy"), lax.axis_index("gz")

    def peer(dx, dy, dz):
        return (
            lax.rem(gx + (dx + SIDE), SIDE),
            lax.rem(gy + (dy + SIDE), SIDE),
            lax.rem(gz + (dz + DEPTH), DEPTH),
        )

    local = []

    def load(src, dst):
        copy = pltpu.make_async_copy(src, dst, local_sem.at[len(local)])
        copy.start()
        local.append(copy)

    for src, dst, first in ((perm, hx, 1), (accum, ax, 0), (source, sx, 0)):
        for half in range(2):
            load(src.at[pl.ds(24, 8), half], dst.at[first + half, pl.ds(0, 8)])
            load(src.at[pl.ds(0, 24), half], dst.at[first + half, pl.ds(8, 24)])
    load(vtrans, vt)

    has_below, has_above = gz > 0, gz < DEPTH - 1
    first_to_above = has_above & (gz != MIDDLE - 1)
    first_to_below = gz == MIDDLE
    next_to_above = gz == MIDDLE - 1
    next_to_below = has_below & (gz != MIDDLE)
    barrier = pltpu.get_barrier_semaphore()
    for dx in range(SIDE):
        for dy in range(SIDE):
            if dx or dy:
                pl.semaphore_signal(barrier, inc=1, device_id=peer(dx, dy, 0), device_id_type=MESH)
    for dz, there in ((-1, first_to_below), (1, first_to_above)):

        @pl.when(there)
        def _():
            pl.semaphore_signal(barrier, inc=1, device_id=peer(0, 0, dz), device_id_type=MESH)

    row = lax.broadcasted_iota(jnp.int32, (8, 128), 0)
    lane = lax.broadcasted_iota(jnp.int32, (8, 128), 1)
    group = lane // 16
    slot_of = lane // 32
    lower = lane < 64
    u_base = jnp.where(group % 2 == 1, 8, 0)
    row0 = row == 0
    row7 = row == 7
    u0 = u_base == 0
    u8 = u_base == 8

    for x in range(8):
        for p in range(2):
            w_x = 1.0 - (u_base + x).astype(F32) / 16.0
            w_y = 1.0 - (2 * row + p).astype(F32) / 16.0
            wt[0, x, p] = w_x
            wt[1, x, p] = w_y
            wt[2, x, p] = w_x * w_y

    hx_rows = hx.reshape(4 * 256, 128)
    ax_rows = ax.reshape(3 * 256, 128)
    sx_rows = sx.reshape(3 * 256, 128)

    def edges(rows, base, at_row, depth, with_high):
        for s in range(SETS):
            for half in range(2):
                first = base + 256 * half + 128 * s
                turned = jnp.concatenate([rows[pl.ds(first + x, 16, stride=8), :] for x in range(8)], axis=0).T
                lo_out[s, half, pl.ds(at_row, depth), :] = turned[:depth]
                if with_high:
                    hi_out[s, half] = turned[120:]

    for copy in local[:4]:
        copy.wait()
    row8[...] = hx_rows[pl.ds(512, LAYERS, stride=8), :]
    edges(hx_rows, 256, 0, 16, True)
    for copy in local[4:]:
        copy.wait()
    edges(ax_rows, 0, 16, 8, False)
    edges(sx_rows, 0, 24, 8, False)

    pl.semaphore_wait(barrier, 15 + next_to_above.astype(jnp.int32) + next_to_below.astype(jnp.int32))

    west, east = peer(-1, 0, 0), peer(1, 0, 0)
    south, north = peer(0, -1, 0), peer(0, 1, 0)

    def halo(s, first=0, end=12):
        mine = pl.ds(16 * s, 16)
        routes = (
            (hx.at[1, mine], hx.at[3, mine], west),
            (row8.at[mine], row24.at[mine], west),
            (lo_out.at[s], lo_n.at[s], south),
            (lo_out.at[s, 0], lo_ne0.at[s], peer(-1, -1, 0)),
            (lo_out.at[s, 1, pl.ds(0, 16)], lo_ne1.at[s], peer(-1, -1, 0)),
            (ax.at[0, mine], ax.at[2, mine], west),
            (sx.at[0, mine], sx.at[2, mine], west),
            (hx.at[2, mine], hx.at[0, mine], east),
            (lo_out.at[s, 1, pl.ds(0, 16)], lo_nw.at[s], peer(1, -1, 0)),
            (hi_out.at[s], hi_s.at[s], north),
            (hi_out.at[s], hi_se.at[s], peer(-1, 1, 0)),
            (hi_out.at[s, 1], hi_sw.at[s], peer(1, 1, 0)),
        )
        return [
            pltpu.make_async_remote_copy(
                src_ref=src, dst_ref=dst, send_sem=send_sem.at[s, i], recv_sem=recv_sem.at[s, i],
                device_id=target, device_id_type=MESH,
            )
            for i, (src, dst, target) in enumerate(routes)
            if first <= i < end
        ]

    def sums_messages(s):
        copies = []
        for dx in range(SIDE):
            for dy in range(SIDE):
                if dx or dy:
                    slot = (-dx % SIDE) * SIDE + (-dy % SIDE)
                    copies.append(
                        pltpu.make_async_remote_copy(
                            src_ref=ga.at[s, 0], dst_ref=ga.at[s, slot],
                            send_sem=gsend_sem.at[s, slot], recv_sem=grecv_sem.at[s, slot],
                            device_id=peer(dx, dy, 0), device_id_type=MESH,
                        )
                    )
        return copies

    for copy in halo(0, 0, 7):
        copy.start()
    for dz, at, there in ((-1, 0, next_to_below), (1, 1, next_to_above)):

        @pl.when(there)
        def _():
            pl.semaphore_signal(ready.at[at], inc=1, device_id=peer(0, 0, dz), device_id_type=MESH)

    def pick(at_group, left, by_left, right, by_right):
        return jnp.where(group == at_group, lane_roll(left, by_left), lane_roll(right, by_right))

    def turn(rows, first, second, fixed=None):
        part = [rows[pl.ds(first, 16, stride=8), :]]
        part.append(fixed if fixed is not None else rows[pl.ds(second, 16, stride=8), :])
        return jnp.concatenate(part * 4, axis=0).T

    def by_slot(load_slot):
        value = load_slot(3)
        for slot in (2, 1, 0):
            value = jnp.where(slot_of == slot, load_slot(slot), value)
        return value

    def relax(most, last, at, step, put_t, put_b):
        def cell(x, off):
            return by_slot(
                lambda slot: tp[last if slot == 3 else most, x, pl.ds(at + step * slot + off, 8, stride=2), :]
            )

        cells = [[cell(x, p) for p in range(2)] for x in range(9)]
        t_e = [[harmonic(cells[x][p], cells[x + 1][p]) for p in range(2)] for x in range(8)]
        for x in range(8):
            t_n = [harmonic(cells[x][0], cells[x][1]), harmonic(cells[x][1], cell(x, 2))]
            t_s = [sub_roll(t_n[1], 1), t_n[0]]
            for p in range(2):
                t_w = t_e[x - 1][p] if x else lane_roll(t_e[7][p], 1)
                put_t(x, p, t_e[x][p], t_n[p])
                inv = inverse((t_w + t_e[x][p]) + (t_s[p] + t_n[p]))
                if p == 0 and x == 0:
                    inv = jnp.where(row0 | u0, 0.0, inv)
                elif p == 0:
                    inv = jnp.where(row0, 0.0, inv)
                elif x == 0:
                    inv = jnp.where(u0, 0.0, inv)
                co[0, x, p] = t_w * inv
                co[1, x, p] = t_e[x][p] * inv
                co[2, x, p] = t_s[p] * inv
                co[3, x, p] = t_n[p] * inv

        def sweep(vals):
            new = []
            for x in range(8):
                pair = []
                for p in range(2):
                    west_v = vals[x - 1][p] if x else lane_roll(vals[7][p], 1)
                    east_v = vals[x + 1][p] if x < 7 else lane_roll(vals[0][p], -1)
                    south_v = vals[x][0] if p else sub_roll(vals[x][1], 1)
                    north_v = sub_roll(vals[x][0], -1) if p else vals[x][1]
                    pair.append(
                        (co[0, x, p] * west_v + co[1, x, p] * east_v) + (co[2, x, p] * south_v + co[3, x, p] * north_v)
                    )
                new.append(pair)
            return new

        def plus(left, right):
            return [[left[x][p] + right[x][p] for p in range(2)] for x in range(8)]

        for kind in range(3):
            push = []
            for x in range(8):
                pair = []
                for p in range(2):
                    w_x, w_y = wt[0, x, p], wt[1, x, p]
                    if kind == LX:
                        value = co[0, x, p] - co[1, x, p]
                    elif kind == LY:
                        value = co[2, x, p] - co[3, x, p]
                    else:
                        value = (co[0, x, p] - co[1, x, p]) * w_y + (co[2, x, p] - co[3, x, p]) * w_x
                    pair.append(value)
                push.append(pair)
            vals = plus(push, sweep(push))
            vals = plus(vals, sweep(sweep(vals)))
            vals = plus(vals, sweep(sweep(sweep(sweep(vals)))))
            for x in range(8):
                for p in range(2):
                    put_b(kind, x, p, wt[kind, x, p] + vals[x][p] * (1.0 / 16.0))

    def gram(s, e):
        at = 8 + 64 * e

        def load_packed(ref, x, p):
            return by_slot(lambda slot: ref[x, pl.ds(at + 16 * slot + p, 8, stride=2), :])

        acc = {}

        def add(key, value):
            acc[key] = value if key not in acc else acc[key] + value

        for x in range(8):
            for p in range(2):
                a = load_packed(ta, x, p)
                src = load_packed(ts, x, p)
                here = [bq[s, kind, e, x, p] for kind in range(3)]
                t_e, t_n = teq[s, e, x, p], tnq[s, e, x, p]
                mass, d_e, d_n = [], [], []
                for kind in range(3):
                    if x < 7:
                        east_v = bq[s, kind, e, x + 1, p]
                    else:
                        east_v = lane_roll(bq[s, kind, e, 0, p], -1)
                        if kind != LY:
                            east_v = jnp.where(u8, 0.0, east_v)
                    if p:
                        north_v = sub_roll(bq[s, kind, e, x, 0], -1)
                        if kind != LX:
                            north_v = jnp.where(row7, 0.0, north_v)
                    else:
                        north_v = bq[s, kind, e, x, 1]
                    d_e.append(here[kind] - east_v)
                    d_n.append(here[kind] - north_v)
                    mass.append(a * here[kind])
                add((0, 0), a)
                add("r0", src)
                for kind in range(3):
                    add((0, kind + 1), mass[kind])
                    add("r" + str(kind + 1), src * here[kind])
                    w_e, w_n = t_e * d_e[kind], t_n * d_n[kind]
                    for other in range(kind, 3):
                        add((kind + 1, other + 1), mass[kind] * here[other] + w_e * d_e[other] + w_n * d_n[other])
        for index, key in enumerate(GRAM + ("r0", "r1", "r2", "r3")):
            value = acc[key]
            value = value + sub_roll(value, 4)
            value = value + sub_roll(value, 2)
            value = value + sub_roll(value, 1)
            sums[e, index] = value + lane_roll(value, -1)

    def owned(s, carry):
        copies = halo(s, 0, 7)
        copies[0].wait_recv()
        copies[1].wait_recv()

        @pl.when(s == 0)
        def _():
            for copy in halo(1, 0, 7) + halo(0, 7):
                copy.start()

        @pl.when(s == 1)
        def _():
            for copy in halo(1, 7):
                copy.start()

        for x in range(9):
            if x < 8:
                value = turn(hx_rows, 512 + 128 * s + x, 768 + 128 * s + x)
            else:
                value = turn(hx_rows, 768 + 128 * s, None, row24[pl.ds(pl.multiple_of(16 * s, 16), 16), :])
            tp[1, x, pl.ds(8, 128), :] = value
            first_rows[s, x] = value[:16]
        for copy in copies[2:5]:
            copy.wait_recv()
        for t in range(2):
            at = pl.ds(8 * t, 8)
            for x in range(8):
                tp[1, x, pl.ds(136 + 8 * t, 8), :] = pick(6, lo_n[s, 1, at, :], 6 - x, lo_ne0[s, at, :], 7 - x)
            tp[1, 8, pl.ds(136 + 8 * t, 8), :] = pick(6, lo_ne0[s, at, :], 6, lo_ne1[s, at, :], 7)

        def unit(e, inner):
            def put_t(x, p, east_t, north_t):
                teq[s, e, x, p] = east_t
                tnq[s, e, x, p] = north_t

            def put_b(kind, x, p, value):
                bq[s, kind, e, x, p] = value

            relax(1, 1, 16 + 64 * e, 16, put_t, put_b)
            return inner

        lax.fori_loop(0, 2, unit, 0)

        copies[5].wait_recv()
        copies[6].wait_recv()
        for rows, turned, at_row in ((ax_rows, ta, 16), (sx_rows, ts, 24)):
            for x in range(8):
                turned[x, pl.ds(0, 128), :] = turn(rows, 256 + 128 * s + x, 512 + 128 * s + x)
                at = pl.ds(at_row, 8)
                turned[x, pl.ds(128, 8), :] = pick(6, lo_n[s, 1, at, :], 6 - x, lo_ne0[s, at, :], 7 - x)

        def one(e, inner):
            gram(s, e)
            return inner

        lax.fori_loop(0, 2, one, 0)

        whole = []
        for index in range(14):
            whole.append(jnp.where(row % 2 == 0, sums[0, index], sums[1, index]))
        entries = corner_sums({key: whole[i] for i, key in enumerate(GRAM)}, whole[10:])
        for m in range(2):
            packed = jnp.zeros((8, 128), F32)
            for t in range(4 * m, min(4 * m + 4, 7)):
                pair = jnp.where(group % 2 == 0, entries[2 * t], lane_roll(entries[2 * t + 1], 1))
                packed = jnp.where(row // 2 == t % 4, pair, packed)
            ga[s, 0, m] = packed
        for copy in sums_messages(s):
            copy.start()
        return carry

    lax.fori_loop(0, SETS, owned, 0)

    def merge(left, right):
        inner = lane_roll(jnp.where(slot_of == 0, right, left), 2)
        outer = lane_roll(jnp.where(slot_of == 1, right, left), 4)
        upper = lane_roll(jnp.where(slot_of == 2, right, left), -2)
        ends = (slot_of == 1) | (slot_of == 2)
        first = jnp.where(slot_of == 0, left, jnp.where(ends, inner, outer))
        second = jnp.where(slot_of == 3, right, jnp.where(ends, upper, outer))
        return first, second

    def to_rows(s, merged, lines, dst):
        for k in range(5):
            for which in range(2):
                if k == 0 and which == 0:
                    continue
                for p in range(2):
                    for part in range(2):
                        value = None
                        for q in range(4):
                            moved = lane_roll(merged[k, 4 * part + q, p], 2 * q - 1 - 4 * which)
                            value = moved if value is None else jnp.where(slot_of == q, moved, value)
                        lines[part, pl.ds(16 * (2 * k - 1 + which) + p, 8, stride=2), :] = value
        for part in range(2):
            turned = lines[part, pl.ds(8, 128), :].T
            for q in range(4):
                for half in range(2):
                    for b in range(2):
                        first = 32 * q + 16 * half + 8 * b
                        layer = lax.rem(16 * s + (8 * b + 24), LAYERS)
                        dst[pl.ds(16 * layer + (8 * half + 4 * part + q), 8, stride=16), :] = turned[first : first + 8]

    low_send = pltpu.make_async_remote_copy(
        src_ref=po.at[pl.ds(0, 16)], dst_ref=up_layer, send_sem=vsend_sem.at[0], recv_sem=vrecv_sem.at[0],
        device_id=peer(0, 0, -1), device_id_type=MESH,
    )
    high_send = pltpu.make_async_remote_copy(
        src_ref=po.at[pl.ds(496, 16)], dst_ref=down_pair.at[0], send_sem=vsend_sem.at[1], recv_sem=vrecv_sem.at[1],
        device_id=peer(0, 0, 1), device_id_type=MESH,
    )
    vt_up = pltpu.make_async_remote_copy(
        src_ref=vt.at[pl.ds(496, 16)], dst_ref=down_pair.at[1], send_sem=vsend_sem.at[2], recv_sem=vrecv_sem.at[2],
        device_id=peer(0, 0, 1), device_id_type=MESH,
    )

    def rest(s, carry):
        for copy in halo(s, 7):
            copy.wait_recv()
        for x in range(9):
            if x < 8:
                value = turn(hx_rows, 128 * s + x, 256 + 128 * s + x)
            else:
                value = turn(hx_rows, 256 + 128 * s, 512 + 128 * s)
            tp[0, x, pl.ds(8, 128), :] = value
            tp[1, x, pl.ds(8, 16), :] = first_rows[s, x]
        for x in range(8):
            for t in range(2):
                at = pl.ds(8 * t, 8)
                tp[0, x, pl.ds(136 + 8 * t, 8), :] = pick(6, lo_nw[s, at, :], 6 - x, lo_n[s, 0, at, :], 7 - x)
            tp[0, x, pl.ds(0, 8), :] = pick(4, hi_sw[s], 4 - x, hi_s[s, 0], 5 - x)
            tp[1, x, pl.ds(0, 8), :] = pick(6, hi_s[s, 1], 6 - x, hi_se[s, 0], 7 - x)
        for t in range(2):
            at = pl.ds(8 * t, 8)
            tp[0, 8, pl.ds(136 + 8 * t, 8), :] = pick(6, lo_n[s, 0, at, :], 6, lo_n[s, 1, at, :], 7)
        tp[0, 8, pl.ds(0, 8), :] = pick(4, hi_s[s, 0], 4, hi_s[s, 1], 5)
        tp[1, 8, pl.ds(0, 8), :] = pick(6, hi_se[s, 0], 6, hi_se[s, 1], 7)

        def unit(e, inner):
            edge = e // 2

            def put_t(x, p, east_t, north_t):
                tew[e, x, p] = east_t
                tnw[e, x, p] = north_t

            def put_b(kind, x, p, value):
                bw[kind, e, x, p] = value

            relax(0, edge, (16 + 64 * e) * (1 - edge), 16 * (1 - edge), put_t, put_b)
            return inner

        lax.fori_loop(0, 3, unit, 0)
        tem[0] = tew[2]
        tnm[0] = tnw[2]

        def merge_t(e, inner):
            for x in range(8):
                for p in range(2):
                    for left, right, out in ((tew, teq, tem), (tnw, tnq, tnm)):
                        first, second = merge(left[e, x, p], right[s, e, x, p])
                        out[1 + 2 * e, x, p] = first
                        out[2 + 2 * e, x, p] = second
            return inner

        lax.fori_loop(0, 2, merge_t, 0)

        for copy in sums_messages(s):
            copy.wait()
        table = []
        for t in range(7):
            even, odd = [], []
            for i in range(SIDE):
                value = None
                for g in range(SIDE):
                    moved = sub_roll(ga[s, i * SIDE + g, t // 4], 2 * g - 2 * (t % 4))
                    value = moved if value is None else jnp.where(row // 2 == g, moved, value)
                even.append(jnp.where(group % 2 == 0, value, lane_roll(value, 1)))
                odd.append(jnp.where(group % 2 == 1, value, lane_roll(value, -1)))
            table.append(even)
            table.append(odd)
        b, c, d_side = assemble(table, slot_of)
        coarse = solve_nodes(b, c, d_side, slot_of)

        for place, i in enumerate((3, 0, 1)):
            nodes[0, place] = coarse[i]
            nodes[1, place] = node_shift(coarse[i], 1, slot_of)

        def line(by, place, j):
            return jnp.broadcast_to(nodes[by, place, pl.ds(j, 1), :], (8, 128))

        def put_weights(unit_at, c0, c1, c2, c3):
            cb[unit_at, 0] = c3
            cb[unit_at, 1] = c2 - c3
            cb[unit_at, 2] = c1 - c3
            cb[unit_at, 3] = (c0 - c1) - (c2 - c3)

        for e in range(2):
            near = [line(0, place, e) for place in range(3)]
            far = [line(1, place, e) for place in range(3)]
            put_weights(e, near[1], near[2], far[1], far[2])
            put_weights(2 + e, near[0], near[1], far[0], far[1])
        last = slot_of == 3
        below = [line(0, place, 7) for place in range(3)]
        first = [line(0, place, 0) for place in range(3)]
        put_weights(
            4,
            *(jnp.where(last, below[k + 1], lane_roll(below[k], -2)) for k in range(2)),
            *(jnp.where(last, lane_roll(first[k + 1], 6), lane_roll(first[k], 4)) for k in range(2)),
        )

        def pressures(w, basis_at, x, p):
            return (w[0] + w[1] * basis_at(0, x, p)) + (w[2] * basis_at(1, x, p) + w[3] * basis_at(2, x, p))

        def interpolate(e, inner):
            w_own = [cb[e, k] for k in range(4)]
            w_west = [cb[2 + e, k] for k in range(4)]
            for x in range(8):
                for p in range(2):
                    own = pressures(w_own, lambda kind, x, p: bq[s, kind, e, x, p], x, p)
                    other = pressures(w_west, lambda kind, x, p: bw[kind, e, x, p], x, p)
                    first, second = merge(other, own)
                    pm[1 + 2 * e, x, p] = first
                    pm[2 + 2 * e, x, p] = second
            return inner

        lax.fori_loop(0, 2, interpolate, 0)
        w_edge = [cb[4, k] for k in range(4)]
        for x in range(8):
            for p in range(2):
                pm[0, x, p] = pressures(w_edge, lambda kind, x, p: bw[kind, 2, x, p], x, p)
        to_rows(s, pm, yp, po)

        @pl.when((s == 0) & first_to_above)
        def _():
            pl.semaphore_wait(ready.at[0], 1)

        @pl.when((s == 0) & has_above)
        def _():
            high_send.start()
            vt_up.start()

        @pl.when((s == 0) & first_to_below)
        def _():
            pl.semaphore_wait(ready.at[1], 1)

        @pl.when((s == 0) & has_below)
        def _():
            low_send.start()

        def balance(k, inner):
            val = [[pm[k, x, p] for p in range(2)] for x in range(8)]
            f_e = [[None, None] for _ in range(8)]
            for x in range(8):
                for p in range(2):
                    east_v = val[x + 1][p] if x < 7 else lane_roll(val[0][p], -1)
                    f_e[x][p] = tem[k, x, p] * (val[x][p] - east_v)
            for x in range(8):
                after = lane_roll(jnp.where(lower, pm[k + 1, x, 0], val[x][0]), 4)
                after = sub_roll(jnp.where(row0, after, val[x][0]), -1)
                f_n0 = tnm[k, x, 0] * (val[x][0] - val[x][1])
                f_n1 = tnm[k, x, 1] * (val[x][1] - after)
                before = lane_roll(jnp.where(lower, f_n1, pu[x]), 4)
                before = sub_roll(jnp.where(row7, before, f_n1), 1)
                pu[x] = f_n1
                f_n = (f_n0, f_n1)
                f_s = (before, f_n0)
                for p in range(2):
                    f_w = f_e[x - 1][p] if x else lane_roll(f_e[7][p], 1)
                    hm[k, x, p] = (f_e[x][p] - f_w) + (f_n[p] - f_s[p])
            return inner

        lax.fori_loop(0, 5, balance, 0)
        to_rows(s, hm, yh, ro)
        return carry

    lax.fori_loop(0, SETS, rest, 0)
    press_copy = pltpu.make_async_copy(po, press_out, out_sem.at[0])
    press_copy.start()

    for half in range(2):
        before = None
        for l in range(LAYERS):
            at = pl.ds(16 * l + 8 * half, 8)
            place = (l + 8) % LAYERS
            here = po[at, :]
            value = sx[half, place] - ax[half, place] * here - ro[at, :]
            if before is not None:
                value = value + before
            if l < LAYERS - 1:
                before = vt[at, :] * (here - po[pl.ds(16 * (l + 1) + 8 * half, 8), :])
                value = value - before
            ro[at, :] = value

    middle_copy = pltpu.make_async_copy(ro.at[pl.ds(16, 480)], resid_out.at[pl.ds(16, 480)], out_sem.at[1])
    middle_copy.start()
    for s in range(SETS):
        for copy in halo(s):
            copy.wait_send()
    press_copy.wait()

    @pl.when(has_below)
    def _():
        vt_up.wait_recv()
        high_send.wait_recv()
        low_send.wait_send()

    @pl.when(has_above)
    def _():
        low_send.wait_recv()
        high_send.wait_send()
        vt_up.wait_send()

    above = jnp.where(has_above, vt[pl.ds(496, 16), :] * (po[pl.ds(496, 16), :] - up_layer[...]), 0.0)
    below = jnp.where(has_below, down_pair[1] * (down_pair[0] - po[pl.ds(0, 16), :]), 0.0)
    ro[pl.ds(496, 16), :] = ro[pl.ds(496, 16), :] - above
    ro[pl.ds(0, 16), :] = ro[pl.ds(0, 16), :] + below
    edge_copies = [
        pltpu.make_async_copy(ro.at[pl.ds(at, 16)], resid_out.at[pl.ds(at, 16)], out_sem.at[2 + i])
        for i, at in enumerate((0, 496))
    ]
    for copy in edge_copies:
        copy.start()
    middle_copy.wait()
    for copy in edge_copies:
        copy.wait()


def body(permeability, accumulation, source_term, vertical_trans):
    split = (LAYERS, 2, 8, 128)
    vmem = lambda *shape: pltpu.VMEM(shape, F32)
    anywhere = pl.BlockSpec(memory_space=pl.ANY)
    in_hbm = pl.BlockSpec(memory_space=pltpu.HBM)
    pressure, residual = pl.pallas_call(
        kernel,
        out_shape=[jax.ShapeDtypeStruct((512, 128), F32)] * 2,
        in_specs=[in_hbm] * 4,
        out_specs=[anywhere] * 2,
        scratch_shapes=[
            vmem(4, 32, 8, 128),
            vmem(3, 32, 8, 128),
            vmem(3, 32, 8, 128),
            vmem(512, 128),
            vmem(32, 128),
            vmem(32, 128),
            vmem(2, 2, 32, 128),
            vmem(2, 2, 8, 128),
            vmem(2, 2, 32, 128),
            vmem(2, 32, 128),
            vmem(2, 16, 128),
            vmem(2, 16, 128),
            vmem(2, 2, 8, 128),
            vmem(2, 2, 8, 128),
            vmem(2, 8, 128),
            vmem(2, 9, 152, 128),
            vmem(2, 9, 16, 128),
            vmem(8, 136, 128),
            vmem(8, 136, 128),
            vmem(2, 2, 8, 2, 8, 128),
            vmem(2, 2, 8, 2, 8, 128),
            vmem(2, 3, 2, 8, 2, 8, 128),
            vmem(3, 8, 2, 8, 128),
            vmem(3, 8, 2, 8, 128),
            vmem(3, 3, 8, 2, 8, 128),
            vmem(5, 8, 2, 8, 128),
            vmem(5, 8, 2, 8, 128),
            vmem(4, 8, 2, 8, 128),
            vmem(3, 8, 2, 8, 128),
            vmem(2, 14, 8, 128),
            vmem(2, 16, 2, 8, 128),
            vmem(2, 3, 8, 128),
            vmem(5, 4, 8, 128),
            vmem(8, 8, 128),
            vmem(6, 8, 2, 8, 128),
            vmem(5, 8, 2, 8, 128),
            vmem(2, 144, 128),
            vmem(2, 144, 128),
            vmem(512, 128),
            vmem(512, 128),
            vmem(16, 128),
            vmem(2, 16, 128),
            pltpu.SemaphoreType.REGULAR((2,)),
            pltpu.SemaphoreType.DMA((13,)),
            pltpu.SemaphoreType.DMA((2, 12)),
            pltpu.SemaphoreType.DMA((2, 12)),
            pltpu.SemaphoreType.DMA((2, 16)),
            pltpu.SemaphoreType.DMA((2, 16)),
            pltpu.SemaphoreType.DMA((3,)),
            pltpu.SemaphoreType.DMA((3,)),
            pltpu.SemaphoreType.DMA((4,)),
        ],
        compiler_params=pltpu.CompilerParams(
            collective_id=0, has_side_effects=True, vmem_limit_bytes=40 * 1024 * 1024
        ),
    )(
        *(
            pltpu.with_memory_space_constraint(value, pltpu.HBM)
            for value in (
                permeability.reshape(split),
                accumulation.reshape(split),
                source_term.reshape(split),
                vertical_trans.reshape(512, 128),
            )
        ),
    )
    return pressure.reshape(32, 16, 128), residual.reshape(32, 16, 128)


def solution(mesh):
    spec = P("gz", "gx", "gy")
    return jax.shard_map(
        body, mesh=mesh, in_specs=(spec,) * 4, out_specs=(spec, spec), check_vma=False
    )
```

```python
import jax
import jax.numpy as jnp
from jax import lax
from jax.experimental import pallas as pl
from jax.experimental.pallas import tpu as pltpu
from jax.sharding import PartitionSpec as P

LAYERS = 32
SETS = 2
SIDE = 4
DEPTH = 16
MIDDLE = DEPTH // 2
DUALS = 9
MESH = pl.DeviceIdType.MESH
F32 = jnp.float32
LX, LY = 0, 1


def lane_roll(value, groups):
    by = (groups * 16) % 128
    return value if by == 0 else pltpu.roll(value, by, axis=1)


def sub_roll(value, by):
    return pltpu.roll(value, by % 8, axis=0)


def inverse(value, rounds=1):
    guess = pl.reciprocal(value, approx=True)
    for _ in range(rounds):
        guess = guess * (2.0 - value * guess)
    return guess


def harmonic(left, right):
    return 2.0 * left * right * inverse(left + right)


def node_shift(value, by, slot):
    if by % 4 == 0:
        return sub_roll(value, -(by // 4))
    turned = lane_roll(value, -2 * by)
    if by > 0:
        return jnp.where(slot < 4 - by, turned, sub_roll(turned, -1))
    return jnp.where(slot >= -by, turned, sub_roll(turned, 1))


def factor(b):
    low = {}
    inv = [None] * 4
    for k in range(4):
        pivot = b[(k, k)]
        for m in range(k):
            if low.get((k, m)) is not None:
                pivot = pivot - low[(k, m)] * work[(k, m)]
        inv[k] = inverse(pivot, 2)
        if k == 0:
            work = {}
        for i in range(k + 1, 4):
            entry = b[(i, k)]
            for m in range(k):
                if low.get((i, m)) is None or work.get((k, m)) is None:
                    continue
                term = low[(i, m)] * work[(k, m)]
                entry = -term if entry is None else entry - term
            work[(i, k)] = entry
            low[(i, k)] = None if entry is None else entry * inv[k]
    return low, inv


def forward(low, column):
    out = []
    for i in range(4):
        value = column[i]
        for m in range(i):
            if low[(i, m)] is not None and out[m] is not None:
                term = low[(i, m)] * out[m]
                value = -term if value is None else value - term
        out.append(value)
    return out


def scaled(inv, column):
    return [None if v is None else v * inv[k] for k, v in enumerate(column)]


def inner(left, right):
    total = None
    for a, b in zip(left, right):
        if a is None or b is None:
            continue
        total = a * b if total is None else total + a * b
    return total


def subtract(value, term):
    if term is None:
        return value
    return -term if value is None else value - term


def shift_or_none(value, by, slot):
    return None if value is None else node_shift(value, by, slot)


def solve_nodes(b, c, d, slot):
    for step in (1, 2, 4, 8):
        a = [[shift_or_none(c[m][k], -step, slot) for m in range(4)] for k in range(4)]
        low, inv = factor(b)
        up = [forward(low, [c[i][k] for i in range(4)]) for k in range(4)]
        down = [forward(low, [a[i][k] for i in range(4)]) for k in range(4)]
        side = scaled(inv, forward(low, d))
        up_s = [scaled(inv, col) for col in up]
        down_s = [scaled(inv, col) for col in down]
        new_b = {}
        for i in range(4):
            for k in range(i + 1):
                value = subtract(b[(i, k)], shift_or_none(inner(up[i], up_s[k]), -step, slot))
                new_b[(i, k)] = subtract(value, shift_or_none(inner(down[i], down_s[k]), step, slot))
        new_d = []
        for i in range(4):
            value = subtract(d[i], shift_or_none(inner(up[i], side), -step, slot))
            new_d.append(subtract(value, shift_or_none(inner(down[i], side), step, slot)))
        new_c = [
            [subtract(None, shift_or_none(inner(down[i], up_s[k]), step, slot)) for k in range(4)]
            for i in range(4)
        ]
        b, c, d = new_b, new_c, new_d
    both = [[c[i][k] + node_shift(c[k][i], -16, slot) for k in range(4)] for i in range(4)]
    low, inv = factor(b)
    cols = [forward(low, [both[i][k] for i in range(4)]) for k in range(4)]
    cols_s = [scaled(inv, col) for col in cols]
    side = scaled(inv, forward(low, d))
    last = {}
    for i in range(4):
        for k in range(i + 1):
            last[(i, k)] = b[(i, k)] - node_shift(inner(cols[i], cols_s[k]), 16, slot)
    right = [d[i] - node_shift(inner(cols[i], side), 16, slot) for i in range(4)]
    low, inv = factor(last)
    value = scaled(inv, forward(low, right))
    for i in (2, 1, 0):
        for k in range(i + 1, 4):
            value[i] = value[i] - low[(k, i)] * value[k]
    return value


def corner_sums(g, r):
    k = [
        g[(3, 3)],
        g[(2, 3)] - g[(3, 3)],
        g[(1, 3)] - g[(3, 3)],
        g[(0, 3)] - g[(1, 3)] - g[(2, 3)] + g[(3, 3)],
        g[(2, 2)] - 2.0 * g[(2, 3)] + g[(3, 3)],
        g[(1, 2)] - g[(1, 3)] - g[(2, 3)] + g[(3, 3)],
        (g[(0, 2)] - g[(1, 2)] - g[(2, 2)]) + (2.0 * g[(2, 3)] - g[(0, 3)] + g[(1, 3)] - g[(3, 3)]),
        g[(1, 1)] - 2.0 * g[(1, 3)] + g[(3, 3)],
        (g[(0, 1)] - g[(1, 1)] - g[(1, 2)]) + (2.0 * g[(1, 3)] - g[(0, 3)] + g[(2, 3)] - g[(3, 3)]),
        (g[(0, 0)] + g[(1, 1)] + g[(2, 2)] + g[(3, 3)])
        - 2.0 * (g[(0, 1)] + g[(0, 2)] + g[(1, 3)] + g[(2, 3)] - g[(0, 3)] - g[(1, 2)]),
        r[3],
        r[2] - r[3],
        r[1] - r[3],
        r[0] - r[1] - r[2] + r[3],
    ]
    return k


GRAM = ((0, 0), (0, 1), (0, 2), (0, 3), (1, 1), (1, 2), (1, 3), (2, 2), (2, 3), (3, 3))


def assemble(t, slot):
    def back(value):
        return node_shift(value, -1, slot)

    b, d = {}, []
    c = [[None] * 4 for _ in range(4)]
    for i in range(4):
        w = (i - 1) % 4
        b[(i, i)] = t[0][i] + t[4][w] + back(t[7][i] + t[9][w])
        d.append(t[10][i] + t[11][w] + back(t[12][i] + t[13][w]))
        edge = t[1][i] + back(t[8][i])
        e = (i + 1) % 4
        b[(max(i, e), min(i, e))] = edge
        c[i][i] = t[2][i] + t[6][w]
        c[i][e] = t[3][i]
        c[e][i] = t[5][i]
    b[(2, 0)] = None
    b[(3, 1)] = None
    return b, c, d


def kernel(
    perm, accum, source, vtrans, press_out, resid_out,
    hx, ax, sx, vt, row24, row8, lo_out, hi_out, lo_n, lo_ne0, lo_ne1, lo_nw, hi_s, hi_se, hi_sw,
    tp, first_rows, ta, ts, teq, tnq, bq, tew, tnw, bw, tem, tnm, co, wt, sums, ga, nodes, cb, pu, ends, pm, hm, yp, yh, po, ro,
    up_layer, down_pair, ready,
    local_sem, send_sem, recv_sem, gsend_sem, grecv_sem, vsend_sem, vrecv_sem, out_sem,
):
    gx, gy, gz = lax.axis_index("gx"), lax.axis_index("gy"), lax.axis_index("gz")

    def peer(dx, dy, dz):
        return (
            lax.rem(gx + (dx + SIDE), SIDE),
            lax.rem(gy + (dy + SIDE), SIDE),
            lax.rem(gz + (dz + DEPTH), DEPTH),
        )

    has_below, has_above = gz > 0, gz < DEPTH - 1
    first_to_above = has_above & (gz != MIDDLE - 1)
    first_to_below = gz == MIDDLE
    next_to_above = gz == MIDDLE - 1
    next_to_below = has_below & (gz != MIDDLE)
    barrier = pltpu.get_barrier_semaphore()
    for dx in range(SIDE):
        for dy in range(SIDE):
            if dx or dy:
                pl.semaphore_signal(barrier, inc=1, device_id=peer(dx, dy, 0), device_id_type=MESH)
    for dz, there in ((-1, first_to_below), (1, first_to_above)):

        @pl.when(there)
        def _():
            pl.semaphore_signal(barrier, inc=1, device_id=peer(0, 0, dz), device_id_type=MESH)

    local = []

    def load(src, dst):
        copy = pltpu.make_async_copy(src, dst, local_sem.at[len(local)])
        copy.start()
        local.append(copy)

    for src, dst, first in ((perm, hx, 1), (accum, ax, 0), (source, sx, 0)):
        for half in range(2):
            load(src.at[pl.ds(24, 8), half], dst.at[first + half, pl.ds(0, 8)])
            load(src.at[pl.ds(0, 24), half], dst.at[first + half, pl.ds(8, 24)])
    load(vtrans, vt)

    row = lax.broadcasted_iota(jnp.int32, (8, 128), 0)
    lane = lax.broadcasted_iota(jnp.int32, (8, 128), 1)
    group = lane // 16
    slot_of = lane // 32
    lower = lane < 64
    u_base = jnp.where(group % 2 == 1, 8, 0)
    row0 = row == 0
    row7 = row == 7
    u0 = u_base == 0
    u8 = u_base == 8

    for x in range(8):
        for p in range(2):
            w_x = 1.0 - (u_base + x).astype(F32) / 16.0
            w_y = 1.0 - (2 * row + p).astype(F32) / 16.0
            wt[0, x, p] = w_x
            wt[1, x, p] = w_y
            wt[2, x, p] = w_x * w_y

    hx_rows = hx.reshape(4 * 256, 128)
    ax_rows = ax.reshape(3 * 256, 128)
    sx_rows = sx.reshape(3 * 256, 128)

    def edges(rows, base, at_row, depth, with_high):
        for s in range(SETS):
            for half in range(2):
                first = base + 256 * half + 128 * s
                turned = jnp.concatenate([rows[pl.ds(first + x, 16, stride=8), :] for x in range(8)], axis=0).T
                lo_out[s, half, pl.ds(at_row, depth), :] = turned[:depth]
                if with_high:
                    hi_out[s, half] = turned[120:]

    for copy in local[:4]:
        copy.wait()
    row8[...] = hx_rows[pl.ds(512, LAYERS, stride=8), :]
    pl.semaphore_wait(barrier, 15 + next_to_above.astype(jnp.int32) + next_to_below.astype(jnp.int32))

    west, east = peer(-1, 0, 0), peer(1, 0, 0)
    south, north = peer(0, -1, 0), peer(0, 1, 0)

    def halo(s, first=0, end=12):
        mine = pl.ds(16 * s, 16)
        routes = (
            (hx.at[1, mine], hx.at[3, mine], west),
            (row8.at[mine], row24.at[mine], west),
            (lo_out.at[s], lo_n.at[s], south),
            (lo_out.at[s, 0], lo_ne0.at[s], peer(-1, -1, 0)),
            (lo_out.at[s, 1, pl.ds(0, 16)], lo_ne1.at[s], peer(-1, -1, 0)),
            (ax.at[0, mine], ax.at[2, mine], west),
            (sx.at[0, mine], sx.at[2, mine], west),
            (hx.at[2, mine], hx.at[0, mine], east),
            (lo_out.at[s, 1, pl.ds(0, 16)], lo_nw.at[s], peer(1, -1, 0)),
            (hi_out.at[s], hi_s.at[s], north),
            (hi_out.at[s], hi_se.at[s], peer(-1, 1, 0)),
            (hi_out.at[s, 1], hi_sw.at[s], peer(1, 1, 0)),
        )
        return [
            pltpu.make_async_remote_copy(
                src_ref=src, dst_ref=dst, send_sem=send_sem.at[s, i], recv_sem=recv_sem.at[s, i],
                device_id=target, device_id_type=MESH,
            )
            for i, (src, dst, target) in enumerate(routes)
            if first <= i < end
        ]

    def sums_messages(s):
        copies = []
        for dx in range(SIDE):
            for dy in range(SIDE):
                if dx or dy:
                    slot = (-dx % SIDE) * SIDE + (-dy % SIDE)
                    copies.append(
                        pltpu.make_async_remote_copy(
                            src_ref=ga.at[s, 0], dst_ref=ga.at[s, slot],
                            send_sem=gsend_sem.at[s, slot], recv_sem=grecv_sem.at[s, slot],
                            device_id=peer(dx, dy, 0), device_id_type=MESH,
                        )
                    )
        return copies

    for copy in halo(0, 0, 2):
        copy.start()
    for copy in local[4:]:
        copy.wait()
    for copy in halo(0, 5, 7):
        copy.start()
    edges(hx_rows, 256, 0, 16, True)
    edges(ax_rows, 0, 16, 8, False)
    edges(sx_rows, 0, 24, 8, False)
    for copy in halo(0, 2, 5):
        copy.start()
    for dz, at, there in ((-1, 0, next_to_below), (1, 1, next_to_above)):

        @pl.when(there)
        def _():
            pl.semaphore_signal(ready.at[at], inc=1, device_id=peer(0, 0, dz), device_id_type=MESH)

    def pick(at_group, left, by_left, right, by_right):
        return jnp.where(group == at_group, lane_roll(left, by_left), lane_roll(right, by_right))

    def turn(rows, first, second, fixed=None):
        part = [rows[pl.ds(first, 16, stride=8), :]]
        part.append(fixed if fixed is not None else rows[pl.ds(second, 16, stride=8), :])
        return jnp.concatenate(part * 4, axis=0).T

    def by_slot(load_slot):
        value = load_slot(3)
        for slot in (2, 1, 0):
            value = jnp.where(slot_of == slot, load_slot(slot), value)
        return value

    def relax(most, last, at, step, put_t, put_b):
        def cell(x, off):
            return by_slot(
                lambda slot: tp[last if slot == 3 else most, x, pl.ds(at + step * slot + off, 8, stride=2), :]
            )

        cells = [[cell(x, p) for p in range(2)] for x in range(9)]
        t_e = [[harmonic(cells[x][p], cells[x + 1][p]) for p in range(2)] for x in range(8)]
        for x in range(8):
            t_n = [harmonic(cells[x][0], cells[x][1]), harmonic(cells[x][1], cell(x, 2))]
            t_s = [sub_roll(t_n[1], 1), t_n[0]]
            for p in range(2):
                t_w = t_e[x - 1][p] if x else lane_roll(t_e[7][p], 1)
                put_t(x, p, t_e[x][p], t_n[p])
                inv = inverse((t_w + t_e[x][p]) + (t_s[p] + t_n[p]))
                if p == 0 and x == 0:
                    inv = jnp.where(row0 | u0, 0.0, inv)
                elif p == 0:
                    inv = jnp.where(row0, 0.0, inv)
                elif x == 0:
                    inv = jnp.where(u0, 0.0, inv)
                co[0, x, p] = t_w * inv
                co[1, x, p] = t_e[x][p] * inv
                co[2, x, p] = t_s[p] * inv
                co[3, x, p] = t_n[p] * inv

        def sweep(kinds):
            new = [[[None, None] for _ in range(8)] for _ in kinds]
            for x in (0, 7, 1, 6, 2, 5, 3, 4):
                for p in range(2):
                    c_w, c_e, c_s, c_n = (co[i, x, p] for i in range(4))
                    for vals, out in zip(kinds, new):
                        west_v = vals[x - 1][p] if x else lane_roll(vals[7][p], 1)
                        east_v = vals[x + 1][p] if x < 7 else lane_roll(vals[0][p], -1)
                        south_v = vals[x][0] if p else sub_roll(vals[x][1], 1)
                        north_v = sub_roll(vals[x][0], -1) if p else vals[x][1]
                        out[x][p] = (c_w * west_v + c_e * east_v) + (c_s * south_v + c_n * north_v)
            return new

        def plus(left, right):
            return [[[a[x][p] + b[x][p] for p in range(2)] for x in range(8)] for a, b in zip(left, right)]

        for kinds in ((0, 1, 2),):
            push = []
            for kind in kinds:
                push.append([[None, None] for _ in range(8)])
                for x in range(8):
                    for p in range(2):
                        w_x, w_y = wt[0, x, p], wt[1, x, p]
                        if kind == LX:
                            value = co[0, x, p] - co[1, x, p]
                        elif kind == LY:
                            value = co[2, x, p] - co[3, x, p]
                        else:
                            value = (co[0, x, p] - co[1, x, p]) * w_y + (co[2, x, p] - co[3, x, p]) * w_x
                        push[-1][x][p] = value
            vals = plus(push, sweep(push))
            vals = plus(vals, sweep(sweep(vals)))
            vals = plus(vals, sweep(sweep(sweep(sweep(vals)))))
            for kind, done in zip(kinds, vals):
                for x in range(8):
                    for p in range(2):
                        put_b(kind, x, p, wt[kind, x, p] + done[x][p] * (1.0 / 16.0))

    def gram(s, e):
        at = 8 + 64 * e

        def load_packed(ref, x, p):
            return by_slot(lambda slot: ref[x, pl.ds(at + 16 * slot + p, 8, stride=2), :])

        acc = {}

        def add(key, value):
            acc[key] = value if key not in acc else acc[key] + value

        for x in range(8):
            for p in range(2):
                a = load_packed(ta, x, p)
                src = load_packed(ts, x, p)
                here = [bq[s, kind, e, x, p] for kind in range(3)]
                t_e, t_n = teq[s, e, x, p], tnq[s, e, x, p]
                mass, d_e, d_n = [], [], []
                for kind in range(3):
                    if x < 7:
                        east_v = bq[s, kind, e, x + 1, p]
                    else:
                        east_v = lane_roll(bq[s, kind, e, 0, p], -1)
                        if kind != LY:
                            east_v = jnp.where(u8, 0.0, east_v)
                    if p:
                        north_v = sub_roll(bq[s, kind, e, x, 0], -1)
                        if kind != LX:
                            north_v = jnp.where(row7, 0.0, north_v)
                    else:
                        north_v = bq[s, kind, e, x, 1]
                    d_e.append(here[kind] - east_v)
                    d_n.append(here[kind] - north_v)
                    mass.append(a * here[kind])
                add((0, 0), a)
                add("r0", src)
                for kind in range(3):
                    add((0, kind + 1), mass[kind])
                    add("r" + str(kind + 1), src * here[kind])
                    w_e, w_n = t_e * d_e[kind], t_n * d_n[kind]
                    for other in range(kind, 3):
                        add((kind + 1, other + 1), mass[kind] * here[other] + w_e * d_e[other] + w_n * d_n[other])
        for index, key in enumerate(GRAM + ("r0", "r1", "r2", "r3")):
            value = acc[key]
            value = value + sub_roll(value, 4)
            value = value + sub_roll(value, 2)
            value = value + sub_roll(value, 1)
            sums[e, index] = value + lane_roll(value, -1)

    def owned(s, carry):
        copies = halo(s, 0, 7)
        copies[0].wait_recv()
        copies[1].wait_recv()

        @pl.when(s == 0)
        def _():
            for copy in halo(1, 0, 7) + halo(0, 7):
                copy.start()

        @pl.when(s == 1)
        def _():
            for copy in halo(1, 7):
                copy.start()

        for x in range(9):
            if x < 8:
                value = turn(hx_rows, 512 + 128 * s + x, 768 + 128 * s + x)
            else:
                value = turn(hx_rows, 768 + 128 * s, None, row24[pl.ds(pl.multiple_of(16 * s, 16), 16), :])
            tp[1, x, pl.ds(8, 128), :] = value
            first_rows[s, x] = value[:16]
        for copy in copies[2:5]:
            copy.wait_recv()
        for t in range(2):
            at = pl.ds(8 * t, 8)
            for x in range(8):
                tp[1, x, pl.ds(136 + 8 * t, 8), :] = pick(6, lo_n[s, 1, at, :], 6 - x, lo_ne0[s, at, :], 7 - x)
            tp[1, 8, pl.ds(136 + 8 * t, 8), :] = pick(6, lo_ne0[s, at, :], 6, lo_ne1[s, at, :], 7)

        def unit(e, inner):
            def put_t(x, p, east_t, north_t):
                teq[s, e, x, p] = east_t
                tnq[s, e, x, p] = north_t

            def put_b(kind, x, p, value):
                bq[s, kind, e, x, p] = value

            relax(1, 1, 16 + 64 * e, 16, put_t, put_b)
            return inner

        lax.fori_loop(0, 2, unit, 0)

        copies[5].wait_recv()
        copies[6].wait_recv()
        for rows, turned, at_row in ((ax_rows, ta, 16), (sx_rows, ts, 24)):
            for x in range(8):
                turned[x, pl.ds(0, 128), :] = turn(rows, 256 + 128 * s + x, 512 + 128 * s + x)
                at = pl.ds(at_row, 8)
                turned[x, pl.ds(128, 8), :] = pick(6, lo_n[s, 1, at, :], 6 - x, lo_ne0[s, at, :], 7 - x)

        def one(e, inner):
            gram(s, e)
            return inner

        lax.fori_loop(0, 2, one, 0)

        whole = []
        for index in range(14):
            whole.append(jnp.where(row % 2 == 0, sums[0, index], sums[1, index]))
        entries = corner_sums({key: whole[i] for i, key in enumerate(GRAM)}, whole[10:])
        for m in range(2):
            packed = jnp.zeros((8, 128), F32)
            for t in range(4 * m, min(4 * m + 4, 7)):
                pair = jnp.where(group % 2 == 0, entries[2 * t], lane_roll(entries[2 * t + 1], 1))
                packed = jnp.where(row // 2 == t % 4, pair, packed)
            ga[s, 0, m] = packed
        for copy in sums_messages(s):
            copy.start()
        return carry

    lax.fori_loop(0, SETS, owned, 0)

    even = group % 2 == 0
    even_slot = slot_of % 2 == 0

    def to_rows(s, tiles, lines, dst):
        for part in range(2):
            for p in range(2):
                for e in range(2):
                    a = [tiles[e, 4 * part + q, p] for q in range(4)]
                    b = [None] * 4
                    for q in range(2):
                        crossed = lane_roll(jnp.where(lower, a[q + 2], a[q]), 4)
                        b[q] = jnp.where(lower, a[q], crossed)
                        b[q + 2] = jnp.where(lower, crossed, a[q + 2])
                    for q in (0, 2):
                        for slot, value in (
                            (q, jnp.where(even_slot, b[q], lane_roll(b[q + 1], 2))),
                            (q + 1, jnp.where(even_slot, lane_roll(b[q], -2), b[q + 1])),
                        ):
                            lines[part, pl.ds(16 * (1 + 4 * e + slot) + p, 8, stride=2), :] = value
                value = tiles[2, 4 * part + 3, p]
                for q in range(3):
                    value = jnp.where(slot_of == q, lane_roll(tiles[2, 4 * part + q, p], 2 * (q - 3)), value)
                lines[part, pl.ds(p, 8, stride=2), :] = value
        for part in range(2):
            turned = lines[part, pl.ds(8, 128), :].T
            for q in range(4):
                for half in range(2):
                    for b in range(2):
                        first = 32 * q + 16 * (1 - half) + 8 * b
                        layer = lax.rem(16 * s + (8 * b + 24), LAYERS)
                        dst[pl.ds(16 * layer + (8 * half + 4 * part + q), 8, stride=16), :] = turned[first : first + 8]

    low_send = pltpu.make_async_remote_copy(
        src_ref=po.at[pl.ds(0, 16)], dst_ref=up_layer, send_sem=vsend_sem.at[0], recv_sem=vrecv_sem.at[0],
        device_id=peer(0, 0, -1), device_id_type=MESH,
    )
    high_send = pltpu.make_async_remote_copy(
        src_ref=po.at[pl.ds(496, 16)], dst_ref=down_pair.at[0], send_sem=vsend_sem.at[1], recv_sem=vrecv_sem.at[1],
        device_id=peer(0, 0, 1), device_id_type=MESH,
    )
    vt_up = pltpu.make_async_remote_copy(
        src_ref=vt.at[pl.ds(496, 16)], dst_ref=down_pair.at[1], send_sem=vsend_sem.at[2], recv_sem=vrecv_sem.at[2],
        device_id=peer(0, 0, 1), device_id_type=MESH,
    )

    def rest(s, carry):
        for copy in halo(s, 7):
            copy.wait_recv()
        for x in range(9):
            if x < 8:
                value = turn(hx_rows, 128 * s + x, 256 + 128 * s + x)
            else:
                value = turn(hx_rows, 256 + 128 * s, 512 + 128 * s)
            tp[0, x, pl.ds(8, 128), :] = value
            tp[1, x, pl.ds(8, 16), :] = first_rows[s, x]
        for x in range(8):
            for t in range(2):
                at = pl.ds(8 * t, 8)
                tp[0, x, pl.ds(136 + 8 * t, 8), :] = pick(6, lo_nw[s, at, :], 6 - x, lo_n[s, 0, at, :], 7 - x)
            tp[0, x, pl.ds(0, 8), :] = pick(4, hi_sw[s], 4 - x, hi_s[s, 0], 5 - x)
            tp[1, x, pl.ds(0, 8), :] = pick(6, hi_s[s, 1], 6 - x, hi_se[s, 0], 7 - x)
        for t in range(2):
            at = pl.ds(8 * t, 8)
            tp[0, 8, pl.ds(136 + 8 * t, 8), :] = pick(6, lo_n[s, 0, at, :], 6, lo_n[s, 1, at, :], 7)
        tp[0, 8, pl.ds(0, 8), :] = pick(4, hi_s[s, 0], 4, hi_s[s, 1], 5)
        tp[1, 8, pl.ds(0, 8), :] = pick(6, hi_se[s, 0], 6, hi_se[s, 1], 7)

        def unit(e, inner):
            edge = e // 2

            def put_t(x, p, east_t, north_t):
                tew[e, x, p] = east_t
                tnw[e, x, p] = north_t

            def put_b(kind, x, p, value):
                bw[kind, e, x, p] = value

            relax(0, edge, (16 + 64 * e) * (1 - edge), 16 * (1 - edge), put_t, put_b)
            return inner

        lax.fori_loop(0, 3, unit, 0)
        for copy in sums_messages(s):
            copy.wait()
        table = []
        for t in range(7):
            pair = ([], [])
            for i in range(SIDE):
                value = None
                for g in range(SIDE):
                    moved = sub_roll(ga[s, i * SIDE + g, t // 4], 2 * g - 2 * (t % 4))
                    value = moved if value is None else jnp.where(row // 2 == g, moved, value)
                pair[0].append(jnp.where(group % 2 == 0, value, lane_roll(value, 1)))
                pair[1].append(jnp.where(group % 2 == 1, value, lane_roll(value, -1)))
            table.append(pair[0])
            table.append(pair[1])
        b, c, d_side = assemble(table, slot_of)
        coarse = solve_nodes(b, c, d_side, slot_of)

        for place, i in enumerate((3, 0, 1)):
            nodes[0, place] = coarse[i]
            nodes[1, place] = node_shift(coarse[i], 1, slot_of)

        def line(by, place, j):
            return jnp.broadcast_to(nodes[by, place, pl.ds(j, 1), :], (8, 128))

        def put_weights(unit_at, c0, c1, c2, c3):
            cb[unit_at, 0] = c3
            cb[unit_at, 1] = c2 - c3
            cb[unit_at, 2] = c1 - c3
            cb[unit_at, 3] = (c0 - c1) - (c2 - c3)

        for e in range(2):
            near = [line(0, place, e) for place in range(3)]
            far = [line(1, place, e) for place in range(3)]
            put_weights(e, near[1], near[2], far[1], far[2])
            put_weights(2 + e, near[0], near[1], far[0], far[1])
        last = slot_of == 3
        below = [line(0, place, 7) for place in range(3)]
        first = [line(0, place, 0) for place in range(3)]
        put_weights(
            4,
            *(jnp.where(last, below[k + 1], lane_roll(below[k], -2)) for k in range(2)),
            *(jnp.where(last, lane_roll(first[k + 1], 6), lane_roll(first[k], 4)) for k in range(2)),
        )

        def pressures(w, basis_at, x, p):
            return (w[0] + w[1] * basis_at(0, x, p)) + (w[2] * basis_at(1, x, p) + w[3] * basis_at(2, x, p))

        def put_ends(k, east_0, west_7, west_0, t_west_7, p, by):
            ends[k, 0, p] = jnp.where(even, lane_roll(east_0, -1), lane_roll(east_0, 1))
            ends[k, 1, p] = lane_roll(t_west_7 * (west_7 - lane_roll(west_0, -1)), by)

        def interpolate(e, inner):
            w_own = [cb[e, k] for k in range(4)]
            w_west = [cb[2 + e, k] for k in range(4)]
            w_both = [jnp.where(even, a, b) for a, b in zip(w_own, w_west)]

            def own(kind, x, p):
                return bq[s, kind, e, x, p]

            def other(kind, x, p):
                return bw[kind, e, x, p]

            def both(kind, x, p):
                return jnp.where(even, bq[s, kind, e, x, p], bw[kind, e, x, p])

            for p in range(2):
                for x in range(8):
                    pm[e, x, p] = pressures(w_both, both, x, p)
                    tem[e, x, p] = jnp.where(even, teq[s, e, x, p], tew[e, x, p])
                    tnm[e, x, p] = jnp.where(even, tnq[s, e, x, p], tnw[e, x, p])
                put_ends(
                    e, pressures(w_own, own, 0, p), pressures(w_west, other, 7, p),
                    pressures(w_west, other, 0, p), tew[e, 7, p], p, 1,
                )
            return inner

        lax.fori_loop(0, 2, interpolate, 0)
        w_edge = [cb[4, k] for k in range(4)]

        def to_own(value):
            return jnp.where(even, value, lane_roll(value, 2))

        for p in range(2):
            edge = [pressures(w_edge, lambda kind, x, p: bw[kind, 2, x, p], x, p) for x in range(8)]
            for x in range(8):
                pm[2, x, p] = to_own(edge[x])
                tem[2, x, p] = to_own(tew[2, x, p])
                tnm[2, x, p] = to_own(tnw[2, x, p])
            put_ends(2, edge[0], edge[7], edge[0], tew[2, 7, p], p, 3)
        to_rows(s, pm, yp, po)

        @pl.when((s == 0) & first_to_above)
        def _():
            pl.semaphore_wait(ready.at[0], 1)

        @pl.when((s == 0) & has_above)
        def _():
            high_send.start()
            vt_up.start()

        @pl.when((s == 0) & first_to_below)
        def _():
            pl.semaphore_wait(ready.at[1], 1)

        @pl.when((s == 0) & has_below)
        def _():
            low_send.start()

        def balance(i, inner):
            k = lax.rem(i + 2, 3)
            val = [[pm[k, x, p] for p in range(2)] for x in range(8)]
            f_e = [[None, None] for _ in range(8)]
            for x in range(8):
                for p in range(2):
                    east_v = val[x + 1][p] if x < 7 else ends[k, 0, p]
                    f_e[x][p] = tem[k, x, p] * (val[x][p] - east_v)
            for x in range(8):
                after = lane_roll(jnp.where(slot_of == 0, pm[i, x, 0], val[x][0]), -2)
                after = sub_roll(jnp.where(row0, after, val[x][0]), -1)
                f_n0 = tnm[k, x, 0] * (val[x][0] - val[x][1])
                f_n1 = tnm[k, x, 1] * (val[x][1] - after)
                before = lane_roll(jnp.where(slot_of == 3, pu[x], f_n1), 2)
                before = sub_roll(jnp.where(row7, before, f_n1), 1)
                pu[x] = f_n1
                f_n = (f_n0, f_n1)
                f_s = (before, f_n0)
                for p in range(2):
                    f_w = f_e[x - 1][p] if x else jnp.where(even, lane_roll(f_e[7][p], -1), ends[k, 1, p])
                    hm[k, x, p] = (f_e[x][p] - f_w) + (f_n[p] - f_s[p])
            return inner

        lax.fori_loop(0, 3, balance, 0)
        to_rows(s, hm, yh, ro)
        return carry

    lax.fori_loop(0, SETS, rest, 0)
    press_copy = pltpu.make_async_copy(po, press_out, out_sem.at[0])
    press_copy.start()

    for half in range(2):
        before = None
        for l in range(LAYERS):
            at = pl.ds(16 * l + 8 * half, 8)
            place = (l + 8) % LAYERS
            here = po[at, :]
            value = sx[half, place] - ax[half, place] * here - ro[at, :]
            if before is not None:
                value = value + before
            if l < LAYERS - 1:
                before = vt[at, :] * (here - po[pl.ds(16 * (l + 1) + 8 * half, 8), :])
                value = value - before
            ro[at, :] = value

    middle_copy = pltpu.make_async_copy(ro.at[pl.ds(16, 480)], resid_out.at[pl.ds(16, 480)], out_sem.at[1])
    middle_copy.start()
    for s in range(SETS):
        for copy in halo(s):
            copy.wait_send()
    press_copy.wait()

    @pl.when(has_below)
    def _():
        vt_up.wait_recv()
        high_send.wait_recv()
        low_send.wait_send()

    @pl.when(has_above)
    def _():
        low_send.wait_recv()
        high_send.wait_send()
        vt_up.wait_send()

    above = jnp.where(has_above, vt[pl.ds(496, 16), :] * (po[pl.ds(496, 16), :] - up_layer[...]), 0.0)
    below = jnp.where(has_below, down_pair[1] * (down_pair[0] - po[pl.ds(0, 16), :]), 0.0)
    ro[pl.ds(496, 16), :] = ro[pl.ds(496, 16), :] - above
    ro[pl.ds(0, 16), :] = ro[pl.ds(0, 16), :] + below
    edge_copies = [
        pltpu.make_async_copy(ro.at[pl.ds(at, 16)], resid_out.at[pl.ds(at, 16)], out_sem.at[2 + i])
        for i, at in enumerate((0, 496))
    ]
    for copy in edge_copies:
        copy.start()
    middle_copy.wait()
    for copy in edge_copies:
        copy.wait()


def body(permeability, accumulation, source_term, vertical_trans):
    split = (LAYERS, 2, 8, 128)
    vmem = lambda *shape: pltpu.VMEM(shape, F32)
    anywhere = pl.BlockSpec(memory_space=pl.ANY)
    in_hbm = pl.BlockSpec(memory_space=pltpu.HBM)
    pressure, residual = pl.pallas_call(
        kernel,
        out_shape=[jax.ShapeDtypeStruct((512, 128), F32)] * 2,
        in_specs=[in_hbm] * 4,
        out_specs=[anywhere] * 2,
        scratch_shapes=[
            vmem(4, 32, 8, 128),
            vmem(3, 32, 8, 128),
            vmem(3, 32, 8, 128),
            vmem(512, 128),
            vmem(32, 128),
            vmem(32, 128),
            vmem(2, 2, 32, 128),
            vmem(2, 2, 8, 128),
            vmem(2, 2, 32, 128),
            vmem(2, 32, 128),
            vmem(2, 16, 128),
            vmem(2, 16, 128),
            vmem(2, 2, 8, 128),
            vmem(2, 2, 8, 128),
            vmem(2, 8, 128),
            vmem(2, 9, 152, 128),
            vmem(2, 9, 16, 128),
            vmem(8, 136, 128),
            vmem(8, 136, 128),
            vmem(2, 2, 8, 2, 8, 128),
            vmem(2, 2, 8, 2, 8, 128),
            vmem(2, 3, 2, 8, 2, 8, 128),
            vmem(3, 8, 2, 8, 128),
            vmem(3, 8, 2, 8, 128),
            vmem(3, 3, 8, 2, 8, 128),
            vmem(3, 8, 2, 8, 128),
            vmem(3, 8, 2, 8, 128),
            vmem(4, 8, 2, 8, 128),
            vmem(3, 8, 2, 8, 128),
            vmem(2, 14, 8, 128),
            vmem(2, 16, 2, 8, 128),
            vmem(2, 3, 8, 128),
            vmem(5, 4, 8, 128),
            vmem(8, 8, 128),
            vmem(3, 2, 2, 8, 128),
            vmem(3, 8, 2, 8, 128),
            vmem(3, 8, 2, 8, 128),
            vmem(2, 144, 128),
            vmem(2, 144, 128),
            vmem(512, 128),
            vmem(512, 128),
            vmem(16, 128),
            vmem(2, 16, 128),
            pltpu.SemaphoreType.REGULAR((2,)),
            pltpu.SemaphoreType.DMA((13,)),
            pltpu.SemaphoreType.DMA((2, 12)),
            pltpu.SemaphoreType.DMA((2, 12)),
            pltpu.SemaphoreType.DMA((2, 16)),
            pltpu.SemaphoreType.DMA((2, 16)),
            pltpu.SemaphoreType.DMA((3,)),
            pltpu.SemaphoreType.DMA((3,)),
            pltpu.SemaphoreType.DMA((4,)),
        ],
        compiler_params=pltpu.CompilerParams(
            collective_id=0, has_side_effects=True, vmem_limit_bytes=40 * 1024 * 1024
        ),
    )(
        *(
            pltpu.with_memory_space_constraint(value, pltpu.HBM)
            for value in (
                permeability.reshape(split),
                accumulation.reshape(split),
                source_term.reshape(split),
                vertical_trans.reshape(512, 128),
            )
        ),
    )
    return pressure.reshape(32, 16, 128), residual.reshape(32, 16, 128)


def solution(mesh):
    spec = P("gz", "gx", "gy")
    return jax.shard_map(
        body, mesh=mesh, in_specs=(spec,) * 4, out_specs=(spec, spec), check_vma=False
    )
```

```python
import jax
import jax.numpy as jnp
from jax import lax
from jax.experimental import pallas as pl
from jax.experimental.pallas import tpu as pltpu
from jax.sharding import PartitionSpec as P

LAYERS = 32
SETS = 2
SIDE = 4
DEPTH = 16
MIDDLE = DEPTH // 2
DUALS = 9
MESH = pl.DeviceIdType.MESH
F32 = jnp.float32
LX, LY = 0, 1


def lane_roll(value, groups):
    by = (groups * 16) % 128
    return value if by == 0 else pltpu.roll(value, by, axis=1)


def sub_roll(value, by):
    return pltpu.roll(value, by % 8, axis=0)


def inverse(value, rounds=1):
    guess = pl.reciprocal(value, approx=True)
    for _ in range(rounds):
        guess = guess * (2.0 - value * guess)
    return guess


def harmonic(left, right):
    return 2.0 * left * right * inverse(left + right)


def node_shift(value, by, slot):
    if by % 4 == 0:
        return sub_roll(value, -(by // 4))
    turned = lane_roll(value, -2 * by)
    if by > 0:
        return jnp.where(slot < 4 - by, turned, sub_roll(turned, -1))
    return jnp.where(slot >= -by, turned, sub_roll(turned, 1))


def factor(b):
    low = {}
    inv = [None] * 4
    for k in range(4):
        pivot = b[(k, k)]
        for m in range(k):
            if low.get((k, m)) is not None:
                pivot = pivot - low[(k, m)] * work[(k, m)]
        inv[k] = inverse(pivot, 2)
        if k == 0:
            work = {}
        for i in range(k + 1, 4):
            entry = b[(i, k)]
            for m in range(k):
                if low.get((i, m)) is None or work.get((k, m)) is None:
                    continue
                term = low[(i, m)] * work[(k, m)]
                entry = -term if entry is None else entry - term
            work[(i, k)] = entry
            low[(i, k)] = None if entry is None else entry * inv[k]
    return low, inv


def forward(low, column):
    out = []
    for i in range(4):
        value = column[i]
        for m in range(i):
            if low[(i, m)] is not None and out[m] is not None:
                term = low[(i, m)] * out[m]
                value = -term if value is None else value - term
        out.append(value)
    return out


def scaled(inv, column):
    return [None if v is None else v * inv[k] for k, v in enumerate(column)]


def inner(left, right):
    total = None
    for a, b in zip(left, right):
        if a is None or b is None:
            continue
        total = a * b if total is None else total + a * b
    return total


def subtract(value, term):
    if term is None:
        return value
    return -term if value is None else value - term


def shift_or_none(value, by, slot):
    return None if value is None else node_shift(value, by, slot)


def solve_nodes(b, c, d, slot):
    for step in (1, 2, 4, 8):
        a = [[shift_or_none(c[m][k], -step, slot) for m in range(4)] for k in range(4)]
        low, inv = factor(b)
        up = [forward(low, [c[i][k] for i in range(4)]) for k in range(4)]
        down = [forward(low, [a[i][k] for i in range(4)]) for k in range(4)]
        side = scaled(inv, forward(low, d))
        up_s = [scaled(inv, col) for col in up]
        down_s = [scaled(inv, col) for col in down]
        new_b = {}
        for i in range(4):
            for k in range(i + 1):
                value = subtract(b[(i, k)], shift_or_none(inner(up[i], up_s[k]), -step, slot))
                new_b[(i, k)] = subtract(value, shift_or_none(inner(down[i], down_s[k]), step, slot))
        new_d = []
        for i in range(4):
            value = subtract(d[i], shift_or_none(inner(up[i], side), -step, slot))
            new_d.append(subtract(value, shift_or_none(inner(down[i], side), step, slot)))
        new_c = [
            [subtract(None, shift_or_none(inner(down[i], up_s[k]), step, slot)) for k in range(4)]
            for i in range(4)
        ]
        b, c, d = new_b, new_c, new_d
    both = [[c[i][k] + node_shift(c[k][i], -16, slot) for k in range(4)] for i in range(4)]
    low, inv = factor(b)
    cols = [forward(low, [both[i][k] for i in range(4)]) for k in range(4)]
    cols_s = [scaled(inv, col) for col in cols]
    side = scaled(inv, forward(low, d))
    last = {}
    for i in range(4):
        for k in range(i + 1):
            last[(i, k)] = b[(i, k)] - node_shift(inner(cols[i], cols_s[k]), 16, slot)
    right = [d[i] - node_shift(inner(cols[i], side), 16, slot) for i in range(4)]
    low, inv = factor(last)
    value = scaled(inv, forward(low, right))
    for i in (2, 1, 0):
        for k in range(i + 1, 4):
            value[i] = value[i] - low[(k, i)] * value[k]
    return value


def corner_sums(g, r):
    k = [
        g[(3, 3)],
        g[(2, 3)] - g[(3, 3)],
        g[(1, 3)] - g[(3, 3)],
        g[(0, 3)] - g[(1, 3)] - g[(2, 3)] + g[(3, 3)],
        g[(2, 2)] - 2.0 * g[(2, 3)] + g[(3, 3)],
        g[(1, 2)] - g[(1, 3)] - g[(2, 3)] + g[(3, 3)],
        (g[(0, 2)] - g[(1, 2)] - g[(2, 2)]) + (2.0 * g[(2, 3)] - g[(0, 3)] + g[(1, 3)] - g[(3, 3)]),
        g[(1, 1)] - 2.0 * g[(1, 3)] + g[(3, 3)],
        (g[(0, 1)] - g[(1, 1)] - g[(1, 2)]) + (2.0 * g[(1, 3)] - g[(0, 3)] + g[(2, 3)] - g[(3, 3)]),
        (g[(0, 0)] + g[(1, 1)] + g[(2, 2)] + g[(3, 3)])
        - 2.0 * (g[(0, 1)] + g[(0, 2)] + g[(1, 3)] + g[(2, 3)] - g[(0, 3)] - g[(1, 2)]),
        r[3],
        r[2] - r[3],
        r[1] - r[3],
        r[0] - r[1] - r[2] + r[3],
    ]
    return k


GRAM = ((0, 0), (0, 1), (0, 2), (0, 3), (1, 1), (1, 2), (1, 3), (2, 2), (2, 3), (3, 3))


def assemble(t, slot):
    def back(value):
        return node_shift(value, -1, slot)

    b, d = {}, []
    c = [[None] * 4 for _ in range(4)]
    for i in range(4):
        w = (i - 1) % 4
        b[(i, i)] = t[0][i] + t[4][w] + back(t[7][i] + t[9][w])
        d.append(t[10][i] + t[11][w] + back(t[12][i] + t[13][w]))
        edge = t[1][i] + back(t[8][i])
        e = (i + 1) % 4
        b[(max(i, e), min(i, e))] = edge
        c[i][i] = t[2][i] + t[6][w]
        c[i][e] = t[3][i]
        c[e][i] = t[5][i]
    b[(2, 0)] = None
    b[(3, 1)] = None
    return b, c, d


def kernel(
    perm, accum, source, vtrans, press_out, resid_out,
    hx, ax, sx, vt, row24, row8, lo_out, hi_out, lo_n, lo_ne0, lo_ne1, lo_nw, hi_s, hi_se, hi_sw,
    tp, first_rows, ta, ts, teq, tnq, bq, tew, tnw, bw, tem, tnm, co, wt, sums, ga, nodes, cb, pu, ends, pm, hm, yp, yh, po, ro,
    up_layer, down_pair, ready,
    local_sem, send_sem, recv_sem, gsend_sem, grecv_sem, vsend_sem, vrecv_sem, out_sem,
):
    gx, gy, gz = lax.axis_index("gx"), lax.axis_index("gy"), lax.axis_index("gz")

    def peer(dx, dy, dz):
        return (
            lax.rem(gx + (dx + SIDE), SIDE),
            lax.rem(gy + (dy + SIDE), SIDE),
            lax.rem(gz + (dz + DEPTH), DEPTH),
        )

    has_below, has_above = gz > 0, gz < DEPTH - 1
    first_to_above = has_above & (gz != MIDDLE - 1)
    first_to_below = gz == MIDDLE
    next_to_above = gz == MIDDLE - 1
    next_to_below = has_below & (gz != MIDDLE)
    barrier = pltpu.get_barrier_semaphore()
    for dx in range(SIDE):
        for dy in range(SIDE):
            if dx or dy:
                pl.semaphore_signal(barrier, inc=1, device_id=peer(dx, dy, 0), device_id_type=MESH)
    for dz, there in ((-1, first_to_below), (1, first_to_above)):

        @pl.when(there)
        def _():
            pl.semaphore_signal(barrier, inc=1, device_id=peer(0, 0, dz), device_id_type=MESH)

    local = []

    def load(src, dst):
        copy = pltpu.make_async_copy(src, dst, local_sem.at[len(local)])
        copy.start()
        local.append(copy)

    for src, dst, first in ((perm, hx, 1), (accum, ax, 0), (source, sx, 0)):
        for half in range(2):
            load(src.at[pl.ds(24, 8), half], dst.at[first + half, pl.ds(0, 8)])
            load(src.at[pl.ds(0, 24), half], dst.at[first + half, pl.ds(8, 24)])
    load(vtrans, vt)

    row = lax.broadcasted_iota(jnp.int32, (8, 128), 0)
    lane = lax.broadcasted_iota(jnp.int32, (8, 128), 1)
    group = lane // 16
    slot_of = lane // 32
    lower = lane < 64
    u_base = jnp.where(group % 2 == 1, 8, 0)
    row0 = row == 0
    row7 = row == 7
    u0 = u_base == 0
    u8 = u_base == 8

    for x in range(8):
        for p in range(2):
            w_x = 1.0 - (u_base + x).astype(F32) / 16.0
            w_y = 1.0 - (2 * row + p).astype(F32) / 16.0
            wt[0, x, p] = w_x
            wt[1, x, p] = w_y
            wt[2, x, p] = w_x * w_y

    hx_rows = hx.reshape(4 * 256, 128)
    ax_rows = ax.reshape(3 * 256, 128)
    sx_rows = sx.reshape(3 * 256, 128)

    def edges(rows, base, at_row, depth, with_high):
        for s in range(SETS):
            for half in range(2):
                first = base + 256 * half + 128 * s
                turned = jnp.concatenate([rows[pl.ds(first + x, 16, stride=8), :] for x in range(8)], axis=0).T
                lo_out[s, half, pl.ds(at_row, depth), :] = turned[:depth]
                if with_high:
                    hi_out[s, half] = turned[120:]

    for copy in local[:4]:
        copy.wait()
    row8[...] = hx_rows[pl.ds(512, LAYERS, stride=8), :]
    pl.semaphore_wait(barrier, 15 + next_to_above.astype(jnp.int32) + next_to_below.astype(jnp.int32))

    west, east = peer(-1, 0, 0), peer(1, 0, 0)
    south, north = peer(0, -1, 0), peer(0, 1, 0)

    def halo(s, first=0, end=12):
        mine = pl.ds(16 * s, 16)
        routes = (
            (hx.at[1, mine], hx.at[3, mine], west),
            (row8.at[mine], row24.at[mine], west),
            (lo_out.at[s], lo_n.at[s], south),
            (lo_out.at[s, 0], lo_ne0.at[s], peer(-1, -1, 0)),
            (lo_out.at[s, 1, pl.ds(0, 16)], lo_ne1.at[s], peer(-1, -1, 0)),
            (ax.at[0, mine], ax.at[2, mine], west),
            (sx.at[0, mine], sx.at[2, mine], west),
            (hx.at[2, mine], hx.at[0, mine], east),
            (lo_out.at[s, 1, pl.ds(0, 16)], lo_nw.at[s], peer(1, -1, 0)),
            (hi_out.at[s], hi_s.at[s], north),
            (hi_out.at[s], hi_se.at[s], peer(-1, 1, 0)),
            (hi_out.at[s, 1], hi_sw.at[s], peer(1, 1, 0)),
        )
        return [
            pltpu.make_async_remote_copy(
                src_ref=src, dst_ref=dst, send_sem=send_sem.at[s, i], recv_sem=recv_sem.at[s, i],
                device_id=target, device_id_type=MESH,
            )
            for i, (src, dst, target) in enumerate(routes)
            if first <= i < end
        ]

    def sums_messages(s):
        copies = []
        for dx in range(SIDE):
            for dy in range(SIDE):
                if dx or dy:
                    slot = (-dx % SIDE) * SIDE + (-dy % SIDE)
                    copies.append(
                        pltpu.make_async_remote_copy(
                            src_ref=ga.at[s, 0], dst_ref=ga.at[s, slot],
                            send_sem=gsend_sem.at[s, slot], recv_sem=grecv_sem.at[s, slot],
                            device_id=peer(dx, dy, 0), device_id_type=MESH,
                        )
                    )
        return copies

    for copy in halo(0, 0, 2):
        copy.start()
    for copy in local[4:]:
        copy.wait()
    for copy in halo(0, 5, 7):
        copy.start()
    edges(hx_rows, 256, 0, 16, True)
    edges(ax_rows, 0, 16, 8, False)
    edges(sx_rows, 0, 24, 8, False)
    for copy in halo(0, 2, 5):
        copy.start()
    for dz, at, there in ((-1, 0, next_to_below), (1, 1, next_to_above)):

        @pl.when(there)
        def _():
            pl.semaphore_signal(ready.at[at], inc=1, device_id=peer(0, 0, dz), device_id_type=MESH)

    def pick(at_group, left, by_left, right, by_right):
        return jnp.where(group == at_group, lane_roll(left, by_left), lane_roll(right, by_right))

    def turn(rows, first, second, fixed=None):
        part = [rows[pl.ds(first, 16, stride=8), :]]
        part.append(fixed if fixed is not None else rows[pl.ds(second, 16, stride=8), :])
        return jnp.concatenate(part * 4, axis=0).T

    def by_slot(load_slot):
        value = load_slot(3)
        for slot in (2, 1, 0):
            value = jnp.where(slot_of == slot, load_slot(slot), value)
        return value

    def relax(most, last, at, step, put_t, put_b):
        def cell(x, off):
            return by_slot(
                lambda slot: tp[last if slot == 3 else most, x, pl.ds(at + step * slot + off, 8, stride=2), :]
            )

        cells = [[cell(x, p) for p in range(2)] for x in range(9)]
        t_e = [[harmonic(cells[x][p], cells[x + 1][p]) for p in range(2)] for x in range(8)]
        for x in range(8):
            t_n = [harmonic(cells[x][0], cells[x][1]), harmonic(cells[x][1], cell(x, 2))]
            t_s = [sub_roll(t_n[1], 1), t_n[0]]
            for p in range(2):
                t_w = t_e[x - 1][p] if x else lane_roll(t_e[7][p], 1)
                put_t(x, p, t_e[x][p], t_n[p])
                inv = inverse((t_w + t_e[x][p]) + (t_s[p] + t_n[p]))
                if p == 0 and x == 0:
                    inv = jnp.where(row0 | u0, 0.0, inv)
                elif p == 0:
                    inv = jnp.where(row0, 0.0, inv)
                elif x == 0:
                    inv = jnp.where(u0, 0.0, inv)
                co[0, x, p] = t_w * inv
                co[1, x, p] = t_e[x][p] * inv
                co[2, x, p] = t_s[p] * inv
                co[3, x, p] = t_n[p] * inv

        def sweep(kinds):
            new = [[[None, None] for _ in range(8)] for _ in kinds]
            for x in (0, 7, 1, 6, 2, 5, 3, 4):
                for p in range(2):
                    c_w, c_e, c_s, c_n = (co[i, x, p] for i in range(4))
                    for vals, out in zip(kinds, new):
                        west_v = vals[x - 1][p] if x else lane_roll(vals[7][p], 1)
                        east_v = vals[x + 1][p] if x < 7 else lane_roll(vals[0][p], -1)
                        south_v = vals[x][0] if p else sub_roll(vals[x][1], 1)
                        north_v = sub_roll(vals[x][0], -1) if p else vals[x][1]
                        out[x][p] = (c_w * west_v + c_e * east_v) + (c_s * south_v + c_n * north_v)
            return new

        def plus(left, right):
            return [[[a[x][p] + b[x][p] for p in range(2)] for x in range(8)] for a, b in zip(left, right)]

        for kinds in ((0, 1, 2),):
            push = []
            for kind in kinds:
                push.append([[None, None] for _ in range(8)])
                for x in range(8):
                    for p in range(2):
                        w_x, w_y = wt[0, x, p], wt[1, x, p]
                        if kind == LX:
                            value = co[0, x, p] - co[1, x, p]
                        elif kind == LY:
                            value = co[2, x, p] - co[3, x, p]
                        else:
                            value = (co[0, x, p] - co[1, x, p]) * w_y + (co[2, x, p] - co[3, x, p]) * w_x
                        push[-1][x][p] = value
            vals = plus(push, sweep(push))
            vals = plus(vals, sweep(sweep(vals)))
            vals = plus(vals, sweep(sweep(sweep(sweep(vals)))))
            for kind, done in zip(kinds, vals):
                for x in range(8):
                    for p in range(2):
                        put_b(kind, x, p, wt[kind, x, p] + done[x][p] * (1.0 / 16.0))

    def gram(s, e):
        at = 8 + 64 * e

        def load_packed(ref, x, p):
            return by_slot(lambda slot: ref[x, pl.ds(at + 16 * slot + p, 8, stride=2), :])

        acc = {}

        def add(key, value):
            acc[key] = value if key not in acc else acc[key] + value

        for x in range(8):
            for p in range(2):
                a = load_packed(ta, x, p)
                src = load_packed(ts, x, p)
                here = [bq[s, kind, e, x, p] for kind in range(3)]
                t_e, t_n = teq[s, e, x, p], tnq[s, e, x, p]
                mass, d_e, d_n = [], [], []
                for kind in range(3):
                    if x < 7:
                        east_v = bq[s, kind, e, x + 1, p]
                    else:
                        east_v = lane_roll(bq[s, kind, e, 0, p], -1)
                        if kind != LY:
                            east_v = jnp.where(u8, 0.0, east_v)
                    if p:
                        north_v = sub_roll(bq[s, kind, e, x, 0], -1)
                        if kind != LX:
                            north_v = jnp.where(row7, 0.0, north_v)
                    else:
                        north_v = bq[s, kind, e, x, 1]
                    d_e.append(here[kind] - east_v)
                    d_n.append(here[kind] - north_v)
                    mass.append(a * here[kind])
                add((0, 0), a)
                add("r0", src)
                for kind in range(3):
                    add((0, kind + 1), mass[kind])
                    add("r" + str(kind + 1), src * here[kind])
                    w_e, w_n = t_e * d_e[kind], t_n * d_n[kind]
                    for other in range(kind, 3):
                        add((kind + 1, other + 1), mass[kind] * here[other] + w_e * d_e[other] + w_n * d_n[other])
        for index, key in enumerate(GRAM + ("r0", "r1", "r2", "r3")):
            value = acc[key]
            value = value + sub_roll(value, 4)
            value = value + sub_roll(value, 2)
            value = value + sub_roll(value, 1)
            sums[e, index] = value + lane_roll(value, -1)

    def owned(s, carry):
        copies = halo(s, 0, 7)
        copies[0].wait_recv()
        copies[1].wait_recv()

        @pl.when(s == 0)
        def _():
            for copy in halo(1, 0, 7) + halo(0, 7):
                copy.start()

        @pl.when(s == 1)
        def _():
            for copy in halo(1, 7):
                copy.start()

        for x in range(9):
            if x < 8:
                value = turn(hx_rows, 512 + 128 * s + x, 768 + 128 * s + x)
            else:
                value = turn(hx_rows, 768 + 128 * s, None, row24[pl.ds(pl.multiple_of(16 * s, 16), 16), :])
            tp[1, x, pl.ds(8, 128), :] = value
            first_rows[s, x] = value[:16]
        for copy in copies[2:5]:
            copy.wait_recv()
        for t in range(2):
            at = pl.ds(8 * t, 8)
            for x in range(8):
                tp[1, x, pl.ds(136 + 8 * t, 8), :] = pick(6, lo_n[s, 1, at, :], 6 - x, lo_ne0[s, at, :], 7 - x)
            tp[1, 8, pl.ds(136 + 8 * t, 8), :] = pick(6, lo_ne0[s, at, :], 6, lo_ne1[s, at, :], 7)

        def unit(e, inner):
            def put_t(x, p, east_t, north_t):
                teq[s, e, x, p] = east_t
                tnq[s, e, x, p] = north_t

            def put_b(kind, x, p, value):
                bq[s, kind, e, x, p] = value

            relax(1, 1, 16 + 64 * e, 16, put_t, put_b)
            return inner

        lax.fori_loop(0, 2, unit, 0)

        copies[5].wait_recv()
        copies[6].wait_recv()
        for rows, turned, at_row in ((ax_rows, ta, 16), (sx_rows, ts, 24)):
            for x in range(8):
                turned[x, pl.ds(0, 128), :] = turn(rows, 256 + 128 * s + x, 512 + 128 * s + x)
                at = pl.ds(at_row, 8)
                turned[x, pl.ds(128, 8), :] = pick(6, lo_n[s, 1, at, :], 6 - x, lo_ne0[s, at, :], 7 - x)

        def one(e, inner):
            gram(s, e)
            return inner

        lax.fori_loop(0, 2, one, 0)

        whole = []
        for index in range(14):
            whole.append(jnp.where(row % 2 == 0, sums[0, index], sums[1, index]))
        entries = corner_sums({key: whole[i] for i, key in enumerate(GRAM)}, whole[10:])
        for m in range(2):
            packed = jnp.zeros((8, 128), F32)
            for t in range(4 * m, min(4 * m + 4, 7)):
                pair = jnp.where(group % 2 == 0, entries[2 * t], lane_roll(entries[2 * t + 1], 1))
                packed = jnp.where(row // 2 == t % 4, pair, packed)
            ga[s, 0, m] = packed
        for copy in sums_messages(s):
            copy.start()
        return carry

    lax.fori_loop(0, SETS, owned, 0)

    even = group % 2 == 0
    even_slot = slot_of % 2 == 0

    def to_rows(s, tiles, lines, dst):
        for part in range(2):
            for p in range(2):
                for e in range(2):
                    a = [tiles[e, 4 * part + q, p] for q in range(4)]
                    b = [None] * 4
                    for q in range(2):
                        crossed = lane_roll(jnp.where(lower, a[q + 2], a[q]), 4)
                        b[q] = jnp.where(lower, a[q], crossed)
                        b[q + 2] = jnp.where(lower, crossed, a[q + 2])
                    for q in (0, 2):
                        for slot, value in (
                            (q, jnp.where(even_slot, b[q], lane_roll(b[q + 1], 2))),
                            (q + 1, jnp.where(even_slot, lane_roll(b[q], -2), b[q + 1])),
                        ):
                            lines[part, pl.ds(16 * (1 + 4 * e + slot) + p, 8, stride=2), :] = value
                value = tiles[2, 4 * part + 3, p]
                for q in range(3):
                    value = jnp.where(slot_of == q, lane_roll(tiles[2, 4 * part + q, p], 2 * (q - 3)), value)
                lines[part, pl.ds(p, 8, stride=2), :] = value
        for part in range(2):
            turned = lines[part, pl.ds(8, 128), :].T
            for q in range(4):
                for half in range(2):
                    for b in range(2):
                        first = 32 * q + 16 * (1 - half) + 8 * b
                        layer = lax.rem(16 * s + (8 * b + 24), LAYERS)
                        dst[pl.ds(16 * layer + (8 * half + 4 * part + q), 8, stride=16), :] = turned[first : first + 8]

    low_send = pltpu.make_async_remote_copy(
        src_ref=po.at[pl.ds(0, 16)], dst_ref=up_layer, send_sem=vsend_sem.at[0], recv_sem=vrecv_sem.at[0],
        device_id=peer(0, 0, -1), device_id_type=MESH,
    )
    high_send = pltpu.make_async_remote_copy(
        src_ref=po.at[pl.ds(496, 16)], dst_ref=down_pair.at[0], send_sem=vsend_sem.at[1], recv_sem=vrecv_sem.at[1],
        device_id=peer(0, 0, 1), device_id_type=MESH,
    )
    vt_up = pltpu.make_async_remote_copy(
        src_ref=vt.at[pl.ds(496, 16)], dst_ref=down_pair.at[1], send_sem=vsend_sem.at[2], recv_sem=vrecv_sem.at[2],
        device_id=peer(0, 0, 1), device_id_type=MESH,
    )

    def rest(s, carry):
        for copy in halo(s, 7):
            copy.wait_recv()
        for x in range(9):
            if x < 8:
                value = turn(hx_rows, 128 * s + x, 256 + 128 * s + x)
            else:
                value = turn(hx_rows, 256 + 128 * s, 512 + 128 * s)
            tp[0, x, pl.ds(8, 128), :] = value
            tp[1, x, pl.ds(8, 16), :] = first_rows[s, x]
        for x in range(8):
            for t in range(2):
                at = pl.ds(8 * t, 8)
                tp[0, x, pl.ds(136 + 8 * t, 8), :] = pick(6, lo_nw[s, at, :], 6 - x, lo_n[s, 0, at, :], 7 - x)
            tp[0, x, pl.ds(0, 8), :] = pick(4, hi_sw[s], 4 - x, hi_s[s, 0], 5 - x)
            tp[1, x, pl.ds(0, 8), :] = pick(6, hi_s[s, 1], 6 - x, hi_se[s, 0], 7 - x)
        for t in range(2):
            at = pl.ds(8 * t, 8)
            tp[0, 8, pl.ds(136 + 8 * t, 8), :] = pick(6, lo_n[s, 0, at, :], 6, lo_n[s, 1, at, :], 7)
        tp[0, 8, pl.ds(0, 8), :] = pick(4, hi_s[s, 0], 4, hi_s[s, 1], 5)
        tp[1, 8, pl.ds(0, 8), :] = pick(6, hi_se[s, 0], 6, hi_se[s, 1], 7)

        def unit(e, inner):
            edge = e // 2

            def put_t(x, p, east_t, north_t):
                tew[e, x, p] = east_t
                tnw[e, x, p] = north_t

            def put_b(kind, x, p, value):
                bw[kind, e, x, p] = value

            relax(0, edge, (16 + 64 * e) * (1 - edge), 16 * (1 - edge), put_t, put_b)
            return inner

        lax.fori_loop(0, 3, unit, 0)
        for copy in sums_messages(s):
            copy.wait()
        table = []
        for t in range(7):
            pair = ([], [])
            for i in range(SIDE):
                value = None
                for g in range(SIDE):
                    moved = sub_roll(ga[s, i * SIDE + g, t // 4], 2 * g - 2 * (t % 4))
                    value = moved if value is None else jnp.where(row // 2 == g, moved, value)
                pair[0].append(jnp.where(group % 2 == 0, value, lane_roll(value, 1)))
                pair[1].append(jnp.where(group % 2 == 1, value, lane_roll(value, -1)))
            table.append(pair[0])
            table.append(pair[1])
        b, c, d_side = assemble(table, slot_of)
        coarse = solve_nodes(b, c, d_side, slot_of)

        for place, i in enumerate((3, 0, 1)):
            nodes[0, place] = coarse[i]
            nodes[1, place] = node_shift(coarse[i], 1, slot_of)

        def line(by, place, j):
            return jnp.broadcast_to(nodes[by, place, pl.ds(j, 1), :], (8, 128))

        def put_weights(unit_at, c0, c1, c2, c3):
            cb[unit_at, 0] = c3
            cb[unit_at, 1] = c2 - c3
            cb[unit_at, 2] = c1 - c3
            cb[unit_at, 3] = (c0 - c1) - (c2 - c3)

        for e in range(2):
            near = [line(0, place, e) for place in range(3)]
            far = [line(1, place, e) for place in range(3)]
            put_weights(e, near[1], near[2], far[1], far[2])
            put_weights(2 + e, near[0], near[1], far[0], far[1])
        last = slot_of == 3
        below = [line(0, place, 7) for place in range(3)]
        first = [line(0, place, 0) for place in range(3)]
        put_weights(
            4,
            *(jnp.where(last, below[k + 1], lane_roll(below[k], -2)) for k in range(2)),
            *(jnp.where(last, lane_roll(first[k + 1], 6), lane_roll(first[k], 4)) for k in range(2)),
        )

        def pressures(w, basis_at, x, p):
            return (w[0] + w[1] * basis_at(0, x, p)) + (w[2] * basis_at(1, x, p) + w[3] * basis_at(2, x, p))

        def put_ends(k, east_0, west_7, west_0, t_west_7, p, by):
            ends[k, 0, p] = jnp.where(even, lane_roll(east_0, -1), lane_roll(east_0, 1))
            ends[k, 1, p] = lane_roll(t_west_7 * (west_7 - lane_roll(west_0, -1)), by)

        def interpolate(e, inner):
            w_own = [cb[e, k] for k in range(4)]
            w_west = [cb[2 + e, k] for k in range(4)]
            w_both = [jnp.where(even, a, b) for a, b in zip(w_own, w_west)]

            def own(kind, x, p):
                return bq[s, kind, e, x, p]

            def other(kind, x, p):
                return bw[kind, e, x, p]

            def both(kind, x, p):
                return jnp.where(even, bq[s, kind, e, x, p], bw[kind, e, x, p])

            for p in range(2):
                for x in range(8):
                    pm[e, x, p] = pressures(w_both, both, x, p)
                    tem[e, x, p] = jnp.where(even, teq[s, e, x, p], tew[e, x, p])
                    tnm[e, x, p] = jnp.where(even, tnq[s, e, x, p], tnw[e, x, p])
                put_ends(
                    e, pressures(w_own, own, 0, p), pressures(w_west, other, 7, p),
                    pressures(w_west, other, 0, p), tew[e, 7, p], p, 1,
                )
            return inner

        lax.fori_loop(0, 2, interpolate, 0)
        w_edge = [cb[4, k] for k in range(4)]

        def to_own(value):
            return jnp.where(even, value, lane_roll(value, 2))

        for p in range(2):
            edge = [pressures(w_edge, lambda kind, x, p: bw[kind, 2, x, p], x, p) for x in range(8)]
            for x in range(8):
                pm[2, x, p] = to_own(edge[x])
                tem[2, x, p] = to_own(tew[2, x, p])
                tnm[2, x, p] = to_own(tnw[2, x, p])
            put_ends(2, edge[0], edge[7], edge[0], tew[2, 7, p], p, 3)
        to_rows(s, pm, yp, po)

        @pl.when((s == 0) & first_to_above)
        def _():
            pl.semaphore_wait(ready.at[0], 1)

        @pl.when((s == 0) & has_above)
        def _():
            high_send.start()
            vt_up.start()

        @pl.when((s == 0) & first_to_below)
        def _():
            pl.semaphore_wait(ready.at[1], 1)

        @pl.when((s == 0) & has_below)
        def _():
            low_send.start()

        def balance(i, inner):
            k = lax.rem(i + 2, 3)
            val = [[pm[k, x, p] for p in range(2)] for x in range(8)]
            f_e = [[None, None] for _ in range(8)]
            for x in range(8):
                for p in range(2):
                    east_v = val[x + 1][p] if x < 7 else ends[k, 0, p]
                    f_e[x][p] = tem[k, x, p] * (val[x][p] - east_v)
            for x in range(8):
                after = lane_roll(jnp.where(slot_of == 0, pm[i, x, 0], val[x][0]), -2)
                after = sub_roll(jnp.where(row0, after, val[x][0]), -1)
                f_n0 = tnm[k, x, 0] * (val[x][0] - val[x][1])
                f_n1 = tnm[k, x, 1] * (val[x][1] - after)
                before = lane_roll(jnp.where(slot_of == 3, pu[x], f_n1), 2)
                before = sub_roll(jnp.where(row7, before, f_n1), 1)
                pu[x] = f_n1
                f_n = (f_n0, f_n1)
                f_s = (before, f_n0)
                for p in range(2):
                    f_w = f_e[x - 1][p] if x else jnp.where(even, lane_roll(f_e[7][p], -1), ends[k, 1, p])
                    hm[k, x, p] = (f_e[x][p] - f_w) + (f_n[p] - f_s[p])
            return inner

        lax.fori_loop(0, 3, balance, 0)
        to_rows(s, hm, yh, ro)
        return carry

    lax.fori_loop(0, SETS, rest, 0)
    press_copy = pltpu.make_async_copy(po, press_out, out_sem.at[0])
    press_copy.start()

    for half in range(2):
        before = None
        for l in range(LAYERS):
            at = pl.ds(16 * l + 8 * half, 8)
            place = (l + 8) % LAYERS
            here = po[at, :]
            value = sx[half, place] - ax[half, place] * here - ro[at, :]
            if before is not None:
                value = value + before
            if l < LAYERS - 1:
                before = vt[at, :] * (here - po[pl.ds(16 * (l + 1) + 8 * half, 8), :])
                value = value - before
            ro[at, :] = value

    middle_copy = pltpu.make_async_copy(ro.at[pl.ds(16, 480)], resid_out.at[pl.ds(16, 480)], out_sem.at[1])
    middle_copy.start()
    for s in range(SETS):
        for copy in halo(s):
            copy.wait_send()
    press_copy.wait()

    @pl.when(has_below)
    def _():
        vt_up.wait_recv()
        high_send.wait_recv()
        low_send.wait_send()

    @pl.when(has_above)
    def _():
        low_send.wait_recv()
        high_send.wait_send()
        vt_up.wait_send()

    above = jnp.where(has_above, vt[pl.ds(496, 16), :] * (po[pl.ds(496, 16), :] - up_layer[...]), 0.0)
    below = jnp.where(has_below, down_pair[1] * (down_pair[0] - po[pl.ds(0, 16), :]), 0.0)
    ro[pl.ds(496, 16), :] = ro[pl.ds(496, 16), :] - above
    ro[pl.ds(0, 16), :] = ro[pl.ds(0, 16), :] + below
    edge_copies = [
        pltpu.make_async_copy(ro.at[pl.ds(at, 16)], resid_out.at[pl.ds(at, 16)], out_sem.at[2 + i])
        for i, at in enumerate((0, 496))
    ]
    for copy in edge_copies:
        copy.start()
    middle_copy.wait()
    for copy in edge_copies:
        copy.wait()


def flush(press, resid, press_out, resid_out, sem):
    copies = [
        pltpu.make_async_copy(press, press_out, sem.at[0]),
        pltpu.make_async_copy(resid, resid_out, sem.at[1]),
    ]
    for copy in copies:
        copy.start()
    for copy in copies:
        copy.wait()


def body(permeability, accumulation, source_term, vertical_trans):
    split = (LAYERS, 2, 8, 128)
    vmem = lambda *shape: pltpu.VMEM(shape, F32)
    anywhere = pl.BlockSpec(memory_space=pl.ANY)
    in_hbm = pl.BlockSpec(memory_space=pltpu.HBM)
    pressure, residual = pl.pallas_call(
        kernel,
        out_shape=[jax.ShapeDtypeStruct((512, 128), F32)] * 2,
        in_specs=[in_hbm] * 4,
        out_specs=[anywhere] * 2,
        scratch_shapes=[
            vmem(4, 32, 8, 128),
            vmem(3, 32, 8, 128),
            vmem(3, 32, 8, 128),
            vmem(512, 128),
            vmem(32, 128),
            vmem(32, 128),
            vmem(2, 2, 32, 128),
            vmem(2, 2, 8, 128),
            vmem(2, 2, 32, 128),
            vmem(2, 32, 128),
            vmem(2, 16, 128),
            vmem(2, 16, 128),
            vmem(2, 2, 8, 128),
            vmem(2, 2, 8, 128),
            vmem(2, 8, 128),
            vmem(2, 9, 152, 128),
            vmem(2, 9, 16, 128),
            vmem(8, 136, 128),
            vmem(8, 136, 128),
            vmem(2, 2, 8, 2, 8, 128),
            vmem(2, 2, 8, 2, 8, 128),
            vmem(2, 3, 2, 8, 2, 8, 128),
            vmem(3, 8, 2, 8, 128),
            vmem(3, 8, 2, 8, 128),
            vmem(3, 3, 8, 2, 8, 128),
            vmem(3, 8, 2, 8, 128),
            vmem(3, 8, 2, 8, 128),
            vmem(4, 8, 2, 8, 128),
            vmem(3, 8, 2, 8, 128),
            vmem(2, 14, 8, 128),
            vmem(2, 16, 2, 8, 128),
            vmem(2, 3, 8, 128),
            vmem(5, 4, 8, 128),
            vmem(8, 8, 128),
            vmem(3, 2, 2, 8, 128),
            vmem(3, 8, 2, 8, 128),
            vmem(3, 8, 2, 8, 128),
            vmem(2, 144, 128),
            vmem(2, 144, 128),
            vmem(512, 128),
            vmem(512, 128),
            vmem(16, 128),
            vmem(2, 16, 128),
            pltpu.SemaphoreType.REGULAR((2,)),
            pltpu.SemaphoreType.DMA((13,)),
            pltpu.SemaphoreType.DMA((2, 12)),
            pltpu.SemaphoreType.DMA((2, 12)),
            pltpu.SemaphoreType.DMA((2, 16)),
            pltpu.SemaphoreType.DMA((2, 16)),
            pltpu.SemaphoreType.DMA((3,)),
            pltpu.SemaphoreType.DMA((3,)),
            pltpu.SemaphoreType.DMA((4,)),
        ],
        compiler_params=pltpu.CompilerParams(
            collective_id=0, has_side_effects=True, vmem_limit_bytes=40 * 1024 * 1024
        ),
    )(
        *(
            pltpu.with_memory_space_constraint(value, pltpu.HBM)
            for value in (
                permeability.reshape(split),
                accumulation.reshape(split),
                source_term.reshape(split),
                vertical_trans.reshape(512, 128),
            )
        ),
    )
    pressure, residual = pl.pallas_call(
        flush,
        out_shape=[jax.ShapeDtypeStruct((512, 128), F32)] * 2,
        in_specs=[anywhere] * 2,
        out_specs=[anywhere] * 2,
        scratch_shapes=[pltpu.SemaphoreType.DMA((2,))],
        compiler_params=pltpu.CompilerParams(vmem_limit_bytes=1024 * 1024),
    )(pressure, residual)
    return pressure.reshape(32, 16, 128), residual.reshape(32, 16, 128)


def solution(mesh):
    spec = P("gz", "gx", "gy")
    return jax.shard_map(
        body, mesh=mesh, in_specs=(spec,) * 4, out_specs=(spec, spec), check_vma=False
    )
```

```python
import jax
import jax.numpy as jnp
from jax import lax
from jax.experimental import pallas as pl
from jax.experimental.pallas import tpu as pltpu
from jax.sharding import PartitionSpec as P

LAYERS = 32
SETS = 2
SIDE = 4
DEPTH = 16
MIDDLE = DEPTH // 2
DUALS = 9
MESH = pl.DeviceIdType.MESH
F32 = jnp.float32
LX, LY = 0, 1


def lane_roll(value, groups):
    by = (groups * 16) % 128
    return value if by == 0 else pltpu.roll(value, by, axis=1)


def sub_roll(value, by):
    return pltpu.roll(value, by % 8, axis=0)


def inverse(value, rounds=1):
    guess = pl.reciprocal(value, approx=True)
    for _ in range(rounds):
        guess = guess * (2.0 - value * guess)
    return guess


def harmonic(left, right):
    return 2.0 * left * right * inverse(left + right)


def node_shift(value, by, slot):
    if by % 4 == 0:
        return sub_roll(value, -(by // 4))
    turned = lane_roll(value, -2 * by)
    if by > 0:
        return jnp.where(slot < 4 - by, turned, sub_roll(turned, -1))
    return jnp.where(slot >= -by, turned, sub_roll(turned, 1))


def factor(b):
    low = {}
    inv = [None] * 4
    for k in range(4):
        pivot = b[(k, k)]
        for m in range(k):
            if low.get((k, m)) is not None:
                pivot = pivot - low[(k, m)] * work[(k, m)]
        inv[k] = inverse(pivot, 2)
        if k == 0:
            work = {}
        for i in range(k + 1, 4):
            entry = b[(i, k)]
            for m in range(k):
                if low.get((i, m)) is None or work.get((k, m)) is None:
                    continue
                term = low[(i, m)] * work[(k, m)]
                entry = -term if entry is None else entry - term
            work[(i, k)] = entry
            low[(i, k)] = None if entry is None else entry * inv[k]
    return low, inv


def forward(low, column):
    out = []
    for i in range(4):
        value = column[i]
        for m in range(i):
            if low[(i, m)] is not None and out[m] is not None:
                term = low[(i, m)] * out[m]
                value = -term if value is None else value - term
        out.append(value)
    return out


def scaled(inv, column):
    return [None if v is None else v * inv[k] for k, v in enumerate(column)]


def inner(left, right):
    total = None
    for a, b in zip(left, right):
        if a is None or b is None:
            continue
        total = a * b if total is None else total + a * b
    return total


def subtract(value, term):
    if term is None:
        return value
    return -term if value is None else value - term


def shift_or_none(value, by, slot):
    return None if value is None else node_shift(value, by, slot)


def solve_nodes(b, c, d, slot):
    for step in (1, 2, 4, 8):
        a = [[shift_or_none(c[m][k], -step, slot) for m in range(4)] for k in range(4)]
        low, inv = factor(b)
        up = [forward(low, [c[i][k] for i in range(4)]) for k in range(4)]
        down = [forward(low, [a[i][k] for i in range(4)]) for k in range(4)]
        side = scaled(inv, forward(low, d))
        up_s = [scaled(inv, col) for col in up]
        down_s = [scaled(inv, col) for col in down]
        new_b = {}
        for i in range(4):
            for k in range(i + 1):
                value = subtract(b[(i, k)], shift_or_none(inner(up[i], up_s[k]), -step, slot))
                new_b[(i, k)] = subtract(value, shift_or_none(inner(down[i], down_s[k]), step, slot))
        new_d = []
        for i in range(4):
            value = subtract(d[i], shift_or_none(inner(up[i], side), -step, slot))
            new_d.append(subtract(value, shift_or_none(inner(down[i], side), step, slot)))
        new_c = [
            [subtract(None, shift_or_none(inner(down[i], up_s[k]), step, slot)) for k in range(4)]
            for i in range(4)
        ]
        b, c, d = new_b, new_c, new_d
    both = [[c[i][k] + node_shift(c[k][i], -16, slot) for k in range(4)] for i in range(4)]
    low, inv = factor(b)
    cols = [forward(low, [both[i][k] for i in range(4)]) for k in range(4)]
    cols_s = [scaled(inv, col) for col in cols]
    side = scaled(inv, forward(low, d))
    last = {}
    for i in range(4):
        for k in range(i + 1):
            last[(i, k)] = b[(i, k)] - node_shift(inner(cols[i], cols_s[k]), 16, slot)
    right = [d[i] - node_shift(inner(cols[i], side), 16, slot) for i in range(4)]
    low, inv = factor(last)
    value = scaled(inv, forward(low, right))
    for i in (2, 1, 0):
        for k in range(i + 1, 4):
            value[i] = value[i] - low[(k, i)] * value[k]
    return value


def corner_sums(g, r):
    k = [
        g[(3, 3)],
        g[(2, 3)] - g[(3, 3)],
        g[(1, 3)] - g[(3, 3)],
        g[(0, 3)] - g[(1, 3)] - g[(2, 3)] + g[(3, 3)],
        g[(2, 2)] - 2.0 * g[(2, 3)] + g[(3, 3)],
        g[(1, 2)] - g[(1, 3)] - g[(2, 3)] + g[(3, 3)],
        (g[(0, 2)] - g[(1, 2)] - g[(2, 2)]) + (2.0 * g[(2, 3)] - g[(0, 3)] + g[(1, 3)] - g[(3, 3)]),
        g[(1, 1)] - 2.0 * g[(1, 3)] + g[(3, 3)],
        (g[(0, 1)] - g[(1, 1)] - g[(1, 2)]) + (2.0 * g[(1, 3)] - g[(0, 3)] + g[(2, 3)] - g[(3, 3)]),
        (g[(0, 0)] + g[(1, 1)] + g[(2, 2)] + g[(3, 3)])
        - 2.0 * (g[(0, 1)] + g[(0, 2)] + g[(1, 3)] + g[(2, 3)] - g[(0, 3)] - g[(1, 2)]),
        r[3],
        r[2] - r[3],
        r[1] - r[3],
        r[0] - r[1] - r[2] + r[3],
    ]
    return k


GRAM = ((0, 0), (0, 1), (0, 2), (0, 3), (1, 1), (1, 2), (1, 3), (2, 2), (2, 3), (3, 3))


def assemble(t, slot):
    def back(value):
        return node_shift(value, -1, slot)

    b, d = {}, []
    c = [[None] * 4 for _ in range(4)]
    for i in range(4):
        w = (i - 1) % 4
        b[(i, i)] = t[0][i] + t[4][w] + back(t[7][i] + t[9][w])
        d.append(t[10][i] + t[11][w] + back(t[12][i] + t[13][w]))
        edge = t[1][i] + back(t[8][i])
        e = (i + 1) % 4
        b[(max(i, e), min(i, e))] = edge
        c[i][i] = t[2][i] + t[6][w]
        c[i][e] = t[3][i]
        c[e][i] = t[5][i]
    b[(2, 0)] = None
    b[(3, 1)] = None
    return b, c, d


def kernel(
    perm, accum, source, vtrans, press_out, resid_out,
    hx, ax, sx, vt, row24, row8, lo_out, hi_out, lo_n, lo_ne0, lo_ne1, lo_nw, hi_s, hi_se, hi_sw,
    tp, first_rows, ta, ts, teq, tnq, bq, tew, tnw, bw, tem, tnm, co, wt, sums, ga, nodes, cb, pu, ends, pm, hm, yp, yh, po, ro,
    up_layer, down_pair, ready,
    local_sem, send_sem, recv_sem, gsend_sem, grecv_sem, vsend_sem, vrecv_sem, out_sem,
):
    gx, gy, gz = lax.axis_index("gx"), lax.axis_index("gy"), lax.axis_index("gz")

    def peer(dx, dy, dz):
        return (
            lax.rem(gx + (dx + SIDE), SIDE),
            lax.rem(gy + (dy + SIDE), SIDE),
            lax.rem(gz + (dz + DEPTH), DEPTH),
        )

    has_below, has_above = gz > 0, gz < DEPTH - 1
    first_to_above = has_above & (gz != MIDDLE - 1)
    first_to_below = gz == MIDDLE
    next_to_above = gz == MIDDLE - 1
    next_to_below = has_below & (gz != MIDDLE)
    barrier = pltpu.get_barrier_semaphore()
    for dx in range(SIDE):
        for dy in range(SIDE):
            if dx or dy:
                pl.semaphore_signal(barrier, inc=1, device_id=peer(dx, dy, 0), device_id_type=MESH)
    for dz, there in ((-1, first_to_below), (1, first_to_above)):

        @pl.when(there)
        def _():
            pl.semaphore_signal(barrier, inc=1, device_id=peer(0, 0, dz), device_id_type=MESH)

    local = []

    def load(src, dst):
        copy = pltpu.make_async_copy(src, dst, local_sem.at[len(local)])
        copy.start()
        local.append(copy)

    for src, dst, first in ((perm, hx, 1), (accum, ax, 0), (source, sx, 0)):
        for half in range(2):
            load(src.at[pl.ds(24, 8), half], dst.at[first + half, pl.ds(0, 8)])
            load(src.at[pl.ds(0, 24), half], dst.at[first + half, pl.ds(8, 24)])
    load(vtrans, vt)

    row = lax.broadcasted_iota(jnp.int32, (8, 128), 0)
    lane = lax.broadcasted_iota(jnp.int32, (8, 128), 1)
    group = lane // 16
    slot_of = lane // 32
    lower = lane < 64
    u_base = jnp.where(group % 2 == 1, 8, 0)
    row0 = row == 0
    row7 = row == 7
    u0 = u_base == 0
    u8 = u_base == 8

    for x in range(8):
        for p in range(2):
            w_x = 1.0 - (u_base + x).astype(F32) / 16.0
            w_y = 1.0 - (2 * row + p).astype(F32) / 16.0
            wt[0, x, p] = w_x
            wt[1, x, p] = w_y
            wt[2, x, p] = w_x * w_y

    hx_rows = hx.reshape(4 * 256, 128)
    ax_rows = ax.reshape(3 * 256, 128)
    sx_rows = sx.reshape(3 * 256, 128)

    def edges(rows, base, at_row, depth, with_high):
        for s in range(SETS):
            for half in range(2):
                first = base + 256 * half + 128 * s
                turned = jnp.concatenate([rows[pl.ds(first + x, 16, stride=8), :] for x in range(8)], axis=0).T
                lo_out[s, half, pl.ds(at_row, depth), :] = turned[:depth]
                if with_high:
                    hi_out[s, half] = turned[120:]

    for copy in local[:4]:
        copy.wait()
    row8[...] = hx_rows[pl.ds(512, LAYERS, stride=8), :]
    pl.semaphore_wait(barrier, 15 + next_to_above.astype(jnp.int32) + next_to_below.astype(jnp.int32))

    west, east = peer(-1, 0, 0), peer(1, 0, 0)
    south, north = peer(0, -1, 0), peer(0, 1, 0)

    def halo(s, first=0, end=12):
        mine = pl.ds(16 * s, 16)
        routes = (
            (hx.at[1, mine], hx.at[3, mine], west),
            (row8.at[mine], row24.at[mine], west),
            (lo_out.at[s], lo_n.at[s], south),
            (lo_out.at[s, 0], lo_ne0.at[s], peer(-1, -1, 0)),
            (lo_out.at[s, 1, pl.ds(0, 16)], lo_ne1.at[s], peer(-1, -1, 0)),
            (ax.at[0, mine], ax.at[2, mine], west),
            (sx.at[0, mine], sx.at[2, mine], west),
            (hx.at[2, mine], hx.at[0, mine], east),
            (lo_out.at[s, 1, pl.ds(0, 16)], lo_nw.at[s], peer(1, -1, 0)),
            (hi_out.at[s], hi_s.at[s], north),
            (hi_out.at[s], hi_se.at[s], peer(-1, 1, 0)),
            (hi_out.at[s, 1], hi_sw.at[s], peer(1, 1, 0)),
        )
        return [
            pltpu.make_async_remote_copy(
                src_ref=src, dst_ref=dst, send_sem=send_sem.at[s, i], recv_sem=recv_sem.at[s, i],
                device_id=target, device_id_type=MESH,
            )
            for i, (src, dst, target) in enumerate(routes)
            if first <= i < end
        ]

    def sums_messages(s):
        copies = []
        for dx in range(SIDE):
            for dy in range(SIDE):
                if dx or dy:
                    slot = (-dx % SIDE) * SIDE + (-dy % SIDE)
                    copies.append(
                        pltpu.make_async_remote_copy(
                            src_ref=ga.at[s, 0], dst_ref=ga.at[s, slot],
                            send_sem=gsend_sem.at[s, slot], recv_sem=grecv_sem.at[s, slot],
                            device_id=peer(dx, dy, 0), device_id_type=MESH,
                        )
                    )
        return copies

    for copy in halo(0, 0, 2):
        copy.start()
    for copy in local[4:]:
        copy.wait()
    for copy in halo(0, 5, 7):
        copy.start()
    edges(hx_rows, 256, 0, 16, True)
    edges(ax_rows, 0, 16, 8, False)
    edges(sx_rows, 0, 24, 8, False)
    for copy in halo(0, 2, 5):
        copy.start()
    for dz, at, there in ((-1, 0, next_to_below), (1, 1, next_to_above)):

        @pl.when(there)
        def _():
            pl.semaphore_signal(ready.at[at], inc=1, device_id=peer(0, 0, dz), device_id_type=MESH)

    def pick(at_group, left, by_left, right, by_right):
        return jnp.where(group == at_group, lane_roll(left, by_left), lane_roll(right, by_right))

    def turn(rows, first, second, fixed=None):
        part = [rows[pl.ds(first, 16, stride=8), :]]
        part.append(fixed if fixed is not None else rows[pl.ds(second, 16, stride=8), :])
        return jnp.concatenate(part * 4, axis=0).T

    def by_slot(load_slot):
        value = load_slot(3)
        for slot in (2, 1, 0):
            value = jnp.where(slot_of == slot, load_slot(slot), value)
        return value

    def relax(most, last, at, step, put_t, put_b):
        def cell(x, off):
            return by_slot(
                lambda slot: tp[last if slot == 3 else most, x, pl.ds(at + step * slot + off, 8, stride=2), :]
            )

        cells = [[cell(x, p) for p in range(2)] for x in range(9)]
        t_e = [[harmonic(cells[x][p], cells[x + 1][p]) for p in range(2)] for x in range(8)]
        for x in range(8):
            t_n = [harmonic(cells[x][0], cells[x][1]), harmonic(cells[x][1], cell(x, 2))]
            t_s = [sub_roll(t_n[1], 1), t_n[0]]
            for p in range(2):
                t_w = t_e[x - 1][p] if x else lane_roll(t_e[7][p], 1)
                put_t(x, p, t_e[x][p], t_n[p])
                inv = inverse((t_w + t_e[x][p]) + (t_s[p] + t_n[p]))
                if p == 0 and x == 0:
                    inv = jnp.where(row0 | u0, 0.0, inv)
                elif p == 0:
                    inv = jnp.where(row0, 0.0, inv)
                elif x == 0:
                    inv = jnp.where(u0, 0.0, inv)
                co[0, x, p] = t_w * inv
                co[1, x, p] = t_e[x][p] * inv
                co[2, x, p] = t_s[p] * inv
                co[3, x, p] = t_n[p] * inv

        def sweep(kinds):
            new = [[[None, None] for _ in range(8)] for _ in kinds]
            for x in (0, 7, 1, 6, 2, 5, 3, 4):
                for p in range(2):
                    c_w, c_e, c_s, c_n = (co[i, x, p] for i in range(4))
                    for vals, out in zip(kinds, new):
                        west_v = vals[x - 1][p] if x else lane_roll(vals[7][p], 1)
                        east_v = vals[x + 1][p] if x < 7 else lane_roll(vals[0][p], -1)
                        south_v = vals[x][0] if p else sub_roll(vals[x][1], 1)
                        north_v = sub_roll(vals[x][0], -1) if p else vals[x][1]
                        out[x][p] = (c_w * west_v + c_e * east_v) + (c_s * south_v + c_n * north_v)
            return new

        def plus(left, right):
            return [[[a[x][p] + b[x][p] for p in range(2)] for x in range(8)] for a, b in zip(left, right)]

        for kinds in ((0, 1, 2),):
            push = []
            for kind in kinds:
                push.append([[None, None] for _ in range(8)])
                for x in range(8):
                    for p in range(2):
                        w_x, w_y = wt[0, x, p], wt[1, x, p]
                        if kind == LX:
                            value = co[0, x, p] - co[1, x, p]
                        elif kind == LY:
                            value = co[2, x, p] - co[3, x, p]
                        else:
                            value = (co[0, x, p] - co[1, x, p]) * w_y + (co[2, x, p] - co[3, x, p]) * w_x
                        push[-1][x][p] = value
            vals = plus(push, sweep(push))
            vals = plus(vals, sweep(sweep(vals)))
            vals = plus(vals, sweep(sweep(sweep(sweep(vals)))))
            for kind, done in zip(kinds, vals):
                for x in range(8):
                    for p in range(2):
                        put_b(kind, x, p, wt[kind, x, p] + done[x][p] * (1.0 / 16.0))

    def gram(s, e):
        at = 8 + 64 * e

        def load_packed(ref, x, p):
            return by_slot(lambda slot: ref[x, pl.ds(at + 16 * slot + p, 8, stride=2), :])

        acc = {}

        def add(key, value):
            acc[key] = value if key not in acc else acc[key] + value

        for x in range(8):
            for p in range(2):
                a = load_packed(ta, x, p)
                src = load_packed(ts, x, p)
                here = [bq[s, kind, e, x, p] for kind in range(3)]
                t_e, t_n = teq[s, e, x, p], tnq[s, e, x, p]
                mass, d_e, d_n = [], [], []
                for kind in range(3):
                    if x < 7:
                        east_v = bq[s, kind, e, x + 1, p]
                    else:
                        east_v = lane_roll(bq[s, kind, e, 0, p], -1)
                        if kind != LY:
                            east_v = jnp.where(u8, 0.0, east_v)
                    if p:
                        north_v = sub_roll(bq[s, kind, e, x, 0], -1)
                        if kind != LX:
                            north_v = jnp.where(row7, 0.0, north_v)
                    else:
                        north_v = bq[s, kind, e, x, 1]
                    d_e.append(here[kind] - east_v)
                    d_n.append(here[kind] - north_v)
                    mass.append(a * here[kind])
                add((0, 0), a)
                add("r0", src)
                for kind in range(3):
                    add((0, kind + 1), mass[kind])
                    add("r" + str(kind + 1), src * here[kind])
                    w_e, w_n = t_e * d_e[kind], t_n * d_n[kind]
                    for other in range(kind, 3):
                        add((kind + 1, other + 1), mass[kind] * here[other] + w_e * d_e[other] + w_n * d_n[other])
        for index, key in enumerate(GRAM + ("r0", "r1", "r2", "r3")):
            value = acc[key]
            value = value + sub_roll(value, 4)
            value = value + sub_roll(value, 2)
            value = value + sub_roll(value, 1)
            sums[e, index] = value + lane_roll(value, -1)

    def owned(s):
        copies = halo(s, 0, 7)
        copies[0].wait_recv()
        copies[1].wait_recv()

        @pl.when(s == 0)
        def _():
            for copy in halo(1, 0, 7) + halo(0, 7):
                copy.start()

        @pl.when(s == 1)
        def _():
            for copy in halo(1, 7):
                copy.start()

        for x in range(9):
            if x < 8:
                value = turn(hx_rows, 512 + 128 * s + x, 768 + 128 * s + x)
            else:
                value = turn(hx_rows, 768 + 128 * s, None, row24[pl.ds(16 * s, 16), :])
            tp[1, x, pl.ds(8, 128), :] = value
            first_rows[s, x] = value[:16]
        for copy in copies[2:5]:
            copy.wait_recv()
        for t in range(2):
            at = pl.ds(8 * t, 8)
            for x in range(8):
                tp[1, x, pl.ds(136 + 8 * t, 8), :] = pick(6, lo_n[s, 1, at, :], 6 - x, lo_ne0[s, at, :], 7 - x)
            tp[1, 8, pl.ds(136 + 8 * t, 8), :] = pick(6, lo_ne0[s, at, :], 6, lo_ne1[s, at, :], 7)

        def unit(e, inner):
            def put_t(x, p, east_t, north_t):
                teq[s, e, x, p] = east_t
                tnq[s, e, x, p] = north_t

            def put_b(kind, x, p, value):
                bq[s, kind, e, x, p] = value

            relax(1, 1, 16 + 64 * e, 16, put_t, put_b)
            return inner

        lax.fori_loop(0, 2, unit, 0)

    def coarse_sums(s):
        for copy in halo(s, 5, 7):
            copy.wait_recv()
        for rows, turned, at_row in ((ax_rows, ta, 16), (sx_rows, ts, 24)):
            for x in range(8):
                turned[x, pl.ds(0, 128), :] = turn(rows, 256 + 128 * s + x, 512 + 128 * s + x)
                at = pl.ds(at_row, 8)
                turned[x, pl.ds(128, 8), :] = pick(6, lo_n[s, 1, at, :], 6 - x, lo_ne0[s, at, :], 7 - x)

        def one(e, inner):
            gram(s, e)
            return inner

        lax.fori_loop(0, 2, one, 0)

        whole = []
        for index in range(14):
            whole.append(jnp.where(row % 2 == 0, sums[0, index], sums[1, index]))
        entries = corner_sums({key: whole[i] for i, key in enumerate(GRAM)}, whole[10:])
        for m in range(2):
            packed = jnp.zeros((8, 128), F32)
            for t in range(4 * m, min(4 * m + 4, 7)):
                pair = jnp.where(group % 2 == 0, entries[2 * t], lane_roll(entries[2 * t + 1], 1))
                packed = jnp.where(row // 2 == t % 4, pair, packed)
            ga[s, 0, m] = packed
        for copy in sums_messages(s):
            copy.start()

    even = group % 2 == 0
    even_slot = slot_of % 2 == 0

    def to_rows(s, tiles, lines, dst):
        for part in range(2):
            for p in range(2):
                for e in range(2):
                    a = [tiles[e, 4 * part + q, p] for q in range(4)]
                    b = [None] * 4
                    for q in range(2):
                        crossed = lane_roll(jnp.where(lower, a[q + 2], a[q]), 4)
                        b[q] = jnp.where(lower, a[q], crossed)
                        b[q + 2] = jnp.where(lower, crossed, a[q + 2])
                    for q in (0, 2):
                        for slot, value in (
                            (q, jnp.where(even_slot, b[q], lane_roll(b[q + 1], 2))),
                            (q + 1, jnp.where(even_slot, lane_roll(b[q], -2), b[q + 1])),
                        ):
                            lines[part, pl.ds(16 * (1 + 4 * e + slot) + p, 8, stride=2), :] = value
                value = tiles[2, 4 * part + 3, p]
                for q in range(3):
                    value = jnp.where(slot_of == q, lane_roll(tiles[2, 4 * part + q, p], 2 * (q - 3)), value)
                lines[part, pl.ds(p, 8, stride=2), :] = value
        for part in range(2):
            turned = lines[part, pl.ds(8, 128), :].T
            for q in range(4):
                for half in range(2):
                    for b in range(2):
                        first = 32 * q + 16 * (1 - half) + 8 * b
                        layer = (16 * s + 8 * b + 24) % LAYERS
                        dst[pl.ds(16 * layer + (8 * half + 4 * part + q), 8, stride=16), :] = turned[first : first + 8]

    low_send = pltpu.make_async_remote_copy(
        src_ref=po.at[pl.ds(0, 16)], dst_ref=up_layer, send_sem=vsend_sem.at[0], recv_sem=vrecv_sem.at[0],
        device_id=peer(0, 0, -1), device_id_type=MESH,
    )
    high_send = pltpu.make_async_remote_copy(
        src_ref=po.at[pl.ds(496, 16)], dst_ref=down_pair.at[0], send_sem=vsend_sem.at[1], recv_sem=vrecv_sem.at[1],
        device_id=peer(0, 0, 1), device_id_type=MESH,
    )
    vt_up = pltpu.make_async_remote_copy(
        src_ref=vt.at[pl.ds(496, 16)], dst_ref=down_pair.at[1], send_sem=vsend_sem.at[2], recv_sem=vrecv_sem.at[2],
        device_id=peer(0, 0, 1), device_id_type=MESH,
    )

    def others(s):
        for copy in halo(s, 7):
            copy.wait_recv()
        for x in range(9):
            if x < 8:
                value = turn(hx_rows, 128 * s + x, 256 + 128 * s + x)
            else:
                value = turn(hx_rows, 256 + 128 * s, 512 + 128 * s)
            tp[0, x, pl.ds(8, 128), :] = value
            tp[1, x, pl.ds(8, 16), :] = first_rows[s, x]
        for x in range(8):
            for t in range(2):
                at = pl.ds(8 * t, 8)
                tp[0, x, pl.ds(136 + 8 * t, 8), :] = pick(6, lo_nw[s, at, :], 6 - x, lo_n[s, 0, at, :], 7 - x)
            tp[0, x, pl.ds(0, 8), :] = pick(4, hi_sw[s], 4 - x, hi_s[s, 0], 5 - x)
            tp[1, x, pl.ds(0, 8), :] = pick(6, hi_s[s, 1], 6 - x, hi_se[s, 0], 7 - x)
        for t in range(2):
            at = pl.ds(8 * t, 8)
            tp[0, 8, pl.ds(136 + 8 * t, 8), :] = pick(6, lo_n[s, 0, at, :], 6, lo_n[s, 1, at, :], 7)
        tp[0, 8, pl.ds(0, 8), :] = pick(4, hi_s[s, 0], 4, hi_s[s, 1], 5)
        tp[1, 8, pl.ds(0, 8), :] = pick(6, hi_se[s, 0], 6, hi_se[s, 1], 7)

        def unit(e, inner):
            edge = e // 2

            def put_t(x, p, east_t, north_t):
                tew[e, x, p] = east_t
                tnw[e, x, p] = north_t

            def put_b(kind, x, p, value):
                bw[kind, e, x, p] = value

            relax(0, edge, (16 + 64 * e) * (1 - edge), 16 * (1 - edge), put_t, put_b)
            return inner

        lax.fori_loop(0, 3, unit, 0)
    def solution_of(s):
        for copy in sums_messages(s):
            copy.wait()
        table = []
        for t in range(7):
            pair = ([], [])
            for i in range(SIDE):
                value = None
                for g in range(SIDE):
                    moved = sub_roll(ga[s, i * SIDE + g, t // 4], 2 * g - 2 * (t % 4))
                    value = moved if value is None else jnp.where(row // 2 == g, moved, value)
                pair[0].append(jnp.where(group % 2 == 0, value, lane_roll(value, 1)))
                pair[1].append(jnp.where(group % 2 == 1, value, lane_roll(value, -1)))
            table.append(pair[0])
            table.append(pair[1])
        b, c, d_side = assemble(table, slot_of)
        coarse = solve_nodes(b, c, d_side, slot_of)

        for place, i in enumerate((3, 0, 1)):
            nodes[0, place] = coarse[i]
            nodes[1, place] = node_shift(coarse[i], 1, slot_of)

        def line(by, place, j):
            return jnp.broadcast_to(nodes[by, place, pl.ds(j, 1), :], (8, 128))

        def put_weights(unit_at, c0, c1, c2, c3):
            cb[unit_at, 0] = c3
            cb[unit_at, 1] = c2 - c3
            cb[unit_at, 2] = c1 - c3
            cb[unit_at, 3] = (c0 - c1) - (c2 - c3)

        for e in range(2):
            near = [line(0, place, e) for place in range(3)]
            far = [line(1, place, e) for place in range(3)]
            put_weights(e, near[1], near[2], far[1], far[2])
            put_weights(2 + e, near[0], near[1], far[0], far[1])
        last = slot_of == 3
        below = [line(0, place, 7) for place in range(3)]
        first = [line(0, place, 0) for place in range(3)]
        put_weights(
            4,
            *(jnp.where(last, below[k + 1], lane_roll(below[k], -2)) for k in range(2)),
            *(jnp.where(last, lane_roll(first[k + 1], 6), lane_roll(first[k], 4)) for k in range(2)),
        )

        def pressures(w, basis_at, x, p):
            return (w[0] + w[1] * basis_at(0, x, p)) + (w[2] * basis_at(1, x, p) + w[3] * basis_at(2, x, p))

        def put_ends(k, east_0, west_7, west_0, t_west_7, p, by):
            ends[k, 0, p] = jnp.where(even, lane_roll(east_0, -1), lane_roll(east_0, 1))
            ends[k, 1, p] = lane_roll(t_west_7 * (west_7 - lane_roll(west_0, -1)), by)

        def interpolate(e, inner):
            w_own = [cb[e, k] for k in range(4)]
            w_west = [cb[2 + e, k] for k in range(4)]
            w_both = [jnp.where(even, a, b) for a, b in zip(w_own, w_west)]

            def own(kind, x, p):
                return bq[s, kind, e, x, p]

            def other(kind, x, p):
                return bw[kind, e, x, p]

            def both(kind, x, p):
                return jnp.where(even, bq[s, kind, e, x, p], bw[kind, e, x, p])

            for p in range(2):
                for x in range(8):
                    pm[e, x, p] = pressures(w_both, both, x, p)
                    tem[e, x, p] = jnp.where(even, teq[s, e, x, p], tew[e, x, p])
                    tnm[e, x, p] = jnp.where(even, tnq[s, e, x, p], tnw[e, x, p])
                put_ends(
                    e, pressures(w_own, own, 0, p), pressures(w_west, other, 7, p),
                    pressures(w_west, other, 0, p), tew[e, 7, p], p, 1,
                )
            return inner

        lax.fori_loop(0, 2, interpolate, 0)
        w_edge = [cb[4, k] for k in range(4)]

        def to_own(value):
            return jnp.where(even, value, lane_roll(value, 2))

        for p in range(2):
            edge = [pressures(w_edge, lambda kind, x, p: bw[kind, 2, x, p], x, p) for x in range(8)]
            for x in range(8):
                pm[2, x, p] = to_own(edge[x])
                tem[2, x, p] = to_own(tew[2, x, p])
                tnm[2, x, p] = to_own(tnw[2, x, p])
            put_ends(2, edge[0], edge[7], edge[0], tew[2, 7, p], p, 3)
        to_rows(s, pm, yp, po)

        @pl.when((s == 0) & first_to_above)
        def _():
            pl.semaphore_wait(ready.at[0], 1)

        @pl.when((s == 0) & has_above)
        def _():
            high_send.start()
            vt_up.start()

        @pl.when((s == 0) & first_to_below)
        def _():
            pl.semaphore_wait(ready.at[1], 1)

        @pl.when((s == 0) & has_below)
        def _():
            low_send.start()

    def fluxes(s):
        def balance(i, inner):
            k = lax.rem(i + 2, 3)
            val = [[pm[k, x, p] for p in range(2)] for x in range(8)]
            f_e = [[None, None] for _ in range(8)]
            for x in range(8):
                for p in range(2):
                    east_v = val[x + 1][p] if x < 7 else ends[k, 0, p]
                    f_e[x][p] = tem[k, x, p] * (val[x][p] - east_v)
            for x in range(8):
                after = lane_roll(jnp.where(slot_of == 0, pm[i, x, 0], val[x][0]), -2)
                after = sub_roll(jnp.where(row0, after, val[x][0]), -1)
                f_n0 = tnm[k, x, 0] * (val[x][0] - val[x][1])
                f_n1 = tnm[k, x, 1] * (val[x][1] - after)
                before = lane_roll(jnp.where(slot_of == 3, pu[x], f_n1), 2)
                before = sub_roll(jnp.where(row7, before, f_n1), 1)
                pu[x] = f_n1
                f_n = (f_n0, f_n1)
                f_s = (before, f_n0)
                for p in range(2):
                    f_w = f_e[x - 1][p] if x else jnp.where(even, lane_roll(f_e[7][p], -1), ends[k, 1, p])
                    hm[k, x, p] = (f_e[x][p] - f_w) + (f_n[p] - f_s[p])
            return inner

        lax.fori_loop(0, 3, balance, 0)
        to_rows(s, hm, yh, ro)

    owned(0)
    coarse_sums(0)
    others(0)
    owned(1)
    solution_of(0)
    coarse_sums(1)
    fluxes(0)
    others(1)
    for s in range(SETS):
        for copy in halo(s):
            copy.wait_send()
    solution_of(1)
    fluxes(1)
    press_copy = pltpu.make_async_copy(po, press_out, out_sem.at[0])
    press_copy.start()

    for half in range(2):
        before = None
        for l in range(LAYERS):
            at = pl.ds(16 * l + 8 * half, 8)
            place = (l + 8) % LAYERS
            here = po[at, :]
            value = sx[half, place] - ax[half, place] * here - ro[at, :]
            if before is not None:
                value = value + before
            if l < LAYERS - 1:
                before = vt[at, :] * (here - po[pl.ds(16 * (l + 1) + 8 * half, 8), :])
                value = value - before
            ro[at, :] = value

    middle_copy = pltpu.make_async_copy(ro.at[pl.ds(16, 480)], resid_out.at[pl.ds(16, 480)], out_sem.at[1])
    middle_copy.start()
    press_copy.wait()

    @pl.when(has_below)
    def _():
        vt_up.wait_recv()
        high_send.wait_recv()
        low_send.wait_send()

    @pl.when(has_above)
    def _():
        low_send.wait_recv()
        high_send.wait_send()
        vt_up.wait_send()

    above = jnp.where(has_above, vt[pl.ds(496, 16), :] * (po[pl.ds(496, 16), :] - up_layer[...]), 0.0)
    below = jnp.where(has_below, down_pair[1] * (down_pair[0] - po[pl.ds(0, 16), :]), 0.0)
    ro[pl.ds(496, 16), :] = ro[pl.ds(496, 16), :] - above
    ro[pl.ds(0, 16), :] = ro[pl.ds(0, 16), :] + below
    edge_copies = [
        pltpu.make_async_copy(ro.at[pl.ds(at, 16)], resid_out.at[pl.ds(at, 16)], out_sem.at[2 + i])
        for i, at in enumerate((0, 496))
    ]
    for copy in edge_copies:
        copy.start()
    middle_copy.wait()
    for copy in edge_copies:
        copy.wait()


def flush(press, resid, press_out, resid_out, sem):
    copies = [
        pltpu.make_async_copy(press, press_out, sem.at[0]),
        pltpu.make_async_copy(resid, resid_out, sem.at[1]),
    ]
    for copy in copies:
        copy.start()
    for copy in copies:
        copy.wait()


def body(permeability, accumulation, source_term, vertical_trans):
    split = (LAYERS, 2, 8, 128)
    vmem = lambda *shape: pltpu.VMEM(shape, F32)
    anywhere = pl.BlockSpec(memory_space=pl.ANY)
    in_hbm = pl.BlockSpec(memory_space=pltpu.HBM)
    pressure, residual = pl.pallas_call(
        kernel,
        out_shape=[jax.ShapeDtypeStruct((512, 128), F32)] * 2,
        in_specs=[in_hbm] * 4,
        out_specs=[anywhere] * 2,
        scratch_shapes=[
            vmem(4, 32, 8, 128),
            vmem(3, 32, 8, 128),
            vmem(3, 32, 8, 128),
            vmem(512, 128),
            vmem(32, 128),
            vmem(32, 128),
            vmem(2, 2, 32, 128),
            vmem(2, 2, 8, 128),
            vmem(2, 2, 32, 128),
            vmem(2, 32, 128),
            vmem(2, 16, 128),
            vmem(2, 16, 128),
            vmem(2, 2, 8, 128),
            vmem(2, 2, 8, 128),
            vmem(2, 8, 128),
            vmem(2, 9, 152, 128),
            vmem(2, 9, 16, 128),
            vmem(8, 136, 128),
            vmem(8, 136, 128),
            vmem(2, 2, 8, 2, 8, 128),
            vmem(2, 2, 8, 2, 8, 128),
            vmem(2, 3, 2, 8, 2, 8, 128),
            vmem(3, 8, 2, 8, 128),
            vmem(3, 8, 2, 8, 128),
            vmem(3, 3, 8, 2, 8, 128),
            vmem(3, 8, 2, 8, 128),
            vmem(3, 8, 2, 8, 128),
            vmem(4, 8, 2, 8, 128),
            vmem(3, 8, 2, 8, 128),
            vmem(2, 14, 8, 128),
            vmem(2, 16, 2, 8, 128),
            vmem(2, 3, 8, 128),
            vmem(5, 4, 8, 128),
            vmem(8, 8, 128),
            vmem(3, 2, 2, 8, 128),
            vmem(3, 8, 2, 8, 128),
            vmem(3, 8, 2, 8, 128),
            vmem(2, 144, 128),
            vmem(2, 144, 128),
            vmem(512, 128),
            vmem(512, 128),
            vmem(16, 128),
            vmem(2, 16, 128),
            pltpu.SemaphoreType.REGULAR((2,)),
            pltpu.SemaphoreType.DMA((13,)),
            pltpu.SemaphoreType.DMA((2, 12)),
            pltpu.SemaphoreType.DMA((2, 12)),
            pltpu.SemaphoreType.DMA((2, 16)),
            pltpu.SemaphoreType.DMA((2, 16)),
            pltpu.SemaphoreType.DMA((3,)),
            pltpu.SemaphoreType.DMA((3,)),
            pltpu.SemaphoreType.DMA((4,)),
        ],
        compiler_params=pltpu.CompilerParams(
            collective_id=0, has_side_effects=True, vmem_limit_bytes=40 * 1024 * 1024
        ),
    )(
        *(
            pltpu.with_memory_space_constraint(value, pltpu.HBM)
            for value in (
                permeability.reshape(split),
                accumulation.reshape(split),
                source_term.reshape(split),
                vertical_trans.reshape(512, 128),
            )
        ),
    )
    pressure, residual = pl.pallas_call(
        flush,
        out_shape=[jax.ShapeDtypeStruct((512, 128), F32)] * 2,
        in_specs=[anywhere] * 2,
        out_specs=[anywhere] * 2,
        scratch_shapes=[pltpu.SemaphoreType.DMA((2,))],
        compiler_params=pltpu.CompilerParams(vmem_limit_bytes=1024 * 1024),
    )(pressure, residual)
    return pressure.reshape(32, 16, 128), residual.reshape(32, 16, 128)


def solution(mesh):
    spec = P("gz", "gx", "gy")
    return jax.shard_map(
        body, mesh=mesh, in_specs=(spec,) * 4, out_specs=(spec, spec), check_vma=False
    )
```
